256 devices in a mesh: dp: 32 (over x, z_hi, y), tensor: 8 (over z_lo, core).
Axes of the slice: x: 4, y: 4, z: 8 (z_hi: 2, z_lo: 4; z = z_hi * 4 + z_lo), core: 2. Of those that a mesh axis runs over, the one named last changes fastest.
Arguments:
- video_patches: bfloat16 [32, 32, 64, 1280], P(None, 'dp'), may hold values from -410 to 410
- frame_count: int32 [32], P('dp'), may hold values from 1 to 32, as said below
- seen_frames: int32 [32, 256], P('dp'), may hold values from 0 to 32, as said below
- base_latents: bfloat16 [64, 1280], replicated, may hold values from -20 to 20
- vision_query: bfloat16 [1280, 1536], P(None, 'tensor'), may hold values from -1 to 1
- vision_kv: bfloat16 [2, 1280, 1536], P(None, None, 'tensor'), may hold values from -1 to 1
- vision_out: bfloat16 [1536, 1280], P('tensor'), may hold values from -0.3125 to 0.3125
- hidden_states: bfloat16 [8192, 8192], P('dp'), may hold values from -600 to 600
- text_query: bfloat16 [8192, 4096], P('dp', 'tensor'), may hold values from -1 to 1
- text_kv: bfloat16 [2, 1280, 4096], P(None, 'dp', 'tensor'), may hold values from -1 to 1
Outputs:
- latents_out: bfloat16 [32, 32, 64, 1280], P(None, 'dp', 'tensor')
- attended: bfloat16 [8192, 4096], P('dp', 'tensor')
The draws below stay inside these ranges and needn't reach their ends.
Inputs may be any that keep to these rules, and one draw needn't show every extreme that they name: `frame_count`: some video has all 32 frames. `seen_frames`: never falls along a video's tokens; the first token of each video sees 0 frames and the last 32.
All inputs are finite; a program needn't handle non-finite values.
Results may differ from the reference program's by a relative error of at most 0.019.
Values may be sent and summed in bfloat16 or wider, within the bound.
A program may use at most 128 MiB of HBM per device.

```python
import math
import jax
import jax.numpy as jnp
from jax import lax

D = 8192
HEAD_DIM = 128
HEADS = 32
DV = 1280
VHEADS = 16
VHEAD_DIM = 96
LATENTS = 64
PATCH = 64
TOK_DEV = 256
FRAMES = 32
SAMPLES = 32
TOKENS = 8192
N_TENSOR = 8


def scaled_field(key, base_values, row_shape, column_shape):
    first_key, second_key = jax.random.split(key)
    row_scale = jnp.exp(jax.random.uniform(first_key, row_shape, jnp.float32, 0.0, math.log(10.0)))
    column_scale = jnp.exp(jax.random.uniform(second_key, column_shape, jnp.float32, 0.0, math.log(10.0)))
    return base_values * row_scale * column_scale


def draw_video_patches(key, part):
    key = jax.random.fold_in(key, 1)
    subkeys = jax.random.split(key, 2)
    shape = (SAMPLES, FRAMES, PATCH, DV)
    base_values = jnp.clip(jax.random.normal(subkeys[0], shape, jnp.float32), -4.0, 4.0)
    field_values = scaled_field(subkeys[1], base_values, (SAMPLES, FRAMES, PATCH, 1), (1, 1, 1, DV))
    return jnp.clip(field_values, -410.0, 410.0).astype(jnp.bfloat16)


def draw_hidden_states(key, part):
    key = jax.random.fold_in(key, 2)
    subkeys = jax.random.split(key, 2)
    shape = (TOKENS, D)
    base_values = jnp.clip(jax.random.normal(subkeys[0], shape, jnp.float32), -4.0, 4.0)
    field_values = scaled_field(subkeys[1], base_values, (TOKENS, 1), (1, D))
    return jnp.clip(field_values, -600.0, 600.0).astype(jnp.bfloat16)


def draw_base_latents(key, part):
    key = jax.random.fold_in(key, 3)
    subkeys = jax.random.split(key, 1)
    shape = (LATENTS, DV)
    base_values = jnp.clip(jax.random.normal(subkeys[0], shape, jnp.float32), -4.0, 4.0)
    return jnp.clip(base_values, -20.0, 20.0).astype(jnp.bfloat16)


def draw_vision_query(key, part):
    key = jax.random.fold_in(key, 4)
    shape = (DV, VHEADS * VHEAD_DIM)
    weights = jnp.clip(jax.random.normal(key, shape, jnp.float32), -4.0, 4.0) * 2.0 / math.sqrt(DV)
    return jnp.clip(weights, -1.0, 1.0).astype(jnp.bfloat16)


def draw_vision_kv(key, part):
    key = jax.random.fold_in(key, 5)
    shape = (2, DV, VHEADS * VHEAD_DIM)
    weights = jnp.clip(jax.random.normal(key, shape, jnp.float32), -4.0, 4.0) / math.sqrt(DV)
    return jnp.clip(weights, -1.0, 1.0).astype(jnp.bfloat16)


def draw_text_query(key, part):
    key = jax.random.fold_in(key, 6)
    shape = (D, HEADS * HEAD_DIM)
    weights = jnp.clip(jax.random.normal(key, shape, jnp.float32), -4.0, 4.0) * 2.0 / math.sqrt(D)
    return jnp.clip(weights, -1.0, 1.0).astype(jnp.bfloat16)


def draw_text_kv(key, part):
    key = jax.random.fold_in(key, 7)
    shape = (2, DV, HEADS * HEAD_DIM)
    weights = jnp.clip(jax.random.normal(key, shape, jnp.float32), -4.0, 4.0) / math.sqrt(DV)
    return jnp.clip(weights, -1.0, 1.0).astype(jnp.bfloat16)


def draw_frame_count(key, part):
    key = jax.random.fold_in(key, 8)
    first_key, second_key = jax.random.split(key)
    counts = jax.random.randint(first_key, (SAMPLES,), 1, FRAMES + 1)
    fullest = jax.random.randint(second_key, (), 0, SAMPLES)
    return jnp.where(jnp.arange(SAMPLES) == fullest, FRAMES, counts).astype(jnp.int32)


def draw_seen_frames(key, part):
    key = jax.random.fold_in(key, 9)
    seen_count = jnp.sort(jax.random.randint(key, (SAMPLES, TOK_DEV), 0, FRAMES + 1), axis=1)
    seen_count = seen_count.at[:, 0].set(0).at[:, TOK_DEV - 1].set(FRAMES)
    return seen_count.astype(jnp.int32)


def levels(key, extent, cuts, smallest, high):
    def one(axis_at, shards_of):
        steps = jax.random.uniform(jax.random.fold_in(jax.random.fold_in(key, 6), axis_at), (shards_of,), jnp.float32, smallest / len(cuts), high / len(cuts))
        return jnp.repeat(jnp.exp(steps), extent[axis_at] // shards_of).reshape((-1,) + (1,) * (len(extent) - axis_at - 1))

    factor_of = one(*cuts[0])
    for cut in cuts[1:]:
        factor_of = factor_of * one(*cut)
    return factor_of


def gaussian(key, dims, deviation, most, cuts=(), kind=jnp.bfloat16):
    array = deviation * jax.random.normal(key, dims, jnp.float32)
    if cuts:
        array = array * levels(key, dims, cuts, -0.22, 0.18)
    return jnp.clip(array, -most, most).astype(kind)


def setup_inputs(seed: int = 0) -> dict:
    arg_keys = jax.random.split(jax.random.key(seed), 11)
    video_patches = draw_video_patches(jax.random.fold_in(arg_keys[10], 71), 0)
    frame_count = draw_frame_count(jax.random.fold_in(arg_keys[10], 71), 0)
    seen_frames = draw_seen_frames(jax.random.fold_in(arg_keys[10], 71), 0)
    base_latents = draw_base_latents(jax.random.fold_in(arg_keys[10], 71), 0)
    vision_query = draw_vision_query(jax.random.fold_in(arg_keys[10], 71), 0)
    vision_kv = draw_vision_kv(jax.random.fold_in(arg_keys[10], 71), 0)
    vision_out = gaussian(arg_keys[6], (VHEADS * VHEAD_DIM, DV), (VHEADS * VHEAD_DIM // 4) ** -0.5, 0.3125, ((0, 8),))
    hidden_states = draw_hidden_states(jax.random.fold_in(arg_keys[10], 71), 0)
    text_query = draw_text_query(jax.random.fold_in(arg_keys[10], 71), 0)
    text_kv = draw_text_kv(jax.random.fold_in(arg_keys[10], 71), 0)
    return dict(video_patches=video_patches, frame_count=frame_count, seen_frames=seen_frames, base_latents=base_latents, vision_query=vision_query, vision_kv=vision_kv, vision_out=vision_out, hidden_states=hidden_states, text_query=text_query, text_kv=text_kv)


EPSILON = 1e-05
MASKED = -1e+30

def layer_norm(field_values):
    average = lax.optimization_barrier(jnp.mean(field_values, axis=-1, keepdims=True))
    centered = field_values - average
    variance = lax.optimization_barrier(jnp.mean(centered * centered, axis=-1, keepdims=True))
    return centered * lax.rsqrt(variance + EPSILON)

def masked_softmax(scores, allowed):
    scores = jnp.where(allowed, scores, MASKED)
    largest = lax.optimization_barrier(jnp.max(scores, axis=-1, keepdims=True))
    exponent = jnp.exp(scores - largest)
    return exponent / lax.optimization_barrier(jnp.sum(exponent, axis=-1, keepdims=True))

def rounded(field_values):
    return lax.optimization_barrier(field_values.astype(jnp.bfloat16)).astype(jnp.float32)

def reference(video_patches, frame_count, seen_frames, base_latents, vision_query, vision_kv, vision_out, hidden_states, text_query, text_kv):
    vis_cols = VHEADS * VHEAD_DIM
    group_cols = vis_cols // N_TENSOR
    lat_norm = layer_norm(base_latents.astype(jnp.float32)).astype(jnp.bfloat16)
    latent_queries = (jnp.dot(lat_norm, vision_query, preferred_element_type=jnp.float32) * VHEAD_DIM ** (-0.5)).astype(jnp.bfloat16)
    query_heads = latent_queries.astype(jnp.float32).reshape(LATENTS, VHEADS, VHEAD_DIM)
    latent_kv = jnp.einsum('ld,cdh->clh', lat_norm.astype(jnp.float32), vision_kv.astype(jnp.float32)).astype(jnp.bfloat16)
    out_groups = vision_out.astype(jnp.float32).reshape(N_TENSOR, group_cols, DV)
    base_float = base_latents.astype(jnp.float32)

    def one_video(patches):
        context = layer_norm(patches.astype(jnp.float32)).astype(jnp.bfloat16)
        context_kv = jnp.einsum('fpd,cdh->cfph', context.astype(jnp.float32), vision_kv.astype(jnp.float32)).astype(jnp.bfloat16)
        lat_wide = jnp.broadcast_to(latent_kv[:, None], (2, FRAMES, LATENTS, vis_cols))
        stacked = jnp.concatenate([context_kv, lat_wide], axis=2).astype(jnp.float32)
        vis_keys = stacked[0].reshape(FRAMES, PATCH + LATENTS, VHEADS, VHEAD_DIM)
        vis_values = stacked[1].reshape(FRAMES, PATCH + LATENTS, VHEADS, VHEAD_DIM)
        scores = jnp.einsum('lhd,fkhd->fhlk', query_heads, vis_keys)
        vis_probs = rounded(masked_softmax(scores, True))
        mixed_heads = rounded(jnp.einsum('fhlk,fkhd->flhd', vis_probs, vis_values))
        mixed_heads = mixed_heads.reshape(FRAMES, LATENTS, N_TENSOR, group_cols)
        partial_value = rounded(jnp.einsum('flgc,gcd->gfld', mixed_heads, out_groups))
        head_mix = lax.optimization_barrier(jnp.sum(partial_value, axis=0))
        return layer_norm(base_float[None] + head_mix).astype(jnp.bfloat16)
    latents_out = lax.map(one_video, video_patches)
    head_cols = HEADS * HEAD_DIM
    tok_norm = layer_norm(hidden_states.astype(jnp.float32)).astype(jnp.bfloat16)
    key_frame = jnp.arange(FRAMES * LATENTS, dtype=jnp.int32) // LATENTS

    def one_text(packed_inputs):
        text_rows, video_latents, seen_rows, frame_total = packed_inputs
        queries = (jnp.dot(text_rows, text_query, preferred_element_type=jnp.float32) * HEAD_DIM ** (-0.5)).astype(jnp.bfloat16)
        lat_rows = video_latents.reshape(FRAMES * LATENTS, DV)
        txt_keys = jnp.dot(lat_rows, text_kv[0], preferred_element_type=jnp.float32).astype(jnp.bfloat16)
        txt_values = jnp.dot(lat_rows, text_kv[1], preferred_element_type=jnp.float32).astype(jnp.bfloat16)
        frame_limit = jnp.minimum(seen_rows, frame_total)
        allowed = key_frame[None, :] < frame_limit[:, None]
        txt_scores = jnp.einsum('lhd,khd->hlk', queries.astype(jnp.float32).reshape(TOK_DEV, HEADS, HEAD_DIM), txt_keys.astype(jnp.float32).reshape(FRAMES * LATENTS, HEADS, HEAD_DIM))
        txt_probs = rounded(masked_softmax(txt_scores, allowed[None]))
        heads_out = jnp.einsum('hlk,khd->lhd', txt_probs, txt_values.astype(jnp.float32).reshape(FRAMES * LATENTS, HEADS, HEAD_DIM))
        heads_out = heads_out.reshape(TOK_DEV, head_cols)
        return jnp.where((frame_limit > 0)[:, None], heads_out, 0.0).astype(jnp.bfloat16)
    attended = lax.map(one_text, (tok_norm.reshape(SAMPLES, TOK_DEV, D), latents_out, seen_frames, frame_count))
    return (latents_out, attended.reshape(TOKENS, head_cols))
```

```python
import functools

import jax
import jax.numpy as jnp
from jax import lax
from jax.experimental import pallas as pl
from jax.experimental.pallas import tpu as pltpu
from jax.sharding import PartitionSpec as P

HEAD_DIM = 128
VHEAD_DIM = 96
EPSILON = 1e-05
MASKED = -1e30
MESH = pl.DeviceIdType.MESH
F32 = jnp.float32
BF16 = jnp.bfloat16


def layer_norm(values):
    average = jnp.mean(values, axis=-1, keepdims=True)
    centered = values - average
    variance = jnp.mean(centered * centered, axis=-1, keepdims=True)
    return centered * lax.rsqrt(variance + EPSILON)


def masked_softmax(scores, allowed):
    scores = jnp.where(allowed, scores, MASKED)
    largest = jnp.max(scores, axis=-1, keepdims=True)
    exponent = jnp.exp(scores - largest)
    return exponent / jnp.sum(exponent, axis=-1, keepdims=True)


def dot(a, b, ca=1, cb=0):
    return lax.dot_general(a, b, (((ca,), (cb,)), ((), ())), preferred_element_type=F32)


def exchange_kernel(
    patches, base, wv, wo_in, q_in, kv_in,
    lat_out, g1, g2, lall,
    ctx, wo, hs, hbuf, base32,
    lsem, w0s, w0r, w1s, w1r, w2s, w2r, wos, wor, sibs, sibr, has, har, v4s, v4r, ups, upr, dns, dnr, lss, lsr,
):
    dp = lax.axis_index("dp")
    t = lax.axis_index("tensor")
    x = dp // 8
    zh = (dp // 4) % 2
    y = dp % 4
    zl = t // 2
    core = t % 2
    z = zh * 4 + zl

    def at(xx, zz, yy):
        return {"dp": (xx * 2 + zz) * 4 + yy, "tensor": t}

    def ring(offset):
        zz = (z + offset + 8) % 8
        return {"dp": (x * 2 + zz // 4) * 4 + y, "tensor": (zz % 4) * 2 + core}

    def tens(tt):
        return {"dp": dp, "tensor": tt}

    sibling = tens(t + 1 - 2 * core)

    def rc(src, dst, ss, rs, device):
        return pltpu.make_async_remote_copy(
            src_ref=src, dst_ref=dst, send_sem=ss, recv_sem=rs, device_id=device, device_id_type=MESH
        )

    barrier = pltpu.get_barrier_semaphore()

    def greet(j, carry):
        pl.semaphore_signal(barrier, inc=1, device_id={"dp": (dp + j) % 32, "tensor": t}, device_id_type=MESH)
        return carry

    lax.fori_loop(1, 32, greet, 0)
    for j in range(1, 8):
        pl.semaphore_signal(barrier, inc=1, device_id=tens((t + j) % 8), device_id_type=MESH)
    for o in (1, -1, 2, -2):
        pl.semaphore_signal(barrier, inc=1, device_id=ring(o), device_id_type=MESH)

    local_q = pltpu.make_async_copy(q_in, g1.at[x, zh, y], lsem.at[0])
    local_kv = pltpu.make_async_copy(kv_in, g2.at[x, zh, y], lsem.at[1])
    local_q.start()
    local_kv.start()

    def w0(k):
        src, dst = ((q_in, g1), (kv_in, g2))[k]
        return rc(src, dst.at[x, zh, y], w0s.at[k], w0r.at[k], at(x, 1 - zh, y))

    def w0_in(k):
        src, dst = ((q_in, g1), (kv_in, g2))[k]
        return rc(src, dst.at[x, 1 - zh, y], w0s.at[k], w0r.at[k], at(x, 1 - zh, y))

    halves = (pl.ds(0, 128), pl.ds(128, 128)), (pl.ds(0, 512), pl.ds(512, 512))

    def w1_copies(b, inbound):
        zz = zh if b == 0 else 1 - zh
        out = []
        for d in range(2):
            for j in (1, 2, 3):
                sign = -j if inbound else j
                if d == 0:
                    px, py = x, (y + sign + 4) % 4
                else:
                    px, py = (x + sign + 4) % 4, y
                bx, by = (px, py) if inbound else (x, y)
                for k in range(2):
                    if k == 0:
                        dst = g1.at[bx, zz, by, halves[0][d]]
                        src = q_in.at[halves[0][d]] if b == 0 else g1.at[x, zz, y, halves[0][d]]
                    else:
                        dst = g2.at[bx, zz, by, :, halves[1][d]]
                        src = kv_in.at[:, halves[1][d]] if b == 0 else g2.at[x, zz, y, :, halves[1][d]]
                    i = ((b * 2 + d) * 3 + j - 1) * 2 + k
                    out.append(rc(src, dst, w1s.at[i], w1r.at[i], at(px, zh, py)))
        return out

    def w2_copies(b, inbound):
        zz = zh if b == 0 else 1 - zh
        out = []
        for d in range(2):
            for j in (1, 2, 3):
                sign = -j if inbound else j
                for k in range(2):
                    if d == 0:
                        px, py = (x + sign + 4) % 4, y
                        bx = px if inbound else x
                        region = (
                            lambda bb: g1.at[bb, zz, :, halves[0][0]]
                            if k == 0 else g2.at[bb, zz, :, :, halves[1][0]]
                        )
                        src, dst = region(x), region(bx)
                    else:
                        px, py = x, (y + sign + 4) % 4
                        by = py if inbound else y
                        region = (
                            lambda bb: g1.at[:, zz, bb, halves[0][1]]
                            if k == 0 else g2.at[:, zz, bb, :, halves[1][1]]
                        )
                        src, dst = region(y), region(by)
                    i = ((b * 2 + d) * 3 + j - 1) * 2 + k
                    out.append(rc(src, dst, w2s.at[i], w2r.at[i], at(px, zh, py)))
        return out

    def wo_block(o):
        return ((zl + o + 4) % 4) * 2 + core

    def wo_copies(inbound):
        mine = 0
        out = []
        for i, o in enumerate((1, -1, 2, -2)):
            block = wo_block(-o if inbound else mine)
            device = ring(-o if inbound else o)
            if i < 2:
                out.append(rc(wo_in, wo.at[block, :, pl.ds(0, 96)], wos.at[i], wor.at[i], device))
            else:
                out.append(rc(wo_in.at[i - 2], wo.at[block, i - 2, pl.ds(0, 96)], wos.at[i], wor.at[i], device))
        return out

    def wo_sibling(o, inbound):
        block = o * 2 + (1 - core if inbound else core)
        region = wo.at[block, :, pl.ds(0, 96)]
        return rc(region, region, sibs.at[o], sibr.at[o], sibling)

    local_wo = pltpu.make_async_copy(wo_in, wo.at[t, :, pl.ds(0, 96)], lsem.at[2])
    local_wo.start()

    pl.semaphore_wait(barrier, 42)

    for k in range(2):
        w0(k).start()
    for cp in wo_copies(False):
        cp.start()
    for cp in w1_copies(0, False):
        cp.start()

    for g in range(8):
        for h in range(2):
            wo[g, h, pl.ds(96, 32), :] = jnp.zeros((32, wo.shape[-1]), BF16)
    base32[...] = base[...].astype(F32)
    lat_norm = layer_norm(base32[...]).astype(BF16)
    lat_all = dot(lat_norm, wv[...])
    q = (lat_all[:, :256] * VHEAD_DIM ** (-0.5)).astype(BF16)
    lat_kv = lat_all[:, 256:].astype(BF16)
    k_lat, v_lat = lat_kv[:, :256], lat_kv[:, 256:]
    blank = jnp.zeros((64, 128), BF16)
    q_block = jnp.concatenate(
        [jnp.concatenate([q[:, :128], blank], 1), jnp.concatenate([blank, q[:, 128:]], 1)], 0
    )
    s_lat = dot(k_lat, q_block, 1, 1)
    m_lat = jnp.max(s_lat, axis=0, keepdims=True)

    def vision_chunk(first):
        def norm(r, carry):
            rows = patches[pl.ds(first * 64 + r * 32, 32), :].astype(F32)
            ctx[pl.ds(r * 32, 32), :] = layer_norm(rows).astype(BF16)
            return carry

        lax.fori_loop(0, 16, norm, 0)

        def pair(g, carry):
            kv = dot(ctx[pl.ds(g * 128, 128), :], wv[:, 256:]).astype(BF16)
            s = dot(kv[:, :256], q_block, 1, 1)
            rows = []
            for v in range(2):
                sv = s[v * 64:(v + 1) * 64]
                m = jnp.maximum(jnp.max(sv, axis=0, keepdims=True), m_lat)
                e = jnp.exp(jnp.concatenate([sv, s_lat], 0) - m)
                p = (e / jnp.sum(e, axis=0, keepdims=True)).astype(BF16)
                values = jnp.concatenate([kv[v * 64:(v + 1) * 64, 256:], v_lat], 0)
                o = dot(p, values, 0, 0)
                rows.append(jnp.concatenate([o[:64, :128], o[64:, 128:]], 1))
            for u in range(8):
                pairrows = jnp.concatenate([r[u * 8:(u + 1) * 8] for r in rows], 0)
                hs[u, pl.ds(pl.multiple_of((first + g * 2) * 8, 16), 16), :] = pairrows.astype(BF16)
            return carry

        lax.fori_loop(0, 4, pair, 0)

    def head_copy(c, j, inbound):
        ch = (x + c) % 4
        other = (t + (8 - j if inbound else j)) % 8
        rows = pl.ds(pl.multiple_of(ch * 64, 64), 64)
        i = c * 8 + j
        if inbound:
            return rc(hs.at[t, rows], hbuf.at[other, rows], has.at[i], har.at[i], tens(other))
        return rc(hs.at[other, rows], hbuf.at[t, rows], has.at[i], har.at[i], tens(other))

    def head_local(c):
        rows = pl.ds(pl.multiple_of(((x + c) % 4) * 64, 64), 64)
        return pltpu.make_async_copy(hs.at[t, rows], hbuf.at[t, rows], lsem.at[4 + c])

    def w2_start(b):
        if b == 0:
            local_q.wait()
            local_kv.wait()
        for cp in w1_copies(b, True):
            cp.wait_recv()
        for cp in w2_copies(b, False):
            cp.start()

    for c in range(4):
        vision_chunk(((x + c) % 4) * 8)
        for j in range(1, 8):
            head_copy(c, j, False).start()
        head_local(c).start()
        if c == 1:
            w2_start(0)

    local_wo.wait()
    for cp in wo_copies(True):
        cp.wait_recv()
    for o in range(4):
        wo_sibling(o, False).start()
    for k in range(2):
        w0_in(k).wait_recv()
    for cp in w1_copies(1, False):
        cp.start()
    for o in range(4):
        wo_sibling(o, True).wait_recv()

    def v4(c, i, inbound):
        if inbound:
            f = ((x - c + 4) % 4) * 8 + (dp % 8 + 8 - i) % 8
            return rc(lat_out.at[0], lall.at[t, f], v4s.at[c * 8 + i], v4r.at[c * 8 + i], {"dp": f, "tensor": t})
        s = ((x + c) % 4) * 8 + (dp % 8 + i) % 8
        return rc(lat_out.at[s], lall.at[t, dp], v4s.at[c * 8 + i], v4r.at[c * 8 + i], {"dp": s, "tensor": t})

    local_lat = pltpu.make_async_copy(lat_out.at[dp], lall.at[t, dp], lsem.at[3])
    my_base = base32[pl.ds(pl.multiple_of(t * 8, 8), 8), :]
    for c in range(4):
        ch = (x + c) % 4
        rows = pl.ds(pl.multiple_of(ch * 64, 64), 64)
        for j in range(1, 8):
            head_copy(c, j, True).wait_recv()
        head_local(c).wait()
        mix = jnp.zeros((64, 1280), F32)
        for g in range(8):
            for h in range(2):
                mix = mix + dot(hbuf[g, rows, h * 128:(h + 1) * 128], wo[g, h])
        mix = mix.reshape(8, 8, 1280) + my_base[None]
        lat_out[pl.ds(ch * 8, 8)] = layer_norm(mix).astype(BF16)
        for i in range(8):
            if c == 0 and i == 0:
                local_lat.start()
            else:
                v4(c, i, False).start()

    w2_start(1)

    def frames(c):
        return pl.ds(((x - c + 4) % 4) * 8, 8)

    def line(up, j, c, inbound):
        away = j + 1 if inbound else j
        origin = zl - away if up else zl + away
        region = lall.at[origin * 2 + core, frames(c)]
        ss, rs = (ups, upr) if up else (dns, dnr)
        step = (2 if up else -2) * (-1 if inbound else 1)
        return rc(region, region, ss.at[j * 4 + c], rs.at[j * 4 + c], tens(t + step))

    def sib(origin, c, slot, inbound):
        region = lall.at[origin * 2 + (1 - core if inbound else core), frames(c)]
        return rc(region, region, lss.at[slot], lsr.at[slot], sibling)

    for c in range(4):
        for i in range(8):
            if c == 0 and i == 0:
                local_lat.wait()
            else:
                v4(c, i, True).wait_recv()
        pl.when(zl < 3)(lambda: line(True, 0, c, False).start())
        pl.when(zl > 0)(lambda: line(False, 0, c, False).start())
        sib(zl, c, c, False).start()

    for j in range(1, 4):
        for c in range(4):
            @pl.when(zl >= j)
            def _():
                line(True, j - 1, c, True).wait_recv()
                if j < 3:
                    pl.when(zl < 3)(lambda: line(True, j, c, False).start())
                sib(zl - j, c, j * 4 + c, False).start()

            @pl.when(zl + j <= 3)
            def _():
                line(False, j - 1, c, True).wait_recv()
                if j < 3:
                    pl.when(zl > 0)(lambda: line(False, j, c, False).start())
                sib(zl + j, c, (j + 3) * 4 + c, False).start()

    for c in range(4):
        sib(zl, c, c, True).wait_recv()
        sib(zl, c, c, False).wait_send()
        pl.when(zl < 3)(lambda: line(True, 0, c, False).wait_send())
        pl.when(zl > 0)(lambda: line(False, 0, c, False).wait_send())
        for j in range(1, 4):
            @pl.when(zl >= j)
            def _():
                sib(zl - j, c, j * 4 + c, True).wait_recv()
                sib(zl - j, c, j * 4 + c, False).wait_send()
                if j < 3:
                    pl.when(zl < 3)(lambda: line(True, j, c, False).wait_send())

            @pl.when(zl + j <= 3)
            def _():
                sib(zl + j, c, (j + 3) * 4 + c, True).wait_recv()
                sib(zl + j, c, (j + 3) * 4 + c, False).wait_send()
                if j < 3:
                    pl.when(zl > 0)(lambda: line(False, j, c, False).wait_send())
        for j in range(1, 8):
            head_copy(c, j, False).wait_send()
        for i in range(8):
            if not (c == 0 and i == 0):
                v4(c, i, False).wait_send()
    for b in range(2):
        for cp in w1_copies(b, False):
            cp.wait_send()
        for cp in w2_copies(b, True):
            cp.wait_recv()
        for cp in w2_copies(b, False):
            cp.wait_send()
    for k in range(2):
        w0(k).wait_send()
    for cp in wo_copies(False):
        cp.wait_send()
    for o in range(4):
        wo_sibling(o, False).wait_send()


def exchange(patches, base, wv, wo_in, q_in, kv_in):
    vm = pl.BlockSpec(memory_space=pltpu.VMEM)
    hbm = pl.BlockSpec(memory_space=pl.ANY)
    dma = lambda n: pltpu.SemaphoreType.DMA((n,))
    return pl.pallas_call(
        exchange_kernel,
        name="exchange",
        out_shape=(
            jax.ShapeDtypeStruct((32, 8, 1280), BF16),
            jax.ShapeDtypeStruct((4, 2, 4, 256, 512), BF16),
            jax.ShapeDtypeStruct((4, 2, 4, 40, 1024), BF16),
            jax.ShapeDtypeStruct((8, 32, 8, 1280), BF16),
        ),
        in_specs=[vm, vm, vm, vm, hbm, hbm],
        out_specs=(vm, hbm, hbm, hbm),
        scratch_shapes=[
            pltpu.VMEM((512, 1280), BF16),
            pltpu.VMEM((8, 2, 128, 1280), BF16),
            pltpu.VMEM((8, 256, 256), BF16),
            pltpu.VMEM((8, 256, 256), BF16),
            pltpu.VMEM((64, 1280), F32),
            dma(8), dma(2), dma(2), dma(24), dma(24), dma(24), dma(24), dma(4), dma(4), dma(4), dma(4),
            dma(32), dma(32), dma(32), dma(32), dma(12), dma(12), dma(12), dma(12), dma(28), dma(28),
        ],
        compiler_params=pltpu.CompilerParams(
            collective_id=0, has_side_effects=True, vmem_limit_bytes=48 * 2**20
        ),
        cost_estimate=pl.CostEstimate(flops=6 * 10**9, bytes_accessed=40 * 10**6, transcendentals=10**6),
    )(patches, base, wv, wo_in, q_in, kv_in)


def pad_heads(weight):
    rows, columns = weight.shape
    heads = columns // VHEAD_DIM
    parts = weight.reshape(rows, heads, VHEAD_DIM)
    return jnp.pad(parts, ((0, 0), (0, 0), (0, 128 - VHEAD_DIM))).reshape(rows, heads * 128)


def local(
    video_patches,
    frame_count,
    seen_frames,
    base_latents,
    vision_query,
    vision_kv,
    vision_out,
    hidden_states,
    text_query,
    text_kv,
):
    width = video_patches.shape[-1]
    latents = base_latents.shape[0]
    wv = jnp.concatenate([pad_heads(vision_query), pad_heads(vision_kv[0]), pad_heads(vision_kv[1])], axis=1)
    kv_in = jnp.concatenate([text_kv[0], text_kv[1]], axis=1)
    latents_out, g1, g2, lall = exchange(
        video_patches.reshape(-1, width), base_latents, wv, vision_out.reshape(2, VHEAD_DIM, width), text_query, kv_in
    )
    query_full = g1.reshape(-1, g1.shape[-1])
    kv_full = g2.reshape(-1, g2.shape[-1])
    lat_rows = lall.reshape(-1, width)
    tokens = hidden_states.shape[0]
    tok_norm = layer_norm(hidden_states.astype(F32)).astype(BF16)
    head_cols = text_query.shape[1]
    queries = (jnp.dot(tok_norm, query_full, preferred_element_type=F32) * HEAD_DIM ** (-0.5)).astype(BF16)
    kv_text = jnp.dot(lat_rows, kv_full, preferred_element_type=F32).astype(BF16)
    text_heads = head_cols // HEAD_DIM
    frame_limit = jnp.minimum(seen_frames[0], frame_count[0])
    key_frame = jnp.arange(lat_rows.shape[0], dtype=jnp.int32) // 8 % 32
    allowed = key_frame[None, :] < frame_limit[:, None]
    txt_scores = jnp.einsum(
        "lhd,khd->hlk",
        queries.reshape(tokens, text_heads, HEAD_DIM),
        kv_text[:, :head_cols].reshape(lat_rows.shape[0], text_heads, HEAD_DIM),
        preferred_element_type=F32,
    )
    txt_probs = masked_softmax(txt_scores, allowed[None]).astype(BF16)
    attended = jnp.einsum(
        "hlk,khd->lhd",
        txt_probs,
        kv_text[:, head_cols:].reshape(lat_rows.shape[0], text_heads, HEAD_DIM),
        preferred_element_type=F32,
    )
    attended = attended.reshape(tokens, head_cols)
    attended = jnp.where((frame_limit > 0)[:, None], attended, 0.0).astype(BF16)
    return latents_out[:, None], attended


def solution(mesh):
    placed = (
        P(None, "dp", None, None),
        P("dp"),
        P("dp", None),
        P(),
        P(None, "tensor"),
        P(None, None, "tensor"),
        P("tensor", None),
        P("dp", None),
        P("dp", "tensor"),
        P(None, "dp", "tensor"),
    )
    return jax.shard_map(
        local,
        mesh=mesh,
        in_specs=placed,
        out_specs=(P(None, "dp", "tensor", None), P("dp", "tensor")),
        check_vma=False,
    )
```

```python
import jax
import jax.numpy as jnp
from jax import lax
from jax.experimental import pallas as pl
from jax.experimental.pallas import tpu as pltpu
from jax.sharding import PartitionSpec as P

HEAD_DIM = 128
VHEAD_DIM = 96
EPSILON = 1e-05
MASKED = -1e30
MESH = pl.DeviceIdType.MESH
F32 = jnp.float32
BF16 = jnp.bfloat16


def layer_norm(values):
    average = jnp.mean(values, axis=-1, keepdims=True)
    centered = values - average
    variance = jnp.mean(centered * centered, axis=-1, keepdims=True)
    return centered * lax.rsqrt(variance + EPSILON)


def dot(a, b, ca=1, cb=0):
    return lax.dot_general(a, b, (((ca,), (cb,)), ((), ())), preferred_element_type=F32)


def fused_kernel(
    patches_in, frame_count, seen, base, wq, wkv_vis, wo_in, hidden_in, q_in, kv_in,
    lat_out, att_out,
    patches, ctx, woa, wob, hs, hbuf, base32, latp, lall, g1, g2, wkv, tokn, qacc, qh, bias, top, acc,
    lsem, w0s, w0r, w1s, w1r, w2s, w2r, wos, wor, sibs, sibr, has, har, v4s, v4r, ups, upr, dns, dnr, lss, lsr,
):
    dp = lax.axis_index("dp")
    t = lax.axis_index("tensor")
    x = dp // 8
    zh = (dp // 4) % 2
    y = dp % 4
    zl = t // 2
    core = t % 2
    z = zh * 4 + zl

    def at(xx, zz, yy):
        return {"dp": (xx * 2 + zz) * 4 + yy, "tensor": t}

    def ring(offset):
        zz = (z + offset + 8) % 8
        return {"dp": (x * 2 + zz // 4) * 4 + y, "tensor": (zz % 4) * 2 + core}

    def tens(tt):
        return {"dp": dp, "tensor": tt}

    sibling = tens(t + 1 - 2 * core)

    def rc(src, dst, ss, rs, device):
        return pltpu.make_async_remote_copy(
            src_ref=src, dst_ref=dst, send_sem=ss, recv_sem=rs, device_id=device, device_id_type=MESH
        )

    barrier = pltpu.get_barrier_semaphore()

    def greet(j, carry):
        pl.semaphore_signal(barrier, inc=1, device_id={"dp": (dp + j) % 32, "tensor": t}, device_id_type=MESH)
        return carry

    lax.fori_loop(1, 32, greet, 0)
    for j in range(1, 8):
        pl.semaphore_signal(barrier, inc=1, device_id=tens((t + j) % 8), device_id_type=MESH)
    for o in (1, -1, 2, -2):
        pl.semaphore_signal(barrier, inc=1, device_id=ring(o), device_id_type=MESH)

    def chunk(c):
        return (x + c) % 4

    def patch_load(c):
        rows = pl.ds(pl.multiple_of(chunk(c) * 512, 512), 512)
        return pltpu.make_async_copy(patches_in.at[rows], patches.at[rows], lsem.at[8 + c])

    for c in range(4):
        patch_load(c).start()
    local_q = pltpu.make_async_copy(q_in, g1.at[x, zh, y], lsem.at[0])
    local_kv = pltpu.make_async_copy(kv_in, g2.at[x, zh, y], lsem.at[1])
    local_woa = pltpu.make_async_copy(wo_in.at[pl.ds(0, 128)], woa.at[t], lsem.at[2])
    local_wob = pltpu.make_async_copy(wo_in.at[pl.ds(128, 64)], wob.at[t], lsem.at[3])
    local_hidden = pltpu.make_async_copy(hidden_in, tokn, lsem.at[12])
    for cp in (local_q, local_kv, local_woa, local_wob, local_hidden):
        cp.start()

    def w0(k):
        src, dst = ((q_in, g1), (kv_in, g2))[k]
        return rc(src, dst.at[x, zh, y], w0s.at[k], w0r.at[k], at(x, 1 - zh, y))

    def w0_in(k):
        src, dst = ((q_in, g1), (kv_in, g2))[k]
        return rc(src, dst.at[x, 1 - zh, y], w0s.at[k], w0r.at[k], at(x, 1 - zh, y))

    halves = (pl.ds(0, 128), pl.ds(128, 128))

    def w1_copies(b, inbound):
        zz = zh if b == 0 else 1 - zh
        out = []
        for j in (1, 3, 2):
            for d in range(2):
                sign = -j if inbound else j
                if d == 0:
                    px, py = x, (y + sign + 4) % 4
                else:
                    px, py = (x + sign + 4) % 4, y
                bx, by = (px, py) if inbound else (x, y)
                for k in range(2):
                    if k == 0:
                        dst = g1.at[bx, zz, by, halves[d]]
                        src = q_in.at[halves[d]] if b == 0 else g1.at[x, zz, y, halves[d]]
                    else:
                        dst = g2.at[bx, zz, by, d]
                        src = kv_in.at[d] if b == 0 else g2.at[x, zz, y, d]
                    i = ((b * 2 + d) * 3 + j - 1) * 2 + k
                    out.append(rc(src, dst, w1s.at[i], w1r.at[i], at(px, zh, py)))
        return out

    def w2_copies(b, inbound):
        zz = zh if b == 0 else 1 - zh
        out = []
        for j in (1, 3, 2):
            for d in range(2):
                sign = -j if inbound else j
                for k in (1, 0):
                    if d == 0:
                        px, py = (x + sign + 4) % 4, y
                        bx = px if inbound else x
                        if k == 0:
                            src, dst = g1.at[x, zz, :, halves[0]], g1.at[bx, zz, :, halves[0]]
                        else:
                            src, dst = g2.at[x, zz, :, 0], g2.at[bx, zz, :, 0]
                    else:
                        px, py = x, (y + sign + 4) % 4
                        by = py if inbound else y
                        if k == 0:
                            src, dst = g1.at[:, zz, y, halves[1]], g1.at[:, zz, by, halves[1]]
                        else:
                            src, dst = g2.at[:, zz, y, 1], g2.at[:, zz, by, 1]
                    i = ((b * 2 + d) * 3 + j - 1) * 2 + k
                    out.append(rc(src, dst, w2s.at[i], w2r.at[i], at(px, zh, py)))
        return out

    def w2_start(b):
        if b == 0:
            local_q.wait()
            local_kv.wait()
        for cp in w1_copies(b, True):
            cp.wait_recv()
        for cp in w2_copies(b, False):
            cp.start()

    def wo_block(o):
        return ((zl + o + 4) % 4) * 2 + core

    def wo_near(inbound):
        out = []
        for i, o in enumerate((1, -1)):
            block = wo_block(-o if inbound else 0)
            device = ring(-o if inbound else o)
            out.append(rc(wo_in.at[pl.ds(0, 128)], woa.at[block], wos.at[2 * i], wor.at[2 * i], device))
            out.append(rc(wo_in.at[pl.ds(128, 64)], wob.at[block], wos.at[2 * i + 1], wor.at[2 * i + 1], device))
        return out

    def wo_far(inbound):
        out = []
        for i, (o, part) in enumerate(((1, pl.ds(0, 96)), (-1, pl.ds(96, 32)), (-1, None))):
            block = wo_block(-2 * o if inbound else -o)
            device = ring(-o if inbound else o)
            region = wob.at[block] if part is None else woa.at[block, part]
            out.append(rc(region, region, wos.at[4 + i], wor.at[4 + i], device))
        return out

    def wo_sibling(o, inbound):
        block = o * 2 + (1 - core if inbound else core)
        return [
            rc(woa.at[block], woa.at[block], sibs.at[2 * o], sibr.at[2 * o], sibling),
            rc(wob.at[block], wob.at[block], sibs.at[2 * o + 1], sibr.at[2 * o + 1], sibling),
        ]

    base32[...] = base[...].astype(F32)
    lat_norm = layer_norm(base32[...]).astype(BF16)
    q = dot(lat_norm, wq[...]) * VHEAD_DIM ** (-0.5)
    k_lat = dot(lat_norm, wkv_vis[0]).astype(BF16)
    v_lat = dot(lat_norm, wkv_vis[1]).astype(BF16)
    lane = lax.broadcasted_iota(jnp.int32, (64, 192), 1)
    first_head = lane < VHEAD_DIM
    q_block = jnp.concatenate([jnp.where(first_head, q, 0.0), jnp.where(first_head, 0.0, q)], 0).astype(BF16)
    s_lat = dot(k_lat, q_block, 1, 1)
    m_lat = jnp.max(s_lat, axis=0, keepdims=True)

    def vision_chunk(c):
        ch = chunk(c)
        patch_load(c).wait()

        def norm(r, carry):
            rows = patches[pl.ds(pl.multiple_of(ch * 512 + r * 64, 64), 64), :].astype(F32)
            ctx[pl.ds(pl.multiple_of(r * 64, 64), 64), :] = layer_norm(rows).astype(BF16)
            return carry

        lax.fori_loop(0, 8, norm, 0)
        kc = dot(ctx[...], wkv_vis[0]).astype(BF16)
        vc = dot(ctx[...], wkv_vis[1]).astype(BF16)
        s = dot(kc, q_block, 1, 1).reshape(8, 64, 128)
        m = jnp.maximum(jnp.max(s, axis=1, keepdims=True), m_lat[None])
        e_ctx = jnp.exp(s - m)
        e_lat = jnp.exp(s_lat[None] - m)
        total = jnp.sum(e_ctx, axis=1, keepdims=True) + jnp.sum(e_lat, axis=1, keepdims=True)
        inverse = 1.0 / total
        p_ctx = (e_ctx * inverse).astype(BF16)
        p_lat = (e_lat * inverse).astype(BF16)
        mixed = []
        for v in range(8):
            p = jnp.concatenate([p_ctx[v], p_lat[v]], 0)
            values = jnp.concatenate([vc[v * 64:(v + 1) * 64], v_lat], 0)
            o = dot(p, values, 0, 0)
            mixed.append(jnp.where(first_head, o[:64], o[64:]))
        for u in range(8):
            rows = jnp.concatenate([o[u * 8:(u + 1) * 8] for o in mixed], 0)
            hs[u, ch, pl.ds(0, 64)] = rows[:, :128].astype(BF16)
            hs[u, ch, pl.ds(64, 32)] = jnp.concatenate([rows[:32, 128:], rows[32:, 128:]], 1).astype(BF16)

    def head_copy(c, j, inbound):
        ch = chunk(c)
        other = (t + (8 - j if inbound else j)) % 8
        i = c * 8 + j
        if inbound:
            return rc(hs.at[t, ch], hbuf.at[other, ch], has.at[i], har.at[i], tens(other))
        return rc(hs.at[other, ch], hbuf.at[t, ch], has.at[i], har.at[i], tens(other))

    def head_local(c):
        return pltpu.make_async_copy(hs.at[t, chunk(c)], hbuf.at[t, chunk(c)], lsem.at[4 + c])

    def head_start(c):
        for j in range(1, 8):
            head_copy(c, j, False).start()
        head_local(c).start()

    pl.semaphore_wait(barrier, 42)
    for cp in w1_copies(0, False) + wo_near(False):
        cp.start()
    for k in range(2):
        w0(k).start()

    vision_chunk(0)
    head_start(0)
    vision_chunk(1)
    head_start(1)
    for cp in wo_near(True):
        cp.wait_recv()
    for cp in wo_far(False):
        cp.start()
    vision_chunk(2)
    head_start(2)
    w2_start(0)
    vision_chunk(3)
    head_start(3)

    local_woa.wait()
    local_wob.wait()
    for cp in wo_far(True):
        cp.wait_recv()
    for o in range(4):
        for cp in wo_sibling(o, False):
            cp.start()
    for k in range(2):
        w0_in(k).wait_recv()
    for cp in w1_copies(1, False):
        cp.start()

    local_hidden.wait()

    def norm_tokens(r, carry):
        rows = pl.ds(pl.multiple_of(r * 16, 16), 16)
        tokn[rows, :] = layer_norm(tokn[rows, :].astype(F32)).astype(BF16)
        return carry

    lax.fori_loop(0, 16, norm_tokens, 0)

    for o in range(4):
        for cp in wo_sibling(o, True):
            cp.wait_recv()

    def v4(c, i, inbound):
        n = c * 8 + i
        if inbound:
            f = ((x - c + 4) % 4) * 8 + (dp % 8 + 8 - i) % 8
            return rc(latp.at[0], lall.at[t, f], v4s.at[n], v4r.at[n], {"dp": f, "tensor": t})
        s = ((x + c) % 4) * 8 + (dp % 8 + i) % 8
        return rc(latp.at[s], lall.at[t, dp], v4s.at[n], v4r.at[n], {"dp": s, "tensor": t})

    local_lat = pltpu.make_async_copy(latp.at[dp], lall.at[t, dp], lsem.at[13])
    my_base = base32[pl.ds(pl.multiple_of(t * 8, 8), 8), :]

    def project(c):
        ch = chunk(c)
        for j in range(1, 8):
            head_copy(c, j, True).wait_recv()
        head_local(c).wait()
        wide = jnp.concatenate([hbuf[g, ch, pl.ds(0, 64)] for g in range(8)], 1)
        narrow = []
        for g in range(8):
            packed = hbuf[g, ch, pl.ds(64, 32)]
            narrow.append(jnp.concatenate([packed[:, :64], packed[:, 64:]], 0))
        narrow = jnp.concatenate(narrow, 1)
        mix = dot(wide, woa[...].reshape(1024, 1280)) + dot(narrow, wob[...].reshape(512, 1280))
        mix = mix.reshape(8, 8, 1280) + my_base[None]
        mix = layer_norm(mix)
        lat_out[pl.ds(ch * 8, 8)] = mix.astype(BF16)
        latp[pl.ds(ch * 8, 8)] = jnp.concatenate([mix[:, :, :640], mix[:, :, 640:]], 1).astype(BF16)
        for i in range(8):
            if c == 0 and i == 0:
                local_lat.start()
            else:
                v4(c, i, False).start()

    project(0)
    project(1)
    w2_start(1)
    project(2)
    project(3)

    def frames(c):
        return pl.ds(((x - c + 4) % 4) * 8, 8)

    def line(up, j, c, inbound):
        away = j + 1 if inbound else j
        origin = zl - away if up else zl + away
        region = lall.at[origin * 2 + core, frames(c)]
        ss, rs = (ups, upr) if up else (dns, dnr)
        step = (2 if up else -2) * (-1 if inbound else 1)
        return rc(region, region, ss.at[j * 4 + c], rs.at[j * 4 + c], tens(t + step))

    def sib(origin, c, slot, inbound):
        region = lall.at[origin * 2 + (1 - core if inbound else core), frames(c)]
        return rc(region, region, lss.at[slot], lsr.at[slot], sibling)

    for c in range(4):
        for i in range(8):
            if c == 0 and i == 0:
                local_lat.wait()
            else:
                v4(c, i, True).wait_recv()
        pl.when(zl < 3)(lambda: line(True, 0, c, False).start())
        pl.when(zl > 0)(lambda: line(False, 0, c, False).start())
        sib(zl, c, c, False).start()

    def hop(j):
        for c in range(4):
            @pl.when(zl >= j)
            def _():
                line(True, j - 1, c, True).wait_recv()
                if j < 3:
                    pl.when(zl < 3)(lambda: line(True, j, c, False).start())
                sib(zl - j, c, j * 4 + c, False).start()

            @pl.when(zl + j <= 3)
            def _():
                line(False, j - 1, c, True).wait_recv()
                if j < 3:
                    pl.when(zl > 0)(lambda: line(False, j, c, False).start())
                sib(zl + j, c, (j + 3) * 4 + c, False).start()

    def query_half(zz, first):
        def step(i, carry):
            columns = pl.ds(pl.multiple_of((i * 2 + zz) * 1024, 1024), 1024)
            part = dot(tokn[:, columns], g1[i, zz].reshape(1024, 512))
            qacc[...] = qacc[...] + part
            return carry

        if first:
            qacc[...] = jnp.zeros_like(qacc)
        lax.fori_loop(0, 4, step, 0)

    def pack_weights(zz):
        for xx in range(4):
            rows = pl.ds(pl.multiple_of((xx * 2 + zz) * 160, 160), 160)
            for k in range(2):
                block = g2[xx, zz, :, k].astype(F32).reshape(160, 512)
                wkv[rows, k * 512:(k + 1) * 512] = block.astype(BF16)

    def attend(origin):
        lat = lall[origin].astype(F32)
        rows = jnp.concatenate([lat[:, :8], lat[:, 8:]], 2).reshape(256, 1280).astype(BF16)
        kv = dot(rows, wkv[...]).astype(BF16)
        ones = jnp.ones((256, 128), BF16)
        for h in range(4):
            own = slice(h * 128, (h + 1) * 128)
            s = dot(qh[:, own], kv[:, own], 1, 1) + bias[...]
            m_old = top[h]
            m = jnp.maximum(m_old, jnp.max(s, axis=1, keepdims=True))
            p = jnp.exp(s - m[:, :1]).astype(BF16)
            values = jnp.concatenate([kv[:, 512 + h * 128:512 + (h + 1) * 128], ones], 1)
            shrink = jnp.exp(m_old - m)
            acc[h] = acc[h] * jnp.concatenate([shrink, shrink], 1) + dot(p, values)
            top[h] = m

    hop(1)
    for cp in w2_copies(0, True):
        cp.wait_recv()
    query_half(zh, True)
    pack_weights(zh)
    limit = jnp.minimum(seen[...], frame_count[...])
    key_frame = lax.broadcasted_iota(jnp.int32, (256, 256), 0) // 8
    bias[...] = jnp.where(key_frame < limit, 0.0, MASKED).T
    top[...] = jnp.full_like(top, MASKED)
    acc[...] = jnp.zeros_like(acc)
    hop(2)
    for cp in w2_copies(1, True):
        cp.wait_recv()
    query_half(1 - zh, False)
    pack_weights(1 - zh)
    qh[...] = (qacc[...] * HEAD_DIM ** (-0.5)).astype(BF16)
    attend(t)
    hop(3)

    for c in range(4):
        sib(zl, c, c, True).wait_recv()
    attend(zl * 2 + 1 - core)

    for j in range(1, 4):
        for c in range(4):
            @pl.when(zl >= j)
            def _():
                sib(zl - j, c, j * 4 + c, True).wait_recv()

            @pl.when(zl + j <= 3)
            def _():
                sib(zl + j, c, (j + 3) * 4 + c, True).wait_recv()

    def others(j, carry):
        attend(((zl + j) % 4) * 2)
        attend(((zl + j) % 4) * 2 + 1)
        return carry

    lax.fori_loop(1, 4, others, 0)
    seen_any = bias[:, :1] == 0.0
    for h in range(4):
        result = acc[h]
        result = result[:, :128] / result[:, 128:]
        att_out[:, h * 128:(h + 1) * 128] = jnp.where(seen_any, result, 0.0).astype(BF16)

    for c in range(4):
        sib(zl, c, c, False).wait_send()
        pl.when(zl < 3)(lambda: line(True, 0, c, False).wait_send())
        pl.when(zl > 0)(lambda: line(False, 0, c, False).wait_send())
        for j in range(1, 4):
            @pl.when(zl >= j)
            def _():
                sib(zl - j, c, j * 4 + c, False).wait_send()
                if j < 3:
                    pl.when(zl < 3)(lambda: line(True, j, c, False).wait_send())

            @pl.when(zl + j <= 3)
            def _():
                sib(zl + j, c, (j + 3) * 4 + c, False).wait_send()
                if j < 3:
                    pl.when(zl > 0)(lambda: line(False, j, c, False).wait_send())
        for j in range(1, 8):
            head_copy(c, j, False).wait_send()
        for i in range(8):
            if not (c == 0 and i == 0):
                v4(c, i, False).wait_send()
    for b in range(2):
        for cp in w1_copies(b, False) + w2_copies(b, False):
            cp.wait_send()
    for k in range(2):
        w0(k).wait_send()
    for cp in wo_near(False) + wo_far(False):
        cp.wait_send()
    for o in range(4):
        for cp in wo_sibling(o, False):
            cp.wait_send()


def local(
    video_patches,
    frame_count,
    seen_frames,
    base_latents,
    vision_query,
    vision_kv,
    vision_out,
    hidden_states,
    text_query,
    text_kv,
):
    width = video_patches.shape[-1]
    vm = pl.BlockSpec(memory_space=pltpu.VMEM)
    hbm = pl.BlockSpec(memory_space=pl.ANY)
    dma = lambda n: pltpu.SemaphoreType.DMA((n,))
    latents_out, attended = pl.pallas_call(
        fused_kernel,
        name="fused",
        out_shape=(
            jax.ShapeDtypeStruct((32, 8, 1280), BF16),
            jax.ShapeDtypeStruct((256, 512), BF16),
        ),
        in_specs=[hbm, vm, vm, vm, vm, vm, hbm, hbm, hbm, hbm],
        out_specs=(vm, vm),
        scratch_shapes=[
            pltpu.VMEM((2048, 1280), BF16),
            pltpu.VMEM((512, 1280), BF16),
            pltpu.VMEM((8, 128, 1280), BF16),
            pltpu.VMEM((8, 64, 1280), BF16),
            pltpu.VMEM((8, 4, 96, 128), BF16),
            pltpu.VMEM((8, 4, 96, 128), BF16),
            pltpu.VMEM((64, 1280), F32),
            pltpu.VMEM((32, 16, 640), BF16),
            pltpu.VMEM((8, 32, 16, 640), BF16),
            pltpu.VMEM((4, 2, 4, 256, 512), BF16),
            pltpu.VMEM((4, 2, 4, 2, 40, 512), BF16),
            pltpu.VMEM((1280, 1024), BF16),
            pltpu.VMEM((256, 8192), BF16),
            pltpu.VMEM((256, 512), F32),
            pltpu.VMEM((256, 512), BF16),
            pltpu.VMEM((256, 256), F32),
            pltpu.VMEM((4, 256, 128), F32),
            pltpu.VMEM((4, 256, 256), F32),
            dma(14), dma(2), dma(2), dma(24), dma(24), dma(24), dma(24), dma(7), dma(7), dma(8), dma(8),
            dma(32), dma(32), dma(32), dma(32), dma(12), dma(12), dma(12), dma(12), dma(28), dma(28),
        ],
        compiler_params=pltpu.CompilerParams(
            collective_id=0, has_side_effects=True, vmem_limit_bytes=60 * 2**20
        ),
        cost_estimate=pl.CostEstimate(flops=14 * 10**9, bytes_accessed=40 * 10**6, transcendentals=3 * 10**6),
    )(
        video_patches.reshape(-1, width),
        frame_count.reshape(1, 1),
        seen_frames,
        base_latents,
        vision_query,
        vision_kv,
        vision_out,
        hidden_states,
        text_query,
        text_kv,
    )
    return latents_out[:, None], attended


def solution(mesh):
    placed = (
        P(None, "dp", None, None),
        P("dp"),
        P("dp", None),
        P(),
        P(None, "tensor"),
        P(None, None, "tensor"),
        P("tensor", None),
        P("dp", None),
        P("dp", "tensor"),
        P(None, "dp", "tensor"),
    )
    return jax.shard_map(
        local,
        mesh=mesh,
        in_specs=placed,
        out_specs=(P(None, "dp", "tensor", None), P("dp", "tensor")),
        check_vma=False,
    )
```

```python
import jax
import jax.numpy as jnp
from jax import lax
from jax.experimental import pallas as pl
from jax.experimental.pallas import tpu as pltpu
from jax.sharding import PartitionSpec as P

HEAD_DIM = 128
VHEAD_DIM = 96
EPSILON = 1e-05
MASKED = -1e30
MESH = pl.DeviceIdType.MESH
F32 = jnp.float32
BF16 = jnp.bfloat16


def layer_norm(values):
    average = jnp.mean(values, axis=-1, keepdims=True)
    centered = values - average
    variance = jnp.mean(centered * centered, axis=-1, keepdims=True)
    return centered * lax.rsqrt(variance + EPSILON)


def dot(a, b, ca=1, cb=0):
    return lax.dot_general(a, b, (((ca,), (cb,)), ((), ())), preferred_element_type=F32)


def fused_kernel(
    patches_in, frame_count, seen, base, wq, wkv_vis, wo_in, hidden_in, q_in, kv_in,
    lat_out, att_out,
    patches, ctx, woa, wob, hs, hbuf, base32, latp, lall, xown, transit, g1, g2, wkv, tokn, qacc, qh, bias, top, acc,
    lsem, w0s, w0r, w1s, w1r, w2s, w2r, wos, wor, sibs, sibr, has, har, v4s, v4r, ups, upr, dns, dnr, trs, trr, lss, lsr,
):
    dp = lax.axis_index("dp")
    t = lax.axis_index("tensor")
    x = dp // 8
    zh = (dp // 4) % 2
    y = dp % 4
    zl = t // 2
    core = t % 2
    z = zh * 4 + zl

    def at(xx, zz, yy):
        return {"dp": (xx * 2 + zz) * 4 + yy, "tensor": t}

    def ring(offset):
        zz = (z + offset + 8) % 8
        return {"dp": (x * 2 + zz // 4) * 4 + y, "tensor": (zz % 4) * 2 + core}

    def tens(tt):
        return {"dp": dp, "tensor": tt}

    sibling = tens(t + 1 - 2 * core)

    def rc(src, dst, ss, rs, device):
        return pltpu.make_async_remote_copy(
            src_ref=src, dst_ref=dst, send_sem=ss, recv_sem=rs, device_id=device, device_id_type=MESH
        )

    barrier = pltpu.get_barrier_semaphore()

    for j in range(1, 16):
        greeted = {"dp": ((x + j // 4) % 4 * 2 + zh) * 4 + (y + j % 4) % 4, "tensor": t}
        pl.semaphore_signal(barrier, inc=1, device_id=greeted, device_id_type=MESH)
    pl.semaphore_signal(barrier, inc=1, device_id=at(x, 1 - zh, y), device_id_type=MESH)
    for j in range(1, 8):
        pl.semaphore_signal(barrier, inc=1, device_id=tens((t + j) % 8), device_id_type=MESH)
    for o in (1, -1):
        pl.semaphore_signal(barrier, inc=1, device_id=ring(o), device_id_type=MESH)

    def chunk(c):
        return (x + c) % 4

    def patch_load(c):
        rows = pl.ds(pl.multiple_of(chunk(c) * 512, 512), 512)
        return pltpu.make_async_copy(patches_in.at[rows], patches.at[rows], lsem.at[8 + c])

    for c in range(4):
        patch_load(c).start()
    local_q = pltpu.make_async_copy(q_in, g1.at[x, zh, y], lsem.at[0])
    local_kv = pltpu.make_async_copy(kv_in, g2.at[x, zh, y], lsem.at[1])
    local_woa = pltpu.make_async_copy(wo_in.at[pl.ds(0, 128)], woa.at[t], lsem.at[2])
    local_wob = pltpu.make_async_copy(wo_in.at[pl.ds(128, 64)], wob.at[t], lsem.at[3])
    local_hidden = pltpu.make_async_copy(hidden_in, tokn, lsem.at[12])
    for cp in (local_q, local_kv, local_woa, local_wob, local_hidden):
        cp.start()

    def w0(k):
        src, dst = ((q_in, g1), (kv_in, g2))[k]
        return rc(src, dst.at[x, zh, y], w0s.at[k], w0r.at[k], at(x, 1 - zh, y))

    def w0_in(k):
        src, dst = ((q_in, g1), (kv_in, g2))[k]
        return rc(src, dst.at[x, 1 - zh, y], w0s.at[k], w0r.at[k], at(x, 1 - zh, y))

    halves = (pl.ds(0, 128), pl.ds(128, 128))
    quarters = ((pl.ds(0, 64), pl.ds(64, 64)), (pl.ds(128, 64), pl.ds(192, 64)))
    lanes = (pl.ds(0, 256), pl.ds(256, 256))
    pairs = (pl.ds(0, 2), pl.ds(2, 2))

    def along(d, o):
        return at(x, zh, (y + o + 4) % 4) if d == 0 else at((x + o + 4) % 4, zh, y)

    def place(d, o):
        return (x, (y + o + 4) % 4) if d == 0 else ((x + o + 4) % 4, y)

    def slot(b, d, m, k):
        return ((b * 2 + d) * 2 + m) * 2 + k

    def w1_near(b, inbound):
        zz = zh if b == 0 else 1 - zh
        out = []
        for d in range(2):
            for m, o in enumerate((1, -1)):
                bx, by = place(d, -o if inbound else 0)
                device = along(d, -o if inbound else o)
                for k in (1, 0):
                    if k == 0:
                        dst = g1.at[bx, zz, by, halves[d]]
                        src = q_in.at[halves[d]] if b == 0 else g1.at[x, zz, y, halves[d]]
                    else:
                        dst = g2.at[bx, zz, by, d]
                        src = kv_in.at[d] if b == 0 else g2.at[x, zz, y, d]
                    i = slot(b, d, m, k)
                    out.append(rc(src, dst, w1s.at[i], w1r.at[i], device))
        return out

    def w1_far(b, inbound):
        zz = zh if b == 0 else 1 - zh
        out = []
        for d in range(2):
            for m, o in enumerate((1, -1)):
                bx, by = place(d, -2 * o if inbound else -o)
                device = along(d, -o if inbound else o)
                for k in (1, 0):
                    region = g1.at[bx, zz, by, quarters[d][m]] if k == 0 else g2.at[bx, zz, by, d, :, lanes[m]]
                    i = 16 + slot(b, d, m, k)
                    out.append(rc(region, region, w1s.at[i], w1r.at[i], device))
        return out

    def w2_region(b, d, bx, by, part, k):
        zz = zh if b == 0 else 1 - zh
        if d == 0:
            return g1.at[bx, zz, part, halves[0]] if k == 0 else g2.at[bx, zz, part, 0]
        return g1.at[part, zz, by, halves[1]] if k == 0 else g2.at[part, zz, by, 1]

    def w2_near(b, inbound):
        out = []
        for d in range(2):
            for m, o in enumerate((1, -1)):
                bx, by = place(1 - d, -o if inbound else 0)
                device = along(1 - d, -o if inbound else o)
                for k in (1, 0):
                    region = w2_region(b, d, bx, by, pl.ds(0, 4), k)
                    i = slot(b, d, m, k)
                    out.append(rc(region, region, w2s.at[i], w2r.at[i], device))
        return out

    def w2_far(b, inbound):
        out = []
        for d in range(2):
            for m, o in enumerate((1, -1)):
                bx, by = place(1 - d, -2 * o if inbound else -o)
                device = along(1 - d, -o if inbound else o)
                for k in (1, 0):
                    region = w2_region(b, d, bx, by, pairs[m], k)
                    i = 16 + slot(b, d, m, k)
                    out.append(rc(region, region, w2s.at[i], w2r.at[i], device))
        return out

    def start(copies):
        for cp in copies:
            cp.start()

    def arrived(copies):
        for cp in copies:
            cp.wait_recv()

    def w1_forward(b):
        with jax.named_scope("w1_forward"):
            arrived(w1_near(b, True))
            start(w1_far(b, False))

    def w2_begin(b):
        with jax.named_scope("w2_begin"):
            if b == 0:
                local_q.wait()
                local_kv.wait()
            arrived(w1_far(b, True))
            start(w2_near(b, False))

    def w2_forward(b):
        with jax.named_scope("w2_forward"):
            arrived(w2_near(b, True))
            start(w2_far(b, False))

    def wo_block(o):
        return ((zl + o + 4) % 4) * 2 + core

    def wo_near(inbound):
        out = []
        for i, o in enumerate((1, -1)):
            block = wo_block(-o if inbound else 0)
            device = ring(-o if inbound else o)
            out.append(rc(wo_in.at[pl.ds(0, 128)], woa.at[block], wos.at[2 * i], wor.at[2 * i], device))
            out.append(rc(wo_in.at[pl.ds(128, 64)], wob.at[block], wos.at[2 * i + 1], wor.at[2 * i + 1], device))
        return out

    def wo_far(inbound):
        out = []
        for i, (o, part) in enumerate(((1, pl.ds(0, 96)), (-1, pl.ds(96, 32)), (-1, None))):
            block = wo_block(-2 * o if inbound else -o)
            device = ring(-o if inbound else o)
            region = wob.at[block] if part is None else woa.at[block, part]
            out.append(rc(region, region, wos.at[4 + i], wor.at[4 + i], device))
        return out

    def wo_sibling(o, inbound):
        block = o * 2 + (1 - core if inbound else core)
        return [
            rc(woa.at[block], woa.at[block], sibs.at[2 * o], sibr.at[2 * o], sibling),
            rc(wob.at[block], wob.at[block], sibs.at[2 * o + 1], sibr.at[2 * o + 1], sibling),
        ]

    base32[...] = base[...].astype(F32)
    lat_norm = layer_norm(base32[...]).astype(BF16)
    q = dot(lat_norm, wq[...], 1, 1) * VHEAD_DIM ** (-0.5)
    k_lat = dot(lat_norm, wkv_vis[0], 1, 1).astype(BF16)
    v_lat = dot(lat_norm, wkv_vis[1], 1, 1).astype(BF16)
    lane = lax.broadcasted_iota(jnp.int32, (64, 192), 1)
    first_head = lane < VHEAD_DIM
    q_block = jnp.concatenate([jnp.where(first_head, q, 0.0), jnp.where(first_head, 0.0, q)], 0).astype(BF16)
    s_lat = dot(k_lat, q_block, 1, 1)
    m_lat = jnp.max(s_lat, axis=0, keepdims=True)

    def vision_chunk(c):
        ch = chunk(c)
        patch_load(c).wait()

        def norm(r, carry):
            rows = patches[pl.ds(pl.multiple_of(ch * 512 + r * 64, 64), 64), :].astype(F32)
            ctx[pl.ds(pl.multiple_of(r * 64, 64), 64), :] = layer_norm(rows).astype(BF16)
            return carry

        lax.fori_loop(0, 8, norm, 0)
        kc = dot(ctx[...], wkv_vis[0], 1, 1).astype(BF16)
        vc = dot(ctx[...], wkv_vis[1], 1, 1).astype(BF16)
        s = dot(kc, q_block, 1, 1).reshape(8, 64, 128)
        m = jnp.maximum(jnp.max(s, axis=1, keepdims=True), m_lat[None])
        e_ctx = jnp.exp(s - m)
        e_lat = jnp.exp(s_lat[None] - m)
        total = jnp.sum(e_ctx, axis=1, keepdims=True) + jnp.sum(e_lat, axis=1, keepdims=True)
        inverse = 1.0 / total
        p_ctx = (e_ctx * inverse).astype(BF16)
        p_lat = (e_lat * inverse).astype(BF16)
        mixed = []
        for v in range(8):
            p = jnp.concatenate([p_ctx[v], p_lat[v]], 0)
            values = jnp.concatenate([vc[v * 64:(v + 1) * 64], v_lat], 0)
            o = dot(p, values, 0, 0)
            mixed.append(jnp.where(first_head, o[:64], o[64:]))
        for u in range(8):
            rows = jnp.concatenate([o[u * 8:(u + 1) * 8] for o in mixed], 0)
            hs[u, ch, pl.ds(0, 64)] = rows[:, :128].astype(BF16)
            hs[u, ch, pl.ds(64, 32)] = jnp.concatenate([rows[:32, 128:], rows[32:, 128:]], 1).astype(BF16)

    def head_copy(c, j, inbound):
        ch = chunk(c)
        other = (t + (8 - j if inbound else j)) % 8
        i = c * 8 + j
        if inbound:
            return rc(hs.at[t, ch], hbuf.at[other, ch], has.at[i], har.at[i], tens(other))
        return rc(hs.at[other, ch], hbuf.at[t, ch], has.at[i], har.at[i], tens(other))

    def head_local(c):
        return pltpu.make_async_copy(hs.at[t, chunk(c)], hbuf.at[t, chunk(c)], lsem.at[4 + c])

    def head_start(c):
        for j in range(1, 8):
            head_copy(c, j, False).start()
        head_local(c).start()

    with jax.named_scope("entry_barrier"):
        pl.semaphore_wait(barrier, 25)
    start(w1_near(0, False))
    start(wo_near(False))
    with jax.named_scope("vision_0"):
        vision_chunk(0)
    head_start(0)
    w1_forward(0)
    with jax.named_scope("vision_1"):
        vision_chunk(1)
    head_start(1)
    w2_begin(0)
    with jax.named_scope("vision_2"):
        vision_chunk(2)
    head_start(2)
    with jax.named_scope("wait_wo_near"):
        arrived(wo_near(True))
    start(wo_far(False))
    with jax.named_scope("vision_3"):
        vision_chunk(3)
    head_start(3)
    for k in range(2):
        w0(k).start()

    local_hidden.wait()

    def norm_tokens(r, carry):
        rows = pl.ds(pl.multiple_of(r * 16, 16), 16)
        tokn[rows, :] = layer_norm(tokn[rows, :].astype(F32)).astype(BF16)
        return carry

    with jax.named_scope("token_norm"):
        lax.fori_loop(0, 16, norm_tokens, 0)

    local_woa.wait()
    local_wob.wait()
    with jax.named_scope("wait_wo_far"):
        arrived(wo_far(True))
    for o in range(4):
        start(wo_sibling(o, False))
    w2_forward(0)
    with jax.named_scope("wait_wo_sibling"):
        for o in range(4):
            arrived(wo_sibling(o, True))

    def v4(c, i, inbound):
        n = (c * 4 + i) * 2
        if inbound:
            px, py = (x - c + 4) % 4, (y - i + 4) % 4
            device, mine, theirs, here = at(px, zh, py), x * 8 + y, x * 8 + y, px * 4 + py
        else:
            px, py = (x + c) % 4, (y + i) % 4
            device, mine, theirs, here = at(px, zh, py), px * 8 + zh * 4 + py, px * 8 + (1 - zh) * 4 + py, x * 4 + y
        return [
            rc(latp.at[mine], lall.at[zh, t, here], v4s.at[n], v4r.at[n], device),
            rc(latp.at[theirs], xown.at[here], v4s.at[n + 1], v4r.at[n + 1], device),
        ]

    local_lat = (
        pltpu.make_async_copy(latp.at[dp], lall.at[zh, t, x * 4 + y], lsem.at[13]),
        pltpu.make_async_copy(latp.at[x * 8 + (1 - zh) * 4 + y], xown.at[x * 4 + y], lsem.at[14]),
    )
    my_base = base32[pl.ds(pl.multiple_of(t * 8, 8), 8), :]

    def project(c):
        ch = chunk(c)
        with jax.named_scope("wait_heads"):
            for j in range(1, 8):
                head_copy(c, j, True).wait_recv()
            head_local(c).wait()
        wide = jnp.concatenate([hbuf[g, ch, pl.ds(0, 64)] for g in range(8)], 1)
        narrow = []
        for g in range(8):
            packed = hbuf[g, ch, pl.ds(64, 32)]
            narrow.append(jnp.concatenate([packed[:, :64], packed[:, 64:]], 0))
        narrow = jnp.concatenate(narrow, 1)
        mix = dot(wide, woa[...].reshape(1024, 1280)) + dot(narrow, wob[...].reshape(512, 1280))
        mix = mix.reshape(8, 8, 1280) + my_base[None]
        mix = layer_norm(mix)
        lat_out[pl.ds(ch * 8, 8)] = mix.astype(BF16)
        latp[pl.ds(ch * 8, 8)] = jnp.concatenate([mix[:, :, :640], mix[:, :, 640:]], 1).astype(BF16)
        for i in range(4):
            if c == 0 and i == 0:
                start(local_lat)
            else:
                start(v4(c, i, False))

    with jax.named_scope("project_0"):
        project(0)
    with jax.named_scope("project_1"):
        project(1)
    with jax.named_scope("project_2"):
        project(2)
    with jax.named_scope("project_3"):
        project(3)

    def part(c):
        return pl.ds(((x - c + 4) % 4) * 4, 4)

    def block(plane, own_core=True):
        return lall.at[plane // 4, (plane % 4) * 2 + (core if own_core else 1 - core)]

    def level(up):
        return zl if up else 3 - zl

    def flow(up, h, c, inbound, source=None):
        o = 1 if up else -1
        plane = (z - o * h + 8) % 8
        region = block(plane).at[part(c)]
        ss, rs = (ups, upr) if up else (dns, dnr)
        n = (h - 1 if inbound else h) * 4 + c
        src = region if source is None else source.at[part(c)]
        return rc(src, region, ss.at[n], rs.at[n], ring(-o if inbound else o))

    def pass_on(up, c):
        o = 1 if up else -1
        n = (0 if up else 4) + c
        return rc(xown.at[part(c)], transit.at[part(c)], trs.at[n], trr.at[n], ring(o))

    def sib(plane, c, inbound):
        region = block(plane, not inbound).at[part(c)]
        return rc(region, region, lss.at[plane * 4 + c], lsr.at[plane * 4 + c], sibling)

    def offset(up, h):
        return (z - h + 8) % 8 if up else (z + h) % 8

    def wave_own(c):
        for i in range(4):
            if c == 0 and i == 0:
                for cp in local_lat:
                    cp.wait()
            else:
                arrived(v4(c, i, True))
        for up in (True, False):
            at_level = level(up)
            pl.when(at_level < 3)(lambda: flow(up, 0, c, False).start())
            pl.when(at_level == 2)(lambda: pass_on(up, c).start())
            pl.when(at_level == 3)(lambda: flow(up, 0, c, False, xown).start())
        sib(z, c, False).start()

    def wave(h, c):
        for up in (True, False):
            at_level = level(up)
            if h == 1:
                @pl.when(at_level == 3)
                def _():
                    pass_on(up, c).wait_recv()
                    flow(up, 1, c, False, transit).start()

            @pl.when(at_level + 2 >= h)
            def _():
                flow(up, h, c, True).wait_recv()
                if h < 5:
                    pl.when(at_level < 3)(lambda: flow(up, h, c, False).start())
                sib(offset(up, h), c, False).start()

    def query_half(zz, first):
        def step(i, carry):
            columns = pl.ds(pl.multiple_of((i * 2 + zz) * 1024, 1024), 1024)
            part = dot(tokn[:, columns], g1[i, zz].reshape(1024, 512))
            qacc[...] = qacc[...] + part
            return carry

        if first:
            qacc[...] = jnp.zeros_like(qacc)
        lax.fori_loop(0, 4, step, 0)

    def pack_weights(zz):
        for xx in range(4):
            rows = pl.ds(pl.multiple_of((xx * 2 + zz) * 160, 160), 160)
            for k in range(2):
                block = g2[xx, zz, :, k].astype(F32).reshape(160, 512)
                wkv[rows, k * 512:(k + 1) * 512] = block.astype(BF16)

    def attend(plane):
        lat = lall[plane // 4, pl.ds((plane % 4) * 2, 2)].astype(F32).reshape(32, 16, 640)
        rows = jnp.concatenate([lat[:, :8], lat[:, 8:]], 2).reshape(256, 1280).astype(BF16)
        kv = dot(rows, wkv[...]).astype(BF16)
        ones = jnp.ones((256, 128), BF16)
        for h in range(4):
            own = slice(h * 128, (h + 1) * 128)
            s = dot(qh[:, own], kv[:, own], 1, 1) + bias[plane // 4]
            m_old = top[h]
            m = jnp.maximum(m_old, jnp.max(s, axis=1, keepdims=True))
            p = jnp.exp(s - m[:, :1]).astype(BF16)
            values = jnp.concatenate([kv[:, 512 + h * 128:512 + (h + 1) * 128], ones], 1)
            shrink = jnp.exp(m_old - m)
            acc[h] = acc[h] * jnp.concatenate([shrink, shrink], 1) + dot(p, values)
            top[h] = m

    def attend_ready(plane):
        for c in range(4):
            sib(plane, c, True).wait_recv()
        with jax.named_scope("attend"):
            attend(plane)

    def attend_wave(up, h):
        pl.when(level(up) + 2 >= h)(lambda: attend_ready(offset(up, h)))

    for k in range(2):
        w0_in(k).wait_recv()
    start(w1_near(1, False))
    with jax.named_scope("wave_own"):
        for c in range(4):
            wave_own(c)
    w1_forward(1)
    with jax.named_scope("query_0"):
        arrived(w2_far(0, True))
        query_half(zh, True)
        pack_weights(zh)
    limit = jnp.minimum(seen[...], frame_count[...])
    row = lax.broadcasted_iota(jnp.int32, (256, 256), 0) % 128 // 8
    for zz in range(2):
        key_frame = row // 4 * 8 + zz * 4 + row % 4
        bias[zz] = jnp.where(key_frame < limit, 0.0, MASKED).T
    top[...] = jnp.full_like(top, MASKED)
    acc[...] = jnp.zeros_like(acc)
    w2_begin(1)
    with jax.named_scope("wave_1"):
        for c in range(4):
            wave(1, c)
    with jax.named_scope("wave_2"):
        for c in range(4):
            wave(2, c)
    w2_forward(1)
    with jax.named_scope("wave_3"):
        for c in range(4):
            wave(3, c)
    with jax.named_scope("query_1"):
        arrived(w2_far(1, True))
        query_half(1 - zh, False)
        pack_weights(1 - zh)
        qh[...] = (qacc[...] * HEAD_DIM ** (-0.5)).astype(BF16)
    attend_ready(z)
    for h in (1, 2):
        for up in (True, False):
            attend_wave(up, h)
            for c in (0, 1) if up else (2, 3):
                wave(h + 3, c)
    for h in (3, 4, 5):
        for up in (True, False):
            attend_wave(up, h)
    seen_any = bias[0, :, :1] == 0.0
    for h in range(4):
        result = acc[h]
        result = result[:, :128] / result[:, 128:]
        att_out[:, h * 128:(h + 1) * 128] = jnp.where(seen_any, result, 0.0).astype(BF16)

    for c in range(4):
        sib(z, c, False).wait_send()
        for up in (True, False):
            at_level = level(up)
            flow(up, 0, c, False).wait_send()
            pl.when(at_level == 2)(lambda: pass_on(up, c).wait_send())
            pl.when(at_level == 3)(lambda: flow(up, 1, c, False).wait_send())
            for h in range(1, 6):
                @pl.when(at_level + 2 >= h)
                def _():
                    if h < 5:
                        pl.when(at_level < 3)(lambda: flow(up, h, c, False).wait_send())
                    sib(offset(up, h), c, False).wait_send()

        for j in range(1, 8):
            head_copy(c, j, False).wait_send()
        for i in range(4):
            if not (c == 0 and i == 0):
                for cp in v4(c, i, False):
                    cp.wait_send()
    for b in range(2):
        for cp in w1_near(b, False) + w1_far(b, False) + w2_near(b, False) + w2_far(b, False):
            cp.wait_send()
    for k in range(2):
        w0(k).wait_send()
    for cp in wo_near(False) + wo_far(False):
        cp.wait_send()
    for o in range(4):
        for cp in wo_sibling(o, False):
            cp.wait_send()


def local(
    video_patches,
    frame_count,
    seen_frames,
    base_latents,
    vision_query,
    vision_kv,
    vision_out,
    hidden_states,
    text_query,
    text_kv,
):
    width = video_patches.shape[-1]
    vm = pl.BlockSpec(memory_space=pltpu.VMEM)
    hbm = pl.BlockSpec(memory_space=pl.ANY)
    dma = lambda n: pltpu.SemaphoreType.DMA((n,))
    latents_out, attended = pl.pallas_call(
        fused_kernel,
        name="fused",
        out_shape=(
            jax.ShapeDtypeStruct((32, 8, 1280), BF16),
            jax.ShapeDtypeStruct((256, 512), BF16),
        ),
        in_specs=[hbm, vm, vm, vm, vm, vm, hbm, hbm, hbm, hbm],
        out_specs=(vm, vm),
        scratch_shapes=[
            pltpu.VMEM((2048, 1280), BF16),
            pltpu.VMEM((512, 1280), BF16),
            pltpu.VMEM((8, 128, 1280), BF16),
            pltpu.VMEM((8, 64, 1280), BF16),
            pltpu.VMEM((8, 4, 96, 128), BF16),
            pltpu.VMEM((8, 4, 96, 128), BF16),
            pltpu.VMEM((64, 1280), F32),
            pltpu.VMEM((32, 16, 640), BF16),
            pltpu.VMEM((2, 8, 16, 16, 640), BF16),
            pltpu.VMEM((16, 16, 640), BF16),
            pltpu.VMEM((16, 16, 640), BF16),
            pltpu.VMEM((4, 2, 4, 256, 512), BF16),
            pltpu.VMEM((4, 2, 4, 2, 40, 512), BF16),
            pltpu.VMEM((1280, 1024), BF16),
            pltpu.VMEM((256, 8192), BF16),
            pltpu.VMEM((256, 512), F32),
            pltpu.VMEM((256, 512), BF16),
            pltpu.VMEM((2, 256, 256), F32),
            pltpu.VMEM((4, 256, 128), F32),
            pltpu.VMEM((4, 256, 256), F32),
            dma(15), dma(2), dma(2), dma(32), dma(32), dma(32), dma(32), dma(7), dma(7), dma(8), dma(8),
            dma(32), dma(32), dma(32), dma(32), dma(20), dma(20), dma(20), dma(20), dma(8), dma(8), dma(32), dma(32),
        ],
        compiler_params=pltpu.CompilerParams(
            collective_id=0, has_side_effects=True, vmem_limit_bytes=60 * 2**20
        ),
        cost_estimate=pl.CostEstimate(flops=14 * 10**9, bytes_accessed=40 * 10**6, transcendentals=3 * 10**6),
    )(
        video_patches.reshape(-1, width),
        frame_count.reshape(1, 1),
        seen_frames,
        base_latents,
        vision_query.T,
        vision_kv.transpose(0, 2, 1),
        vision_out,
        hidden_states,
        text_query,
        text_kv,
    )
    return latents_out[:, None], attended


def solution(mesh):
    placed = (
        P(None, "dp", None, None),
        P("dp"),
        P("dp", None),
        P(),
        P(None, "tensor"),
        P(None, None, "tensor"),
        P("tensor", None),
        P("dp", None),
        P("dp", "tensor"),
        P(None, "dp", "tensor"),
    )
    return jax.shard_map(
        local,
        mesh=mesh,
        in_specs=placed,
        out_specs=(P(None, "dp", "tensor", None), P("dp", "tensor")),
        check_vma=False,
    )
```

```python
import jax
import jax.numpy as jnp
from jax import lax
from jax.experimental import pallas as pl
from jax.experimental.pallas import tpu as pltpu
from jax.sharding import PartitionSpec as P

HEAD_DIM = 128
VHEAD_DIM = 96
EPSILON = 1e-05
MASKED = -1e30
MESH = pl.DeviceIdType.MESH
F32 = jnp.float32
BF16 = jnp.bfloat16


def layer_norm(values):
    average = jnp.mean(values, axis=-1, keepdims=True)
    centered = values - average
    variance = jnp.mean(centered * centered, axis=-1, keepdims=True)
    return centered * lax.rsqrt(variance + EPSILON)


def dot(a, b, ca=1, cb=0):
    return lax.dot_general(a, b, (((ca,), (cb,)), ((), ())), preferred_element_type=F32)


def fused_kernel(
    patches_in, frame_count, seen, base, wq, wkv_vis, wo_in, hidden_in, q_in, kv_in,
    lat_out, att_out,
    patches, ctx, wo, hs, hbuf, base32, latp, lall, xown, transit, g1, g2, wkv, tokn, qacc, qh, kv_text, bias, top, acc,
    lsem, w0s, w0r, w1s, w1r, w2s, w2r, wos, wor, sibs, sibr, has, har, v4s, v4r, ups, upr, dns, dnr, trs, trr, lss, lsr,
):
    dp = lax.axis_index("dp")
    t = lax.axis_index("tensor")
    x = dp // 8
    zh = (dp // 4) % 2
    y = dp % 4
    zl = t // 2
    core = t % 2
    z = zh * 4 + zl

    def at(xx, zz, yy):
        return {"dp": (xx * 2 + zz) * 4 + yy, "tensor": t}

    def ring(offset):
        zz = (z + offset + 8) % 8
        return {"dp": (x * 2 + zz // 4) * 4 + y, "tensor": (zz % 4) * 2 + core}

    def tens(tt):
        return {"dp": dp, "tensor": tt}

    sibling = tens(t + 1 - 2 * core)

    def rc(src, dst, ss, rs, device):
        return pltpu.make_async_remote_copy(
            src_ref=src, dst_ref=dst, send_sem=ss, recv_sem=rs, device_id=device, device_id_type=MESH
        )

    barrier = pltpu.get_barrier_semaphore()

    for j in range(1, 16):
        greeted = {"dp": ((x + j // 4) % 4 * 2 + zh) * 4 + (y + j % 4) % 4, "tensor": t}
        pl.semaphore_signal(barrier, inc=1, device_id=greeted, device_id_type=MESH)
    pl.semaphore_signal(barrier, inc=1, device_id=at(x, 1 - zh, y), device_id_type=MESH)
    for j in range(1, 8):
        pl.semaphore_signal(barrier, inc=1, device_id=tens((t + j) % 8), device_id_type=MESH)
    for o in (1, -1, 2, -2):
        pl.semaphore_signal(barrier, inc=1, device_id=ring(o), device_id_type=MESH)

    def chunk(c):
        return (x + c) % 4

    def patch_load(c):
        rows = pl.ds(pl.multiple_of(chunk(c) * 512, 512), 512)
        return pltpu.make_async_copy(patches_in.at[rows], patches.at[rows], lsem.at[8 + c])

    for c in range(4):
        patch_load(c).start()
    local_q = pltpu.make_async_copy(q_in, g1.at[x, zh, y], lsem.at[0])
    local_kv = pltpu.make_async_copy(kv_in, g2.at[x, zh, y], lsem.at[1])
    local_wo = pltpu.make_async_copy(wo_in, wo.at[t], lsem.at[2])
    local_hidden = pltpu.make_async_copy(hidden_in, tokn, lsem.at[12])
    for cp in (local_q, local_kv, local_wo, local_hidden):
        cp.start()

    def w0(k):
        src, dst = ((q_in, g1), (kv_in, g2))[k]
        return rc(src, dst.at[x, zh, y], w0s.at[k], w0r.at[k], at(x, 1 - zh, y))

    def w0_in(k):
        src, dst = ((q_in, g1), (kv_in, g2))[k]
        return rc(src, dst.at[x, 1 - zh, y], w0s.at[k], w0r.at[k], at(x, 1 - zh, y))

    halves = (pl.ds(0, 128), pl.ds(128, 128))
    quarters = ((pl.ds(0, 64), pl.ds(64, 64)), (pl.ds(128, 64), pl.ds(192, 64)))
    lanes = (pl.ds(0, 256), pl.ds(256, 256))
    pairs = (pl.ds(0, 2), pl.ds(2, 2))

    def along(d, o):
        return at(x, zh, (y + o + 4) % 4) if d == 0 else at((x + o + 4) % 4, zh, y)

    def place(d, o):
        return (x, (y + o + 4) % 4) if d == 0 else ((x + o + 4) % 4, y)

    def slot(b, d, m, k):
        return ((b * 2 + d) * 2 + m) * 2 + k

    def w1_near(b, inbound, ks=(1, 0)):
        zz = zh if b == 0 else 1 - zh
        out = []
        for d in range(2):
            for m, o in enumerate((1, -1)):
                bx, by = place(d, -o if inbound else 0)
                device = along(d, -o if inbound else o)
                for k in ks:
                    if k == 0:
                        dst = g1.at[bx, zz, by, halves[d]]
                        src = q_in.at[halves[d]] if b == 0 else g1.at[x, zz, y, halves[d]]
                    else:
                        dst = g2.at[bx, zz, by, d]
                        src = kv_in.at[d] if b == 0 else g2.at[x, zz, y, d]
                    i = slot(b, d, m, k)
                    out.append(rc(src, dst, w1s.at[i], w1r.at[i], device))
        return out

    def w1_far(b, inbound, ks=(1, 0)):
        zz = zh if b == 0 else 1 - zh
        out = []
        for d in range(2):
            for m, o in enumerate((1, -1)):
                bx, by = place(d, -2 * o if inbound else -o)
                device = along(d, -o if inbound else o)
                for k in ks:
                    region = g1.at[bx, zz, by, quarters[d][m]] if k == 0 else g2.at[bx, zz, by, d, :, lanes[m]]
                    i = 16 + slot(b, d, m, k)
                    out.append(rc(region, region, w1s.at[i], w1r.at[i], device))
        return out

    def w2_region(b, d, bx, by, part, k):
        zz = zh if b == 0 else 1 - zh
        if d == 0:
            return g1.at[bx, zz, part, halves[0]] if k == 0 else g2.at[bx, zz, part, 0]
        return g1.at[part, zz, by, halves[1]] if k == 0 else g2.at[part, zz, by, 1]

    def w2_near(b, inbound, ks=(1, 0)):
        out = []
        for d in range(2):
            for m, o in enumerate((1, -1)):
                bx, by = place(1 - d, -o if inbound else 0)
                device = along(1 - d, -o if inbound else o)
                for k in ks:
                    region = w2_region(b, d, bx, by, pl.ds(0, 4), k)
                    i = slot(b, d, m, k)
                    out.append(rc(region, region, w2s.at[i], w2r.at[i], device))
        return out

    def w2_far(b, inbound, ks=(1, 0)):
        out = []
        for d in range(2):
            for m, o in enumerate((1, -1)):
                bx, by = place(1 - d, -2 * o if inbound else -o)
                device = along(1 - d, -o if inbound else o)
                for k in ks:
                    region = w2_region(b, d, bx, by, pairs[m], k)
                    i = 16 + slot(b, d, m, k)
                    out.append(rc(region, region, w2s.at[i], w2r.at[i], device))
        return out

    def start(copies):
        for cp in copies:
            cp.start()

    def arrived(copies):
        for cp in copies:
            cp.wait_recv()

    def w1_forward(b, ks=(1, 0)):
        with jax.named_scope("w1_forward"):
            arrived(w1_near(b, True, ks))
            start(w1_far(b, False, ks))

    def w2_begin(b, ks=(1, 0)):
        with jax.named_scope("w2_begin"):
            if b == 0:
                local_q.wait()
                local_kv.wait()
            arrived(w1_far(b, True, ks))
            start(w2_near(b, False, ks))

    def w2_forward(b, ks=(1, 0)):
        with jax.named_scope("w2_forward"):
            arrived(w2_near(b, True, ks))
            start(w2_far(b, False, ks))

    columns = (pl.ds(0, 640), pl.ds(640, 640))

    def quarter(d, px, py):
        return pl.ds(pl.multiple_of((px if d == 0 else py) * 48, 16), 48)

    def wo_z(inbound):
        out = []
        for i, (o, d) in enumerate(((1, 0), (1, 1), (-1, 0), (-1, 1), (2, 0), (-2, 1))):
            plane = (zl - o + 4) % 4 if inbound else zl
            rows = quarter(d, x, y)
            out.append(
                rc(
                    wo_in.at[rows, columns[d]], wo.at[plane * 2 + core, rows, columns[d]], wos.at[i], wor.at[i],
                    ring(-o if inbound else o),
                )
            )
        return out

    def wo_plane(j, inbound):
        out = []
        for o in (1, 3, 2):
            for d in range(2):
                sign = -o if inbound else o
                px, py = ((x + sign + 4) % 4, y) if d == 0 else (x, (y + sign + 4) % 4)
                rows = quarter(d, px, py) if inbound else quarter(d, x, y)
                region = wo.at[((zl + j) % 4) * 2 + core, rows, columns[d]]
                n = 6 + (j - 1) * 6 + (o - 1) * 2 + d
                out.append(rc(region, region, wos.at[n], wor.at[n], at(px, zh, py)))
        return out

    def wo_sibling(j, inbound):
        region = wo.at[((zl + j) % 4) * 2 + (1 - core if inbound else core)]
        return rc(region, region, sibs.at[j], sibr.at[j], sibling)

    base32[...] = base[...].astype(F32)
    lat_norm = layer_norm(base32[...]).astype(BF16)
    q = dot(lat_norm, wq[...], 1, 1) * VHEAD_DIM ** (-0.5)
    k_lat = dot(lat_norm, wkv_vis[0], 1, 1).astype(BF16)
    v_lat = dot(lat_norm, wkv_vis[1], 1, 1).astype(BF16)
    lane = lax.broadcasted_iota(jnp.int32, (64, 192), 1)
    first_head = lane < VHEAD_DIM
    q_block = jnp.concatenate([jnp.where(first_head, q, 0.0), jnp.where(first_head, 0.0, q)], 0).astype(BF16)
    s_lat = dot(k_lat, q_block, 1, 1)
    m_lat = jnp.max(s_lat, axis=0, keepdims=True)

    def vision_chunk(c):
        ch = chunk(c)
        patch_load(c).wait()

        def norm(r, carry):
            rows = patches[pl.ds(pl.multiple_of(ch * 512 + r * 64, 64), 64), :].astype(F32)
            ctx[pl.ds(pl.multiple_of(r * 64, 64), 64), :] = layer_norm(rows).astype(BF16)
            return carry

        lax.fori_loop(0, 8, norm, 0)
        kc = dot(ctx[...], wkv_vis[0], 1, 1).astype(BF16)
        vc = dot(ctx[...], wkv_vis[1], 1, 1).astype(BF16)
        s = dot(kc, q_block, 1, 1).reshape(8, 64, 128)
        m = jnp.maximum(jnp.max(s, axis=1, keepdims=True), m_lat[None])
        e_ctx = jnp.exp(s - m)
        e_lat = jnp.exp(s_lat[None] - m)
        total = jnp.sum(e_ctx, axis=1, keepdims=True) + jnp.sum(e_lat, axis=1, keepdims=True)
        inverse = 1.0 / total
        p_ctx = (e_ctx * inverse).astype(BF16)
        p_lat = (e_lat * inverse).astype(BF16)
        mixed = []
        for v in range(8):
            p = jnp.concatenate([p_ctx[v], p_lat[v]], 0)
            values = jnp.concatenate([vc[v * 64:(v + 1) * 64], v_lat], 0)
            o = dot(p, values, 0, 0)
            mixed.append(jnp.where(first_head, o[:64], o[64:]))
        for u in range(8):
            rows = jnp.concatenate([o[u * 8:(u + 1) * 8] for o in mixed], 0)
            hs[u, ch, pl.ds(0, 64)] = rows[:, :128].astype(BF16)
            hs[u, ch, pl.ds(64, 32)] = jnp.concatenate([rows[:32, 128:], rows[32:, 128:]], 1).astype(BF16)

    def head_copy(c, j):
        ch = chunk(c)
        other = (t + j) % 8
        return rc(hs.at[other, ch], hbuf.at[t, ch], has.at[c], har.at[c], tens(other))

    def head_group(c):
        return rc(hs.at[pl.ds(0, 7), chunk(c)], hbuf.at[pl.ds(0, 7), chunk(c)], has.at[c], har.at[c], sibling)

    def head_local(c):
        return pltpu.make_async_copy(hs.at[t, chunk(c)], hbuf.at[t, chunk(c)], lsem.at[4 + c])

    def head_start(c):
        for j in range(1, 8):
            head_copy(c, j).start()
        head_local(c).start()

    with jax.named_scope("vision_0"):
        vision_chunk(0)
    with jax.named_scope("entry_barrier"):
        pl.semaphore_wait(barrier, 27)
    start(wo_z(False))
    head_start(0)
    w0(1).start()
    start(w1_near(0, False))
    with jax.named_scope("vision_1"):
        vision_chunk(1)
    head_start(1)
    w1_forward(0)
    local_wo.wait()
    wo_sibling(0, False).start()
    with jax.named_scope("vision_2"):
        vision_chunk(2)
    head_start(2)
    with jax.named_scope("wo_plane"):
        arrived(wo_z(True))
        for j in range(1, 4):
            start(wo_plane(j, False))
    w2_begin(0)
    with jax.named_scope("vision_3"):
        vision_chunk(3)
    head_start(3)
    w0(0).start()
    w0_in(1).wait_recv()
    start(w1_near(1, False, (1,)))

    local_hidden.wait()

    def norm_tokens(r, carry):
        rows = pl.ds(pl.multiple_of(r * 16, 16), 16)
        tokn[rows, :] = layer_norm(tokn[rows, :].astype(F32)).astype(BF16)
        return carry

    with jax.named_scope("token_norm"):
        lax.fori_loop(0, 8, norm_tokens, 0)
    w1_forward(1, (1,))
    with jax.named_scope("token_norm"):
        lax.fori_loop(8, 16, norm_tokens, 0)
    w2_begin(1, (1,))

    with jax.named_scope("wait_wo_plane"):
        for j in range(1, 4):
            arrived(wo_plane(j, True))
            wo_sibling(j, False).start()
    with jax.named_scope("wait_wo_sibling"):
        for j in range(4):
            wo_sibling(j, True).wait_recv()

    def v4(c, i):
        px, py = (x + c) % 4, (y + i) % 4
        device, mine, theirs, here = at(px, zh, py), px * 8 + zh * 4 + py, px * 8 + (1 - zh) * 4 + py, x * 4 + y
        return [
            rc(latp.at[mine], lall.at[zh, t, here], v4s.at[c * 2], v4r.at[c * 2], device),
            rc(latp.at[theirs], xown.at[here], v4s.at[c * 2 + 1], v4r.at[c * 2 + 1], device),
        ]

    def v4_group(c):
        some = pl.ds(0, 3 if c == 0 else 4)
        return [
            rc(latp.at[some], lall.at[zh, t, some], v4s.at[c * 2], v4r.at[c * 2], sibling),
            rc(latp.at[some], xown.at[some], v4s.at[c * 2 + 1], v4r.at[c * 2 + 1], sibling),
        ]

    local_lat = (
        pltpu.make_async_copy(latp.at[dp], lall.at[zh, t, x * 4 + y], lsem.at[13]),
        pltpu.make_async_copy(latp.at[x * 8 + (1 - zh) * 4 + y], xown.at[x * 4 + y], lsem.at[14]),
    )
    my_base = base32[pl.ds(pl.multiple_of(t * 8, 8), 8), :]

    def project(c):
        ch = chunk(c)
        with jax.named_scope("wait_heads"):
            head_group(c).wait_recv()
            head_local(c).wait()
        wide = jnp.concatenate([hbuf[g, ch, pl.ds(0, 64)] for g in range(8)], 1)
        narrow = []
        for g in range(8):
            packed = hbuf[g, ch, pl.ds(64, 32)]
            narrow.append(jnp.concatenate([packed[:, :64], packed[:, 64:]], 0))
        narrow = jnp.concatenate(narrow, 1)
        mix = dot(wide, wo[:, :128].reshape(1024, 1280)) + dot(narrow, wo[:, 128:].reshape(512, 1280))
        mix = mix.reshape(8, 8, 1280) + my_base[None]
        mix = layer_norm(mix)
        lat_out[pl.ds(ch * 8, 8)] = mix.astype(BF16)
        latp[pl.ds(ch * 8, 8)] = jnp.concatenate([mix[:, :, :640], mix[:, :, 640:]], 1).astype(BF16)
        for i in range(4):
            if c == 0 and i == 0:
                start(local_lat)
            else:
                start(v4(c, i))

    with jax.named_scope("project_0"):
        project(0)
    with jax.named_scope("project_1"):
        project(1)
    with jax.named_scope("project_2"):
        project(2)
    with jax.named_scope("project_3"):
        project(3)

    def part(c):
        return pl.ds(((x - c + 4) % 4) * 4, 4)

    def block(plane, own_core=True):
        return lall.at[plane // 4, (plane % 4) * 2 + (core if own_core else 1 - core)]

    def level(up):
        return zl if up else 3 - zl

    def flow(up, h, c, inbound, source=None):
        o = 1 if up else -1
        plane = (z - o * h + 8) % 8
        region = block(plane).at[part(c)]
        ss, rs = (ups, upr) if up else (dns, dnr)
        n = (h - 1 if inbound else h) * 4 + c
        src = region if source is None else source.at[part(c)]
        return rc(src, region, ss.at[n], rs.at[n], ring(-o if inbound else o))

    def pass_on(up, c):
        o = 1 if up else -1
        n = (0 if up else 4) + c
        return rc(xown.at[part(c)], transit.at[part(c)], trs.at[n], trr.at[n], ring(o))

    def sib(plane, c, inbound):
        region = block(plane, not inbound).at[part(c)]
        return rc(region, region, lss.at[plane * 4 + c], lsr.at[plane * 4 + c], sibling)

    def offset(up, h):
        return (z - h + 8) % 8 if up else (z + h) % 8

    def wave_own(c):
        if c == 0:
            for cp in local_lat:
                cp.wait()
        arrived(v4_group(c))
        for up in (True, False):
            at_level = level(up)
            pl.when(at_level < 3)(lambda: flow(up, 0, c, False).start())
            pl.when(at_level == 2)(lambda: pass_on(up, c).start())
            pl.when(at_level == 3)(lambda: flow(up, 0, c, False, xown).start())
        sib(z, c, False).start()

    def wave(h, c):
        for up in (True, False):
            at_level = level(up)
            if h == 1:
                @pl.when(at_level == 3)
                def _():
                    pass_on(up, c).wait_recv()
                    flow(up, 1, c, False, transit).start()

            @pl.when(at_level + 2 >= h)
            def _():
                flow(up, h, c, True).wait_recv()
                if h < 5:
                    pl.when(at_level < 3)(lambda: flow(up, h, c, False).start())
                sib(offset(up, h), c, False).start()

    def query_half(zz, first):
        def step(i, carry):
            columns = pl.ds(pl.multiple_of((i * 2 + zz) * 1024, 1024), 1024)
            part = dot(tokn[:, columns], g1[i, zz].reshape(1024, 512))
            qacc[...] = qacc[...] + part
            return carry

        if first:
            qacc[...] = jnp.zeros_like(qacc)
        lax.fori_loop(0, 4, step, 0)

    def pack_weights(zz):
        for xx in range(4):
            rows = pl.ds(pl.multiple_of((xx * 2 + zz) * 160, 160), 160)
            for k in range(2):
                block = g2[xx, zz, :, k].astype(F32).reshape(160, 512)
                wkv[rows, k * 512:(k + 1) * 512] = block.astype(BF16)

    def project_text(plane):
        lat = lall[plane // 4, pl.ds((plane % 4) * 2, 2)].astype(F32).reshape(32, 16, 640)
        rows = jnp.concatenate([lat[:, :8], lat[:, 8:]], 2).reshape(256, 1280).astype(BF16)
        kv_text[plane] = dot(rows, wkv[...]).astype(BF16)

    def attend(plane):
        ones = jnp.ones((256, 128), BF16)
        for h in range(4):
            own = slice(h * 128, (h + 1) * 128)
            s = dot(qh[:, own], kv_text[plane, :, own], 1, 1) + bias[plane // 4]
            m_old = top[h]
            m = jnp.maximum(m_old, jnp.max(s, axis=1, keepdims=True))
            p = jnp.exp(s - m[:, :1]).astype(BF16)
            values = jnp.concatenate([kv_text[plane, :, 512 + h * 128:512 + (h + 1) * 128], ones], 1)
            shrink = jnp.exp(m_old - m)
            acc[h] = acc[h] * jnp.concatenate([shrink, shrink], 1) + dot(p, values)
            top[h] = m

    def kv_ready(plane):
        for c in range(4):
            sib(plane, c, True).wait_recv()
        with jax.named_scope("project_text"):
            project_text(plane)

    def kv_wave(up, h):
        pl.when(level(up) + 2 >= h)(lambda: kv_ready(offset(up, h)))

    def attend_wave(up, h):
        @pl.when(level(up) + 2 >= h)
        def _():
            with jax.named_scope("attend"):
                attend(offset(up, h))

    w2_forward(0)
    w2_forward(1, (1,))
    w0_in(0).wait_recv()
    start(w1_near(1, False, (0,)))
    with jax.named_scope("wave_own"):
        for c in range(4):
            wave_own(c)
    w1_forward(1, (0,))
    limit = jnp.minimum(seen[...], frame_count[...])
    row = lax.broadcasted_iota(jnp.int32, (256, 256), 0) % 128 // 8
    for zz in range(2):
        key_frame = row // 4 * 8 + zz * 4 + row % 4
        bias[zz] = jnp.where(key_frame < limit, 0.0, MASKED).T
    top[...] = jnp.full_like(top, MASKED)
    acc[...] = jnp.zeros_like(acc)
    w2_begin(1, (0,))
    with jax.named_scope("wave_1"):
        for c in range(4):
            wave(1, c)
    with jax.named_scope("query_0"):
        arrived(w2_far(0, True))
        query_half(zh, True)
    with jax.named_scope("pack"):
        arrived(w2_far(1, True, (1,)))
        pack_weights(zh)
        pack_weights(1 - zh)
    with jax.named_scope("wave_2"):
        for c in range(4):
            wave(2, c)
    kv_ready(z)
    kv_wave(True, 1)
    w2_forward(1, (0,))
    kv_wave(False, 1)
    with jax.named_scope("wave_3"):
        for c in range(4):
            wave(3, c)
    kv_wave(True, 2)
    kv_wave(False, 2)
    with jax.named_scope("wave_4"):
        for c in range(4):
            wave(4, c)
    with jax.named_scope("query_1"):
        arrived(w2_far(1, True, (0,)))
        query_half(1 - zh, False)
        qh[...] = (qacc[...] * HEAD_DIM ** (-0.5)).astype(BF16)
    with jax.named_scope("attend"):
        attend(z)
    with jax.named_scope("wave_5"):
        for c in range(4):
            wave(5, c)
    kv_wave(True, 3)
    kv_wave(False, 3)
    for h in (1, 2, 3):
        for up in (True, False):
            attend_wave(up, h)
    for h in (4, 5):
        for up in (True, False):
            kv_wave(up, h)
            attend_wave(up, h)
    seen_any = bias[0, :, :1] == 0.0
    for h in range(4):
        result = acc[h]
        result = result[:, :128] / result[:, 128:]
        att_out[:, h * 128:(h + 1) * 128] = jnp.where(seen_any, result, 0.0).astype(BF16)

    for c in range(4):
        sib(z, c, False).wait_send()
        for up in (True, False):
            at_level = level(up)
            flow(up, 0, c, False).wait_send()
            pl.when(at_level == 2)(lambda: pass_on(up, c).wait_send())
            pl.when(at_level == 3)(lambda: flow(up, 1, c, False).wait_send())
            for h in range(1, 6):
                @pl.when(at_level + 2 >= h)
                def _():
                    if h < 5:
                        pl.when(at_level < 3)(lambda: flow(up, h, c, False).wait_send())
                    sib(offset(up, h), c, False).wait_send()

        head_group(c).wait_send()
        for cp in v4_group(c):
            cp.wait_send()
    for b in range(2):
        for cp in w1_near(b, False) + w1_far(b, False) + w2_near(b, False) + w2_far(b, False):
            cp.wait_send()
    for k in range(2):
        w0(k).wait_send()
    for cp in wo_z(False) + wo_plane(1, False) + wo_plane(2, False) + wo_plane(3, False):
        cp.wait_send()
    for j in range(4):
        wo_sibling(j, False).wait_send()


def local(
    video_patches,
    frame_count,
    seen_frames,
    base_latents,
    vision_query,
    vision_kv,
    vision_out,
    hidden_states,
    text_query,
    text_kv,
):
    width = video_patches.shape[-1]
    vm = pl.BlockSpec(memory_space=pltpu.VMEM)
    hbm = pl.BlockSpec(memory_space=pl.ANY)
    dma = lambda n: pltpu.SemaphoreType.DMA((n,))
    latents_out, attended = pl.pallas_call(
        fused_kernel,
        name="fused",
        out_shape=(
            jax.ShapeDtypeStruct((32, 8, 1280), BF16),
            jax.ShapeDtypeStruct((256, 512), BF16),
        ),
        in_specs=[hbm, vm, vm, vm, vm, vm, hbm, hbm, hbm, hbm],
        out_specs=(vm, vm),
        scratch_shapes=[
            pltpu.VMEM((2048, 1280), BF16),
            pltpu.VMEM((512, 1280), BF16),
            pltpu.VMEM((8, 192, 1280), BF16),
            pltpu.VMEM((8, 4, 96, 128), BF16),
            pltpu.VMEM((8, 4, 96, 128), BF16),
            pltpu.VMEM((64, 1280), F32),
            pltpu.VMEM((32, 16, 640), BF16),
            pltpu.VMEM((2, 8, 16, 16, 640), BF16),
            pltpu.VMEM((16, 16, 640), BF16),
            pltpu.VMEM((16, 16, 640), BF16),
            pltpu.VMEM((4, 2, 4, 256, 512), BF16),
            pltpu.VMEM((4, 2, 4, 2, 40, 512), BF16),
            pltpu.VMEM((1280, 1024), BF16),
            pltpu.VMEM((256, 8192), BF16),
            pltpu.VMEM((256, 512), F32),
            pltpu.VMEM((256, 512), BF16),
            pltpu.VMEM((8, 256, 1024), BF16),
            pltpu.VMEM((2, 256, 256), F32),
            pltpu.VMEM((4, 256, 128), F32),
            pltpu.VMEM((4, 256, 256), F32),
            dma(15), dma(2), dma(2), dma(32), dma(32), dma(32), dma(32), dma(24), dma(24), dma(4), dma(4),
            dma(4), dma(4), dma(8), dma(8), dma(20), dma(20), dma(20), dma(20), dma(8), dma(8), dma(32), dma(32),
        ],
        compiler_params=pltpu.CompilerParams(
            collective_id=0, has_side_effects=True, vmem_limit_bytes=60 * 2**20
        ),
        cost_estimate=pl.CostEstimate(flops=14 * 10**9, bytes_accessed=40 * 10**6, transcendentals=3 * 10**6),
    )(
        video_patches.reshape(-1, width),
        frame_count.reshape(1, 1),
        seen_frames,
        base_latents,
        vision_query.T,
        vision_kv.transpose(0, 2, 1),
        vision_out,
        hidden_states,
        text_query,
        text_kv,
    )
    return latents_out[:, None], attended


def solution(mesh):
    placed = (
        P(None, "dp", None, None),
        P("dp"),
        P("dp", None),
        P(),
        P(None, "tensor"),
        P(None, None, "tensor"),
        P("tensor", None),
        P("dp", None),
        P("dp", "tensor"),
        P(None, "dp", "tensor"),
    )
    return jax.shard_map(
        local,
        mesh=mesh,
        in_specs=placed,
        out_specs=(P(None, "dp", "tensor", None), P("dp", "tensor")),
        check_vma=False,
    )
```

```python
import jax
import jax.numpy as jnp
from jax import lax
from jax.experimental import pallas as pl
from jax.experimental.pallas import tpu as pltpu
from jax.sharding import PartitionSpec as P

HEAD_DIM = 128
VHEAD_DIM = 96
EPSILON = 1e-05
MASKED = -1e30
MESH = pl.DeviceIdType.MESH
F32 = jnp.float32
BF16 = jnp.bfloat16


def layer_norm(values):
    average = jnp.mean(values, axis=-1, keepdims=True)
    centered = values - average
    variance = jnp.mean(centered * centered, axis=-1, keepdims=True)
    return centered * lax.rsqrt(variance + EPSILON)


def dot(a, b, ca=1, cb=0):
    return lax.dot_general(a, b, (((ca,), (cb,)), ((), ())), preferred_element_type=F32)


def fused_kernel(
    patches_in, frame_count, seen, base_in, wq_in, wkv_vis_in, wo_in, hidden_in, q_in, kv_in,
    lat_out, att_out,
    base, wq, wkv_vis, lat_own, patches, ctx, wo, hs, hbuf, base32, latp, lall, xown, transit, g1, g2, wkv, tokn, qacc, qh, kv_text, bias, top, acc,
    lsem, w0s, w0r, nes, ner, fas, far, wos, wor, sibs, sibr, has, har, v4s, v4r, ups, upr, dns, dnr, trs, trr, lss, lsr,
):
    dp = lax.axis_index("dp")
    t = lax.axis_index("tensor")
    x = dp // 8
    zh = (dp // 4) % 2
    y = dp % 4
    zl = t // 2
    core = t % 2
    z = zh * 4 + zl

    def at(xx, zz, yy):
        return {"dp": (xx * 2 + zz) * 4 + yy, "tensor": t}

    def ring(offset):
        zz = (z + offset + 8) % 8
        return {"dp": (x * 2 + zz // 4) * 4 + y, "tensor": (zz % 4) * 2 + core}

    def tens(tt):
        return {"dp": dp, "tensor": tt}

    sibling = tens(t + 1 - 2 * core)

    def rc(src, dst, ss, rs, device):
        return pltpu.make_async_remote_copy(
            src_ref=src, dst_ref=dst, send_sem=ss, recv_sem=rs, device_id=device, device_id_type=MESH
        )

    barrier = pltpu.get_barrier_semaphore()

    for j in range(1, 16):
        greeted = {"dp": ((x + j // 4) % 4 * 2 + zh) * 4 + (y + j % 4) % 4, "tensor": t}
        pl.semaphore_signal(barrier, inc=1, device_id=greeted, device_id_type=MESH)
    pl.semaphore_signal(barrier, inc=1, device_id=at(x, 1 - zh, y), device_id_type=MESH)
    for j in range(1, 8):
        pl.semaphore_signal(barrier, inc=1, device_id=tens((t + j) % 8), device_id_type=MESH)
    for o in (1, -1, 2, -2):
        pl.semaphore_signal(barrier, inc=1, device_id=ring(o), device_id_type=MESH)

    def chunk(c):
        return (x + c) % 4

    def patch_load(c):
        rows = pl.ds(pl.multiple_of(chunk(c) * 512, 512), 512)
        return pltpu.make_async_copy(patches_in.at[rows], patches.at[rows], lsem.at[8 + c])

    vision_loads = (
        pltpu.make_async_copy(base_in, base, lsem.at[15]),
        pltpu.make_async_copy(wq_in, wq, lsem.at[16]),
        pltpu.make_async_copy(wkv_vis_in, wkv_vis, lsem.at[17]),
    )
    for cp in vision_loads:
        cp.start()
    for c in range(4):
        patch_load(c).start()
    local_q = pltpu.make_async_copy(q_in, g1.at[x, zh, y], lsem.at[0])
    local_kv = pltpu.make_async_copy(kv_in, g2.at[x, zh, y], lsem.at[1])
    local_wo = pltpu.make_async_copy(wo_in, wo.at[t], lsem.at[2])
    local_hidden = pltpu.make_async_copy(hidden_in, tokn, lsem.at[12])
    for cp in (local_q, local_kv, local_wo, local_hidden):
        cp.start()

    def w0(k):
        src, dst = ((q_in, g1), (kv_in, g2))[k]
        return rc(src, dst.at[x, zh, y], w0s.at[k], w0r.at[k], at(x, 1 - zh, y))

    def w0_in(k):
        src, dst = ((q_in, g1), (kv_in, g2))[k]
        return rc(src, dst.at[x, 1 - zh, y], w0s.at[k], w0r.at[k], at(x, 1 - zh, y))

    halves = (pl.ds(0, 128), pl.ds(128, 128))
    quarters = ((pl.ds(0, 64), pl.ds(64, 64)), (pl.ds(128, 64), pl.ds(192, 64)))
    lanes = (pl.ds(0, 256), pl.ds(256, 256))

    def along(d, o):
        return at(x, zh, (y + o + 4) % 4) if d == 0 else at((x + o + 4) % 4, zh, y)

    def near(b, s, ks=(1, 0)):
        zz = zh if b == 0 else 1 - zh
        for k in ks:
            n = (b * 5 + s) * 2 + k
            for d in range(2):
                j = max(s - 1, 0)
                bx, by = (x, (y + j) % 4) if d == 0 else ((x + j) % 4, y)
                dst = g1.at[bx, zz, by, halves[d]] if k == 0 else g2.at[bx, zz, by, d]
                src = dst
                if b == 0 and j == 0:
                    src = q_in.at[halves[d]] if k == 0 else kv_in.at[d]
                for o in (1, -1):
                    rc(src, dst, nes.at[n], ner.at[n], along(d if s == 0 else 1 - d, o)).start()

    def forward(b, s, ks=(1, 0)):
        zz = zh if b == 0 else 1 - zh
        for k in ks:
            n = (b * 5 + s) * 2 + k
            near_group(b, s, k).wait_recv()
            for d in range(2):
                for m, o in enumerate((1, -1)):
                    if s == 0:
                        bx, by = (x, (y - o + 4) % 4) if d == 0 else ((x - o + 4) % 4, y)
                    else:
                        j = s - 1
                        bx, by = ((x - o + 4) % 4, (y + j) % 4) if d == 0 else ((x + j) % 4, (y - o + 4) % 4)
                    region = g1.at[bx, zz, by, quarters[d][m]] if k == 0 else g2.at[bx, zz, by, d, :, lanes[m]]
                    rc(region, region, fas.at[n], far.at[n], along(d if s == 0 else 1 - d, o)).start()

    def near_group(b, s, k):
        n = (b * 5 + s) * 2 + k
        region = g1.at[0, 0, pl.ds(0, 2)] if k == 0 else g2.at[0, 0, pl.ds(0, 2)]
        return rc(region, region, nes.at[n], ner.at[n], sibling)

    def far_group(b, s, k):
        n = (b * 5 + s) * 2 + k
        region = g1.at[0, 0, 0] if k == 0 else g2.at[0, 0, 0]
        return rc(region, region, fas.at[n], far.at[n], sibling)

    def far_arrived(b, stages, ks=(1, 0)):
        for s in stages:
            for k in ks:
                far_group(b, s, k).wait_recv()

    def start(copies):
        for cp in copies:
            cp.start()

    def arrived(copies):
        for cp in copies:
            cp.wait_recv()

    columns = (pl.ds(0, 640), pl.ds(640, 640))

    def quarter(d, px, py):
        return pl.ds(pl.multiple_of((px if d == 0 else py) * 48, 16), 48)

    def wo_z(inbound):
        out = []
        for i, (o, d) in enumerate(((1, 0), (1, 1), (-1, 0), (-1, 1), (2, 0), (-2, 1))):
            plane = (zl - o + 4) % 4 if inbound else zl
            rows = quarter(d, x, y)
            out.append(
                rc(
                    wo_in.at[rows, columns[d]], wo.at[plane * 2 + core, rows, columns[d]], wos.at[i], wor.at[i],
                    ring(-o if inbound else o),
                )
            )
        return out

    def wo_plane(j, inbound):
        out = []
        for o in (1, 3, 2):
            for d in range(2):
                sign = -o if inbound else o
                px, py = ((x + sign + 4) % 4, y) if d == 0 else (x, (y + sign + 4) % 4)
                rows = quarter(d, px, py) if inbound else quarter(d, x, y)
                region = wo.at[((zl + j) % 4) * 2 + core, rows, columns[d]]
                n = 6 + (j - 1) * 6 + (o - 1) * 2 + d
                out.append(rc(region, region, wos.at[n], wor.at[n], at(px, zh, py)))
        return out

    def wo_sibling(j, inbound):
        region = wo.at[((zl + j) % 4) * 2 + (1 - core if inbound else core)]
        return rc(region, region, sibs.at[j], sibr.at[j], sibling)

    for cp in vision_loads:
        cp.wait()
    base32[...] = base[...].astype(F32)
    lat_norm = layer_norm(base32[...]).astype(BF16)
    q = dot(lat_norm, wq[...], 1, 1) * VHEAD_DIM ** (-0.5)
    k_lat = dot(lat_norm, wkv_vis[0], 1, 1).astype(BF16)
    v_lat = dot(lat_norm, wkv_vis[1], 1, 1).astype(BF16)
    lane = lax.broadcasted_iota(jnp.int32, (64, 192), 1)
    first_head = lane < VHEAD_DIM
    q_block = jnp.concatenate([jnp.where(first_head, q, 0.0), jnp.where(first_head, 0.0, q)], 0).astype(BF16)
    s_lat = dot(k_lat, q_block, 1, 1)
    m_lat = jnp.max(s_lat, axis=0, keepdims=True)

    def vision_chunk(c):
        ch = chunk(c)
        patch_load(c).wait()

        def norm(r, carry):
            rows = patches[pl.ds(pl.multiple_of(ch * 512 + r * 64, 64), 64), :].astype(F32)
            ctx[pl.ds(pl.multiple_of(r * 64, 64), 64), :] = layer_norm(rows).astype(BF16)
            return carry

        lax.fori_loop(0, 8, norm, 0)
        kc = dot(ctx[...], wkv_vis[0], 1, 1).astype(BF16)
        vc = dot(ctx[...], wkv_vis[1], 1, 1).astype(BF16)
        s = dot(kc, q_block, 1, 1).reshape(8, 64, 128)
        m = jnp.maximum(jnp.max(s, axis=1, keepdims=True), m_lat[None])
        e_ctx = jnp.exp(s - m)
        e_lat = jnp.exp(s_lat[None] - m)
        total = jnp.sum(e_ctx, axis=1, keepdims=True) + jnp.sum(e_lat, axis=1, keepdims=True)
        inverse = 1.0 / total
        p_ctx = (e_ctx * inverse).astype(BF16)
        p_lat = (e_lat * inverse).astype(BF16)
        mixed = []
        for v in range(8):
            p = jnp.concatenate([p_ctx[v], p_lat[v]], 0)
            values = jnp.concatenate([vc[v * 64:(v + 1) * 64], v_lat], 0)
            o = dot(p, values, 0, 0)
            mixed.append(jnp.where(first_head, o[:64], o[64:]))
        for u in range(8):
            rows = jnp.concatenate([o[u * 8:(u + 1) * 8] for o in mixed], 0)
            hs[u, ch, pl.ds(0, 64)] = rows[:, :128].astype(BF16)
            hs[u, ch, pl.ds(64, 32)] = jnp.concatenate([rows[:32, 128:], rows[32:, 128:]], 1).astype(BF16)

    def head_copy(c, j):
        ch = chunk(c)
        other = (t + j) % 8
        return rc(hs.at[other, ch], hbuf.at[t, ch], has.at[c], har.at[c], tens(other))

    def head_group(c):
        return rc(hs.at[pl.ds(0, 7), chunk(c)], hbuf.at[pl.ds(0, 7), chunk(c)], has.at[c], har.at[c], sibling)

    def head_local(c):
        return pltpu.make_async_copy(hs.at[t, chunk(c)], hbuf.at[t, chunk(c)], lsem.at[4 + c])

    def head_start(c):
        for j in range(1, 8):
            head_copy(c, j).start()
        head_local(c).start()

    with jax.named_scope("vision_0"):
        vision_chunk(0)
    with jax.named_scope("entry_barrier"):
        pl.semaphore_wait(barrier, 27)
    w0(1).start()
    start(wo_z(False))
    head_start(0)
    near(0, 0)
    near(0, 1)
    with jax.named_scope("vision_1"):
        vision_chunk(1)
    head_start(1)
    with jax.named_scope("w_a"):
        forward(0, 0)
    local_wo.wait()
    wo_sibling(0, False).start()
    near(0, 2)
    with jax.named_scope("vision_2"):
        vision_chunk(2)
    head_start(2)
    with jax.named_scope("wo_plane"):
        arrived(wo_z(True))
        for j in range(1, 4):
            start(wo_plane(j, False))
    with jax.named_scope("text_kv"):
        w0_in(1).wait_recv()
        near(1, 0, (1,))
    near(0, 4)
    with jax.named_scope("vision_3"):
        vision_chunk(3)
    head_start(3)
    with jax.named_scope("w_b"):
        far_arrived(0, (0,))
        near(0, 3)

    local_hidden.wait()

    def norm_tokens(r, carry):
        rows = pl.ds(pl.multiple_of(r * 16, 16), 16)
        tokn[rows, :] = layer_norm(tokn[rows, :].astype(F32)).astype(BF16)
        return carry

    with jax.named_scope("token_norm"):
        lax.fori_loop(0, 8, norm_tokens, 0)
    forward(1, 0, (1,))
    with jax.named_scope("token_norm"):
        lax.fori_loop(8, 16, norm_tokens, 0)
    w0(0).start()

    with jax.named_scope("wait_wo_plane"):
        for j in range(1, 4):
            arrived(wo_plane(j, True))
            wo_sibling(j, False).start()
    with jax.named_scope("wait_wo_sibling"):
        for j in range(4):
            wo_sibling(j, True).wait_recv()

    def v4(c, i):
        px, py = (x + c) % 4, (y + i) % 4
        device, mine, theirs, here = at(px, zh, py), px * 8 + zh * 4 + py, px * 8 + (1 - zh) * 4 + py, x * 4 + y
        return [
            rc(latp.at[mine], lall.at[zh, t, here], v4s.at[c * 2], v4r.at[c * 2], device),
            rc(latp.at[theirs], xown.at[here], v4s.at[c * 2 + 1], v4r.at[c * 2 + 1], device),
        ]

    def v4_group(c):
        some = pl.ds(0, 3 if c == 0 else 4)
        return [
            rc(latp.at[some], lall.at[zh, t, some], v4s.at[c * 2], v4r.at[c * 2], sibling),
            rc(latp.at[some], xown.at[some], v4s.at[c * 2 + 1], v4r.at[c * 2 + 1], sibling),
        ]

    local_lat = (
        pltpu.make_async_copy(latp.at[dp], lall.at[zh, t, x * 4 + y], lsem.at[13]),
        pltpu.make_async_copy(latp.at[x * 8 + (1 - zh) * 4 + y], xown.at[x * 4 + y], lsem.at[14]),
    )
    my_base = base32[pl.ds(pl.multiple_of(t * 8, 8), 8), :]

    def project(c):
        ch = chunk(c)
        with jax.named_scope("wait_heads"):
            head_group(c).wait_recv()
            head_local(c).wait()
        wide = jnp.concatenate([hbuf[g, ch, pl.ds(0, 64)] for g in range(8)], 1)
        narrow = []
        for g in range(8):
            packed = hbuf[g, ch, pl.ds(64, 32)]
            narrow.append(jnp.concatenate([packed[:, :64], packed[:, 64:]], 0))
        narrow = jnp.concatenate(narrow, 1)
        mix = dot(wide, wo[:, :128].reshape(1024, 1280)) + dot(narrow, wo[:, 128:].reshape(512, 1280))
        mix = mix.reshape(8, 8, 1280) + my_base[None]
        mix = layer_norm(mix)
        lat_own[pl.ds(ch * 8, 8)] = mix.astype(BF16)
        latp[pl.ds(ch * 8, 8)] = jnp.concatenate([mix[:, :, :640], mix[:, :, 640:]], 1).astype(BF16)
        for i in range(4):
            if c == 0 and i == 0:
                start(local_lat)
            else:
                start(v4(c, i))

    with jax.named_scope("project_0"):
        project(0)
    with jax.named_scope("project_1"):
        project(1)
    with jax.named_scope("project_2"):
        project(2)
    with jax.named_scope("project_3"):
        project(3)

    def part(c):
        return pl.ds(((x - c + 4) % 4) * 4, 4)

    def block(plane, own_core=True):
        return lall.at[plane // 4, (plane % 4) * 2 + (core if own_core else 1 - core)]

    def level(up):
        return zl if up else 3 - zl

    def flow(up, h, c, inbound, source=None):
        o = 1 if up else -1
        plane = (z - o * h + 8) % 8
        region = block(plane).at[part(c)]
        ss, rs = (ups, upr) if up else (dns, dnr)
        src = region if source is None else source.at[part(c)]
        sent, landed = (0, (h - 1) * 4 + c) if inbound else (h, h * 4 + c)
        return rc(src, region, ss.at[sent], rs.at[landed], ring(-o if inbound else o))

    def flow_sent(up, h):
        ss, rs = (ups, upr) if up else (dns, dnr)
        rc(xown, transit, ss.at[h], rs.at[0], sibling).wait_send()

    def pass_on(up, c):
        o = 1 if up else -1
        return rc(xown.at[part(c)], transit.at[part(c)], trs.at[0], trr.at[(0 if up else 4) + c], ring(o))

    def sib(plane, c, inbound):
        region = block(plane, not inbound).at[part(c)]
        return rc(region, region, lss.at[plane], lsr.at[plane], sibling)

    def sib_group(plane, inbound):
        return rc(block(plane, not inbound), block(plane, not inbound), lss.at[plane], lsr.at[plane], sibling)

    def offset(up, h):
        return (z - h + 8) % 8 if up else (z + h) % 8

    def wave_own(c):
        if c == 0:
            for cp in local_lat:
                cp.wait()
        arrived(v4_group(c))
        for up in (True, False):
            at_level = level(up)
            pl.when(at_level < 3)(lambda: flow(up, 0, c, False).start())
            pl.when(at_level == 2)(lambda: pass_on(up, c).start())
            pl.when(at_level == 3)(lambda: flow(up, 0, c, False, xown).start())
        sib(z, c, False).start()

    def wave(h, c):
        for up in (True, False):
            at_level = level(up)
            if h == 1:
                @pl.when(at_level == 3)
                def _():
                    pass_on(up, c).wait_recv()
                    flow(up, 1, c, False, transit).start()

            @pl.when(at_level + 2 >= h)
            def _():
                flow(up, h, c, True).wait_recv()
                if h < 5:
                    pl.when(at_level < 3)(lambda: flow(up, h, c, False).start())
                sib(offset(up, h), c, False).start()

    def query_half(zz, first):
        def step(i, carry):
            columns = pl.ds(pl.multiple_of((i * 2 + zz) * 1024, 1024), 1024)
            part = dot(tokn[:, columns], g1[i, zz].reshape(1024, 512))
            qacc[...] = qacc[...] + part
            return carry

        if first:
            qacc[...] = jnp.zeros_like(qacc)
        lax.fori_loop(0, 4, step, 0)

    def pack_weights(zz):
        for xx in range(4):
            rows = pl.ds(pl.multiple_of((xx * 2 + zz) * 160, 160), 160)
            for k in range(2):
                block = g2[xx, zz, :, k].astype(F32).reshape(160, 512)
                wkv[rows, k * 512:(k + 1) * 512] = block.astype(BF16)

    def project_text(plane):
        lat = lall[plane // 4, pl.ds((plane % 4) * 2, 2)].astype(F32).reshape(32, 16, 640)
        rows = jnp.concatenate([lat[:, :8], lat[:, 8:]], 2).reshape(256, 1280).astype(BF16)
        kv_text[plane] = dot(rows, wkv[...]).astype(BF16)

    def attend(planes, first=False, last=False):
        with jax.named_scope("attend"):
            ones = jnp.ones((256, 128), BF16)
            for h in range(4):
                own = slice(h * 128, (h + 1) * 128)
                scores = [dot(qh[:, own], kv_text[plane, :, own], 1, 1) + bias[plane // 4] for plane in planes]
                m = jnp.max(jnp.maximum(*scores), axis=1, keepdims=True)
                if not first:
                    m = jnp.maximum(top[h], m)
                total = jnp.zeros((256, 256), F32)
                for plane, s in zip(planes, scores):
                    p = jnp.exp(s - m[:, :1]).astype(BF16)
                    values = jnp.concatenate([kv_text[plane, :, 512 + h * 128:512 + (h + 1) * 128], ones], 1)
                    total = total + dot(p, values)
                if not first:
                    shrink = jnp.exp(top[h] - m)
                    total = total + acc[h] * jnp.concatenate([shrink, shrink], 1)
                if last:
                    result = total[:, :128] / total[:, 128:]
                    seen_any = bias[0, :, :1] == 0.0
                    att_out[:, own] = jnp.where(seen_any, result, 0.0).astype(BF16)
                else:
                    acc[h] = total
                    top[h] = jnp.broadcast_to(m, (256, 128))

    def kv_ready(plane):
        sib_group(plane, True).wait_recv()
        with jax.named_scope("project_text"):
            project_text(plane)

    def waves(h, chunks):
        with jax.named_scope("wave_" + str(h)):
            for c in chunks:
                wave(h, c)

    out_lat = pltpu.make_async_copy(lat_own, lat_out, lsem.at[18])
    out_lat.start()
    with jax.named_scope("w_c"):
        far_arrived(1, (0,), (1,))
        for st in (1, 2, 4, 3):
            near(1, st, (1,))
    with jax.named_scope("w_d"):
        for st in (1, 2, 4, 3):
            forward(0, st)
    with jax.named_scope("wave_own"):
        for c in range(4):
            wave_own(c)
    with jax.named_scope("w_e"):
        w0_in(0).wait_recv()
        near(1, 0, (0,))
        near(1, 1, (0,))
    limit = jnp.minimum(seen[...], frame_count[...])
    row = lax.broadcasted_iota(jnp.int32, (256, 256), 0) % 128 // 8
    for zz in range(2):
        key_frame = row // 4 * 8 + zz * 4 + row % 4
        bias[zz] = jnp.where(key_frame < limit, 0.0, MASKED).T
    waves(1, (0, 1, 2, 3))
    with jax.named_scope("w_f"):
        for st in (1, 2, 4, 3):
            forward(1, st, (1,))
    with jax.named_scope("w_g"):
        forward(1, 0, (0,))
        near(1, 2, (0,))
        near(1, 4, (0,))
    waves(2, (0, 1, 2, 3))
    with jax.named_scope("query_0"):
        local_q.wait()
        local_kv.wait()
        far_arrived(0, (1, 2, 3, 4))
        query_half(zh, True)
    with jax.named_scope("w_h"):
        far_arrived(1, (0,), (0,))
        near(1, 3, (0,))
        forward(1, 1, (0,))
    with jax.named_scope("pack"):
        far_arrived(1, (1, 2, 3, 4), (1,))
        pack_weights(zh)
        pack_weights(1 - zh)
    kv_ready(z)
    waves(3, (0, 1, 2, 3))
    with jax.named_scope("w_i"):
        forward(1, 2, (0,))
        forward(1, 4, (0,))
    kv_ready((z + 1) % 8)
    kv_ready((z + 7) % 8)
    waves(4, (0, 1))
    with jax.named_scope("w_j"):
        forward(1, 3, (0,))
    waves(4, (2, 3))
    kv_ready((z + 2) % 8)
    kv_ready((z + 6) % 8)

    with jax.named_scope("drain_early"):
        out_lat.wait()
        for c in range(4):
            head_group(c).wait_send()
            for cp in v4_group(c):
                cp.wait_send()
        for b in range(2):
            for st in range(5):
                for k in range(2):
                    near_group(b, st, k).wait_send()
        for st in range(5):
            far_group(0, st, 0).wait_send()
            far_group(0, st, 1).wait_send()
        for k in range(2):
            w0(k).wait_send()
        for cp in wo_z(False) + wo_plane(1, False) + wo_plane(2, False) + wo_plane(3, False):
            cp.wait_send()
        for j in range(4):
            wo_sibling(j, False).wait_send()
    with jax.named_scope("query_1"):
        far_arrived(1, (1, 2, 3, 4), (0,))
        query_half(1 - zh, False)
        qh[...] = (qacc[...] * HEAD_DIM ** (-0.5)).astype(BF16)
    waves(5, (0, 1))
    attend((z, (z + 1) % 8), first=True)
    waves(5, (2, 3))
    attend(((z + 7) % 8, (z + 2) % 8))
    final = 5 - (zl + 1) // 2
    early = 3 + zl // 3
    between = 12 - final - early
    kv_ready((z + early) % 8)
    attend(((z + 6) % 8, (z + early) % 8))
    kv_ready((z + between) % 8)
    kv_ready((z + final) % 8)
    attend(((z + between) % 8, (z + final) % 8), last=True)

    with jax.named_scope("drain"):
        sib_group(z, False).wait_send()
        for up in (True, False):
            at_level = level(up)
            flow_sent(up, 0)

            @pl.when(at_level == 2)
            def _():
                rc(xown, transit, trs.at[0], trr.at[0], sibling).wait_send()

            pl.when(at_level == 3)(lambda: flow_sent(up, 1))
            for h in range(1, 6):
                @pl.when(at_level + 2 >= h)
                def _():
                    if h < 5:
                        pl.when(at_level < 3)(lambda: flow_sent(up, h))
                    sib_group(offset(up, h), False).wait_send()

        for st in range(5):
            for k in range(2):
                far_group(1, st, k).wait_send()


def place_kernel(lat, att, lat_out, att_out):
    lat_out[...] = lat[...]
    att_out[...] = att[...]


def local(
    video_patches,
    frame_count,
    seen_frames,
    base_latents,
    vision_query,
    vision_kv,
    vision_out,
    hidden_states,
    text_query,
    text_kv,
):
    width = video_patches.shape[-1]
    vm = pl.BlockSpec(memory_space=pltpu.VMEM)
    hbm = pl.BlockSpec(memory_space=pl.ANY)
    dma = lambda n: pltpu.SemaphoreType.DMA((n,))
    latents_out, attended = pl.pallas_call(
        fused_kernel,
        name="fused",
        out_shape=(
            jax.ShapeDtypeStruct((32, 8, 1280), BF16),
            jax.ShapeDtypeStruct((256, 512), BF16),
        ),
        in_specs=[hbm, vm, vm, hbm, hbm, hbm, hbm, hbm, hbm, hbm],
        out_specs=(hbm, vm),
        scratch_shapes=[
            pltpu.VMEM((64, 1280), BF16),
            pltpu.VMEM((192, 1280), BF16),
            pltpu.VMEM((2, 192, 1280), BF16),
            pltpu.VMEM((32, 8, 1280), BF16),
            pltpu.VMEM((2048, 1280), BF16),
            pltpu.VMEM((512, 1280), BF16),
            pltpu.VMEM((8, 192, 1280), BF16),
            pltpu.VMEM((8, 4, 96, 128), BF16),
            pltpu.VMEM((8, 4, 96, 128), BF16),
            pltpu.VMEM((64, 1280), F32),
            pltpu.VMEM((32, 16, 640), BF16),
            pltpu.VMEM((2, 8, 16, 16, 640), BF16),
            pltpu.VMEM((16, 16, 640), BF16),
            pltpu.VMEM((16, 16, 640), BF16),
            pltpu.VMEM((4, 2, 4, 256, 512), BF16),
            pltpu.VMEM((4, 2, 4, 2, 40, 512), BF16),
            pltpu.VMEM((1280, 1024), BF16),
            pltpu.VMEM((256, 8192), BF16),
            pltpu.VMEM((256, 512), F32),
            pltpu.VMEM((256, 512), BF16),
            pltpu.VMEM((8, 256, 1024), BF16),
            pltpu.VMEM((2, 256, 256), F32),
            pltpu.VMEM((4, 256, 128), F32),
            pltpu.VMEM((4, 256, 256), F32),
            dma(19), dma(2), dma(2), dma(20), dma(20), dma(20), dma(20), dma(24), dma(24), dma(4), dma(4),
            dma(4), dma(4), dma(8), dma(8), dma(5), dma(20), dma(5), dma(20), dma(1), dma(8), dma(8), dma(8),
        ],
        compiler_params=pltpu.CompilerParams(
            collective_id=0, has_side_effects=True, vmem_limit_bytes=60 * 2**20
        ),
        cost_estimate=pl.CostEstimate(flops=14 * 10**9, bytes_accessed=40 * 10**6, transcendentals=3 * 10**6),
    )(
        video_patches.reshape(-1, width),
        frame_count.reshape(1, 1),
        seen_frames,
        base_latents,
        vision_query.T,
        vision_kv.transpose(0, 2, 1),
        vision_out,
        hidden_states,
        text_query,
        text_kv,
    )
    latents_out, attended = pl.pallas_call(
        place_kernel,
        name="place",
        out_shape=(
            jax.ShapeDtypeStruct(latents_out.shape, BF16),
            jax.ShapeDtypeStruct(attended.shape, BF16),
        ),
        in_specs=[vm, vm],
        out_specs=(vm, vm),
    )(latents_out, attended)
    return latents_out[:, None], attended


def solution(mesh):
    placed = (
        P(None, "dp", None, None),
        P("dp"),
        P("dp", None),
        P(),
        P(None, "tensor"),
        P(None, None, "tensor"),
        P("tensor", None),
        P("dp", None),
        P("dp", "tensor"),
        P(None, "dp", "tensor"),
    )
    return jax.shard_map(
        local,
        mesh=mesh,
        in_specs=placed,
        out_specs=(P(None, "dp", "tensor", None), P("dp", "tensor")),
        check_vma=False,
    )
```

```python
import jax
import jax.numpy as jnp
from jax import lax
from jax.experimental import pallas as pl
from jax.experimental.pallas import tpu as pltpu
from jax.sharding import PartitionSpec as P

HEAD_DIM = 128
VHEAD_DIM = 96
EPSILON = 1e-05
MASKED = -1e30
LOG2E = 1.4426950408889634
MESH = pl.DeviceIdType.MESH
ORDER = (2, 1, 3, 0)
F32 = jnp.float32
BF16 = jnp.bfloat16


def layer_norm(values):
    average = jnp.mean(values, axis=-1, keepdims=True)
    centered = values - average
    variance = jnp.mean(centered * centered, axis=-1, keepdims=True)
    return centered * lax.rsqrt(variance + EPSILON)


def dot(a, b, ca=1, cb=0):
    return lax.dot_general(a, b, (((ca,), (cb,)), ((), ())), preferred_element_type=F32)


def fused_kernel(
    patches_in, frame_count, seen, base_in, wq_in, wkv_vis_in, wo_in, hidden_in, q_in, kv_in,
    lat_out, att_out,
    base, wq, wkv_vis, patches, ctx, wo, hs, hbuf, base32, latp, lall, xown, transit, g1, g2, wkv, tokn, qacc, qh, kv_text, bias, top, acc,
    lsem, w0s, w0r, nes, ner, fas, far, wos, wor, sibs, sibr, has, har, v4s, v4r, fls, upr, dnr, trr, lss, lsr,
):
    dp = lax.axis_index("dp")
    t = lax.axis_index("tensor")
    x = dp // 8
    zh = (dp // 4) % 2
    y = dp % 4
    zl = t // 2
    core = t % 2
    z = zh * 4 + zl

    def at(xx, zz, yy):
        return {"dp": (xx * 2 + zz) * 4 + yy, "tensor": t}

    def ring(offset):
        zz = (z + offset + 8) % 8
        return {"dp": (x * 2 + zz // 4) * 4 + y, "tensor": (zz % 4) * 2 + core}

    def tens(tt):
        return {"dp": dp, "tensor": tt}

    sibling = tens(t + 1 - 2 * core)

    def rc(src, dst, ss, rs, device):
        return pltpu.make_async_remote_copy(
            src_ref=src, dst_ref=dst, send_sem=ss, recv_sem=rs, device_id=device, device_id_type=MESH
        )

    barrier = pltpu.get_barrier_semaphore()

    for j in range(1, 16):
        greeted = {"dp": ((x + j // 4) % 4 * 2 + zh) * 4 + (y + j % 4) % 4, "tensor": t}
        pl.semaphore_signal(barrier, inc=1, device_id=greeted, device_id_type=MESH)
    pl.semaphore_signal(barrier, inc=1, device_id=at(x, 1 - zh, y), device_id_type=MESH)
    for j in range(1, 8):
        pl.semaphore_signal(barrier, inc=1, device_id=tens((t + j) % 8), device_id_type=MESH)
    for o in (1, -1, 2, -2):
        pl.semaphore_signal(barrier, inc=1, device_id=ring(o), device_id_type=MESH)

    def chunk(c):
        return (x + c) % 4

    def patch_load(c):
        rows = pl.ds(pl.multiple_of(chunk(c) * 512, 512), 512)
        return pltpu.make_async_copy(patches_in.at[rows], patches.at[rows], lsem.at[8 + c])

    vision_loads = (
        pltpu.make_async_copy(base_in, base, lsem.at[15]),
        pltpu.make_async_copy(wq_in, wq, lsem.at[16]),
        pltpu.make_async_copy(wkv_vis_in, wkv_vis, lsem.at[17]),
    )
    for cp in vision_loads:
        cp.start()
    for c in ORDER:
        patch_load(c).start()
    local_q = pltpu.make_async_copy(q_in, g1.at[x, zh, y], lsem.at[0])
    local_kv = pltpu.make_async_copy(kv_in, g2.at[x, zh, y], lsem.at[1])
    local_wo = pltpu.make_async_copy(wo_in, wo.at[t], lsem.at[2])
    local_hidden = pltpu.make_async_copy(hidden_in, tokn, lsem.at[12])
    for cp in (local_q, local_kv, local_wo, local_hidden):
        cp.start()

    def rows_of(n):
        return patches.at[pl.ds(0, n)]

    def take(sem_send, sem_recv, region):
        return rc(region, region, sem_send, sem_recv, sibling)

    halves = (pl.ds(0, 128), pl.ds(128, 128))
    quarters = ((pl.ds(0, 64), pl.ds(64, 64)), (pl.ds(128, 64), pl.ds(192, 64)))
    lanes = (pl.ds(0, 256), pl.ds(256, 256))

    def w0(k):
        if k == 1:
            src, dst = kv_in, g2.at[x, zh, y]
        else:
            src, dst = q_in.at[:, lanes[k - 2]], g1.at[x, zh, y, :, lanes[k - 2]]
        return rc(src, dst, w0s.at[k - 1], w0r.at[k - 1], at(x, 1 - zh, y))

    def along(d, o):
        return at(x, zh, (y + o + 4) % 4) if d == 0 else at((x + o + 4) % 4, zh, y)

    def kind(b, k):
        return {(0, 0): 0, (0, 1): 1, (1, 1): 2, (1, 2): 3, (1, 3): 4}[b, k]

    def piece(bx, zz, by, d, k, m=None):
        if k == 1:
            return g2.at[bx, zz, by, d] if m is None else g2.at[bx, zz, by, d, :, lanes[m]]
        rows = halves[d] if m is None else quarters[d][m]
        return g1.at[bx, zz, by, rows] if k == 0 else g1.at[bx, zz, by, rows, lanes[k - 2]]

    def near(b, s, ks):
        zz = zh if b == 0 else 1 - zh
        for k in ks:
            for d in range(2):
                j = max(s - 1, 0)
                bx, by = (x, (y + j) % 4) if d == 0 else ((x + j) % 4, y)
                dst = piece(bx, zz, by, d, k)
                src = dst
                if b == 0 and j == 0:
                    src = q_in.at[halves[d]] if k == 0 else kv_in.at[d]
                for o in (1, -1):
                    device = along(d if s == 0 else 1 - d, o)
                    rc(src, dst, nes.at[int(k == 1)], ner.at[s * 5 + kind(b, k)], device).start()

    def forward(b, s, ks):
        zz = zh if b == 0 else 1 - zh
        for k in ks:
            bytes_in = (g1.at[0, 0, pl.ds(0, 2)], g2.at[0, 0, pl.ds(0, 2)], g1.at[0, 0, 0], g1.at[0, 0, 0])[k]
            take(nes.at[0], ner.at[s * 5 + kind(b, k)], bytes_in).wait_recv()
            n = kind(b, k) + (0 if s == 0 else 5)
            for d in range(2):
                for m, o in enumerate((1, -1)):
                    if s == 0:
                        bx, by = (x, (y - o + 4) % 4) if d == 0 else ((x - o + 4) % 4, y)
                    else:
                        j = s - 1
                        bx, by = ((x - o + 4) % 4, (y + j) % 4) if d == 0 else ((x + j) % 4, (y - o + 4) % 4)
                    region = piece(bx, zz, by, d, k, m)
                    rc(region, region, fas.at[int(k == 1)], far.at[n], along(d if s == 0 else 1 - d, o)).start()

    def first_ring_done(b, ks):
        for k in ks:
            region = (g1.at[0, 0, 0], g2.at[0, 0, 0], g1.at[0, 0, 0, pl.ds(0, 128)], g1.at[0, 0, 0, pl.ds(0, 128)])[k]
            take(fas.at[0], far.at[kind(b, k)], region).wait_recv()

    def second_ring_done(b, ks):
        for k in ks:
            region = (g1.at[0, 0], g2.at[0, 0], g1.at[0, 0, pl.ds(0, 2)], g1.at[0, 0, pl.ds(0, 2)])[k]
            take(fas.at[0], far.at[5 + kind(b, k)], region).wait_recv()

    def start(copies):
        for cp in copies:
            cp.start()

    def arrived(copies):
        for cp in copies:
            cp.wait_recv()

    columns = (pl.ds(0, 640), pl.ds(640, 640))

    def quarter(d, px, py):
        return pl.ds(pl.multiple_of((px if d == 0 else py) * 48, 16), 48)

    def wo_z():
        rows = quarter(0, x, y), quarter(1, x, y)
        out = []
        for o, d in ((1, 0), (1, 1), (-1, 0), (-1, 1), (2, 0), (-2, 1)):
            dst = wo.at[t, rows[d], columns[d]]
            out.append(rc(wo_in.at[rows[d], columns[d]], dst, wos.at[0], wor.at[0], ring(o)))
        return out

    def wo_plane(j, inbound):
        out = []
        for o in (1, 3, 2):
            for d in range(2):
                sign = -o if inbound else o
                px, py = ((x + sign + 4) % 4, y) if d == 0 else (x, (y + sign + 4) % 4)
                rows = quarter(d, px, py) if inbound else quarter(d, x, y)
                region = wo.at[((zl + j) % 4) * 2 + core, rows, columns[d]]
                out.append(rc(region, region, wos.at[0], wor.at[j], at(px, zh, py)))
        return out

    def wo_sibling(j, inbound):
        region = wo.at[((zl + j) % 4) * 2 + (1 - core if inbound else core)]
        return rc(region, region, sibs.at[0], sibr.at[0], sibling)

    for cp in vision_loads:
        cp.wait()
    base32[...] = base[...].astype(F32)
    lat_norm = layer_norm(base32[...]).astype(BF16)
    q = dot(lat_norm, wq[...], 1, 1) * VHEAD_DIM ** (-0.5)
    k_lat = dot(lat_norm, wkv_vis[0], 1, 1).astype(BF16)
    v_lat = dot(lat_norm, wkv_vis[1], 1, 1).astype(BF16)
    lane = lax.broadcasted_iota(jnp.int32, (64, 192), 1)
    first_head = lane < VHEAD_DIM
    q_block = jnp.concatenate([jnp.where(first_head, q, 0.0), jnp.where(first_head, 0.0, q)], 0).astype(BF16)
    s_lat = dot(k_lat, q_block, 1, 1)
    m_lat = jnp.max(s_lat, axis=0, keepdims=True)

    def vision_chunk(c):
        ch = chunk(c)
        patch_load(c).wait()

        def norm(r, carry):
            rows = patches[pl.ds(pl.multiple_of(ch * 512 + r * 64, 64), 64), :].astype(F32)
            ctx[pl.ds(pl.multiple_of(r * 64, 64), 64), :] = layer_norm(rows).astype(BF16)
            return carry

        lax.fori_loop(0, 8, norm, 0)
        kc = dot(ctx[...], wkv_vis[0], 1, 1).astype(BF16)
        vc = dot(ctx[...], wkv_vis[1], 1, 1).astype(BF16)
        s = dot(kc, q_block, 1, 1).reshape(8, 64, 128)
        m = jnp.maximum(jnp.max(s, axis=1, keepdims=True), m_lat[None])
        e_ctx = jnp.exp(s - m)
        e_lat = jnp.exp(s_lat[None] - m)
        total = jnp.sum(e_ctx, axis=1, keepdims=True) + jnp.sum(e_lat, axis=1, keepdims=True)
        inverse = 1.0 / total
        p_ctx = (e_ctx * inverse).astype(BF16)
        p_lat = (e_lat * inverse).astype(BF16)
        mixed = []
        for v in range(8):
            p = jnp.concatenate([p_ctx[v], p_lat[v]], 0)
            values = jnp.concatenate([vc[v * 64:(v + 1) * 64], v_lat], 0)
            o = dot(p, values, 0, 0)
            mixed.append(jnp.where(first_head, o[:64], o[64:]))
        for u in range(8):
            rows = jnp.concatenate([o[u * 8:(u + 1) * 8] for o in mixed], 0)
            hs[u, ch, pl.ds(0, 64)] = rows[:, :128].astype(BF16)
            hs[u, ch, pl.ds(64, 32)] = jnp.concatenate([rows[:32, 128:], rows[32:, 128:]], 1).astype(BF16)

    def head_copy(c, j):
        ch = chunk(c)
        other = (t + j) % 8
        return rc(hs.at[other, ch], hbuf.at[t, ch], has.at[0], har.at[c], tens(other))

    def head_local(c):
        return pltpu.make_async_copy(hs.at[t, chunk(c)], hbuf.at[t, chunk(c)], lsem.at[4 + c])

    def head_start(c):
        for j in range(1, 8):
            head_copy(c, j).start()
        head_local(c).start()

    with jax.named_scope("vision_0"):
        vision_chunk(ORDER[0])
    with jax.named_scope("entry_barrier"):
        pl.semaphore_wait(barrier, 27)
    start(wo_z())
    head_start(ORDER[0])
    w0(1).start()
    near(0, 0, (1, 0))
    near(0, 1, (1, 0))
    with jax.named_scope("vision_1"):
        vision_chunk(ORDER[1])
    head_start(ORDER[1])
    with jax.named_scope("vision_2"):
        vision_chunk(ORDER[2])
    head_start(ORDER[2])
    with jax.named_scope("w_a"):
        forward(0, 0, (1, 0))
    with jax.named_scope("wo_plane"):
        take(wos.at[0], wor.at[0], rows_of(144)).wait_recv()
        for j in range(1, 4):
            start(wo_plane(j, False))
    local_wo.wait()
    wo_sibling(0, False).start()
    near(0, 2, (1, 0))
    with jax.named_scope("vision_3"):
        vision_chunk(ORDER[3])
    head_start(ORDER[3])
    near(0, 4, (1, 0))
    with jax.named_scope("w_b"):
        first_ring_done(0, (1, 0))
        near(0, 3, (1, 0))

    local_hidden.wait()

    def norm_tokens(r, carry):
        rows = pl.ds(pl.multiple_of(r * 16, 16), 16)
        tokn[rows, :] = layer_norm(tokn[rows, :].astype(F32)).astype(BF16)
        return carry

    with jax.named_scope("token_norm"):
        lax.fori_loop(0, 8, norm_tokens, 0)
    with jax.named_scope("text_kv"):
        w0(1).wait_recv()
        near(1, 0, (1,))
    with jax.named_scope("wait_wo_plane"):
        for j in range(1, 4):
            take(wos.at[0], wor.at[j], rows_of(144)).wait_recv()
            wo_sibling(j, False).start()
    with jax.named_scope("token_norm"):
        lax.fori_loop(8, 12, norm_tokens, 0)

    with jax.named_scope("wait_wo_sibling"):
        take(sibs.at[0], sibr.at[0], rows_of(768)).wait_recv()

    def v4(c, i):
        px, py = (x + c) % 4, (y + i) % 4
        device, mine, theirs, here = at(px, zh, py), px * 8 + zh * 4 + py, px * 8 + (1 - zh) * 4 + py, x * 4 + y
        return [
            rc(latp.at[mine], lall.at[zh, t, here], v4s.at[0], v4r.at[c], device),
            rc(latp.at[theirs], xown.at[here], v4s.at[0], v4r.at[c], device),
        ]

    def v4_arrived(c):
        take(v4s.at[0], v4r.at[c], latp.at[pl.ds(0, 6 if c == 0 else 8)]).wait_recv()

    local_lat = (
        pltpu.make_async_copy(latp.at[dp], lall.at[zh, t, x * 4 + y], lsem.at[13]),
        pltpu.make_async_copy(latp.at[x * 8 + (1 - zh) * 4 + y], xown.at[x * 4 + y], lsem.at[14]),
    )
    my_base = base32[pl.ds(pl.multiple_of(t * 8, 8), 8), :]

    def project(chunks):
        wide, narrow = [], []
        for c in chunks:
            ch = chunk(c)
            with jax.named_scope("wait_heads"):
                take(has.at[0], har.at[c], hs.at[pl.ds(0, 7), ch]).wait_recv()
                head_local(c).wait()
            wide.append(jnp.concatenate([hbuf[g, ch, pl.ds(0, 64)] for g in range(8)], 1))
            parts = []
            for g in range(8):
                packed = hbuf[g, ch, pl.ds(64, 32)]
                parts.append(jnp.concatenate([packed[:, :64], packed[:, 64:]], 0))
            narrow.append(jnp.concatenate(parts, 1))
        if chunks == ORDER[2:]:
            for k in (2, 3):
                w0(k).start()
        wide, narrow = jnp.concatenate(wide, 0), jnp.concatenate(narrow, 0)
        mix = dot(wide, wo[:, :128].reshape(1024, 1280)) + dot(narrow, wo[:, 128:].reshape(512, 1280))
        mix = layer_norm(mix.reshape(16, 8, 1280) + my_base[None])
        packed = jnp.concatenate([mix[:, :, :640], mix[:, :, 640:]], 1).astype(BF16)
        for n, c in enumerate(chunks):
            ch = chunk(c)
            lat_out[pl.ds(ch * 8, 8)] = mix[n * 8:(n + 1) * 8].astype(BF16)
            latp[pl.ds(ch * 8, 8)] = packed[n * 8:(n + 1) * 8]
        for c in chunks:
            for i in range(4):
                if c == 0 and i == 0:
                    start(local_lat)
                else:
                    start(v4(c, i))

    with jax.named_scope("project_0"):
        project(ORDER[:2])
    with jax.named_scope("project_1"):
        project(ORDER[2:])

    def part(c):
        return pl.ds(((x - c + 4) % 4) * 4, 4)

    def block(plane, own_core=True):
        return lall.at[plane // 4, (plane % 4) * 2 + (core if own_core else 1 - core)]

    def level(up):
        return zl if up else 3 - zl

    def flow(up, h, c, inbound, source=None):
        o = 1 if up else -1
        plane = (z - o * h + 8) % 8
        region = block(plane).at[part(c)]
        rs = upr if up else dnr
        src = region if source is None else source.at[part(c)]
        n = (h - 1 if inbound else h) * 4 + c
        return rc(src, region, fls.at[0], rs.at[n], ring(-o if inbound else o))

    def pass_on(up, c):
        o = 1 if up else -1
        return rc(xown.at[part(c)], transit.at[part(c)], fls.at[0], trr.at[(0 if up else 4) + c], ring(o))

    def sib(plane, c, inbound):
        region = block(plane, not inbound).at[part(c)]
        return rc(region, region, lss.at[0], lsr.at[plane], sibling)

    def sib_arrived(plane):
        take(lss.at[0], lsr.at[plane], block(plane, False)).wait_recv()

    def offset(up, h):
        return (z - h + 8) % 8 if up else (z + h) % 8

    def wave_own(c):
        if c == 0:
            for cp in local_lat:
                cp.wait()
        v4_arrived(c)
        for up in (True, False):
            at_level = level(up)
            pl.when(at_level < 3)(lambda: flow(up, 0, c, False).start())
            pl.when(at_level == 2)(lambda: pass_on(up, c).start())
            pl.when(at_level == 3)(lambda: flow(up, 0, c, False, xown).start())
        sib(z, c, False).start()

    def wave(h, c):
        for up in (True, False):
            at_level = level(up)
            if h == 1:
                @pl.when(at_level == 3)
                def _():
                    pass_on(up, c).wait_recv()
                    flow(up, 1, c, False, transit).start()

            @pl.when(at_level + 2 >= h)
            def _():
                flow(up, h, c, True).wait_recv()
                if h < 5:
                    pl.when(at_level < 3)(lambda: flow(up, h, c, False).start())
                sib(offset(up, h), c, False).start()

    def query_half(zz, cols, first):
        def step(i, carry):
            contracted = pl.ds(pl.multiple_of((i * 2 + zz) * 1024, 1024), 1024)
            part = dot(tokn[:, contracted], g1[i, zz, :, :, cols].reshape(1024, -1))
            qacc[:, cols] = qacc[:, cols] + part
            return carry

        if first:
            qacc[...] = jnp.zeros_like(qacc)
        lax.fori_loop(0, 4, step, 0)

    def query_done(half):
        cols = slice(half * 256, (half + 1) * 256)
        second_ring_done(1, (2 + half,))
        query_half(1 - zh, cols, False)
        qh[:, cols] = (qacc[:, cols] * (HEAD_DIM ** (-0.5) * LOG2E)).astype(BF16)

    def pack_weights(zz):
        for xx in range(4):
            rows = pl.ds(pl.multiple_of((xx * 2 + zz) * 160, 160), 160)
            for k in range(2):
                block = g2[xx, zz, :, k].astype(F32).reshape(160, 512)
                wkv[rows, k * 512:(k + 1) * 512] = block.astype(BF16)

    def project_text(plane):
        lat = lall[plane // 4, pl.ds((plane % 4) * 2, 2)].astype(F32).reshape(32, 16, 640)
        rows = jnp.concatenate([lat[:, :8], lat[:, 8:]], 2).reshape(256, 1280).astype(BF16)
        kv_text[plane] = dot(rows, wkv[...]).astype(BF16)

    def attend(planes, heads, first=False, last=False):
        with jax.named_scope("attend"):
            ones = jnp.ones((256, 128), BF16)
            own = {h: slice(h * 128, (h + 1) * 128) for h in heads}
            old = {} if first else {h: top[h] for h in heads}
            masks = [bias[plane // 4] for plane in planes]
            scores, new, totals = {}, {}, {}
            for h in heads:
                scores[h] = [
                    dot(qh[:, own[h]], kv_text[plane, :, own[h]], 1, 1) + mask for plane, mask in zip(planes, masks)
                ]
            for h in heads:
                m = scores[h][0]
                for s in scores[h][1:]:
                    m = jnp.maximum(m, s)
                m = jnp.max(m, axis=1, keepdims=True)
                new[h] = m if first else jnp.maximum(old[h], m)
            for h in heads:
                weights = [jnp.exp2(s - new[h][:, :1]).astype(BF16) for s in scores[h]]
                parts = [
                    dot(p, jnp.concatenate([kv_text[plane, :, 512 + h * 128:512 + (h + 1) * 128], ones], 1))
                    for plane, p in zip(planes, weights)
                ]
                totals[h] = sum(parts[1:], parts[0])
            for h in heads:
                total = totals[h]
                if not first:
                    shrink = jnp.exp2(old[h] - new[h])
                    total = total + acc[h] * jnp.concatenate([shrink, shrink], 1)
                if last:
                    result = total[:, :128] / total[:, 128:]
                    seen_any = bias[0, :, :1] == 0.0
                    att_out[:, own[h]] = jnp.where(seen_any, result, 0.0).astype(BF16)
                else:
                    acc[h] = total
                    top[h] = jnp.broadcast_to(new[h], (256, 128))

    def kv_ready(plane):
        sib_arrived(plane)
        with jax.named_scope("project_text"):
            project_text(plane)

    def waves(h, chunks):
        with jax.named_scope("wave_" + str(h)):
            for c in chunks:
                wave(h, c)

    with jax.named_scope("token_norm"):
        lax.fori_loop(12, 16, norm_tokens, 0)
    with jax.named_scope("wave_own"):
        for c in ORDER[:2]:
            wave_own(c)
        forward(0, 1, (1, 0))
        forward(0, 2, (1, 0))
        for c in ORDER[2:]:
            wave_own(c)
    with jax.named_scope("w_e"):
        w0(2).wait_recv()
        near(1, 0, (2,))
        near(1, 1, (2,))
    with jax.named_scope("w_c0"):
        forward(1, 0, (1,))
    with jax.named_scope("w_d"):
        for st in (4, 3):
            forward(0, st, (1, 0))
    with jax.named_scope("w_c"):
        first_ring_done(1, (1,))
        for st in (1, 2, 4, 3):
            near(1, st, (1,))
    with jax.named_scope("w_e"):
        w0(3).wait_recv()
        near(1, 0, (3,))
        near(1, 1, (3,))
    limit = jnp.minimum(seen[...], frame_count[...])
    row = lax.broadcasted_iota(jnp.int32, (256, 256), 0) % 128 // 8
    for zz in range(2):
        key_frame = row // 4 * 8 + zz * 4 + row % 4
        bias[zz] = jnp.where(key_frame < limit, 0.0, MASKED).T
    waves(1, ORDER)
    with jax.named_scope("w_f"):
        for st in (1, 2, 4, 3):
            forward(1, st, (1,))
    with jax.named_scope("w_g2"):
        forward(1, 0, (2,))
        near(1, 2, (2,))
        near(1, 4, (2,))
        forward(1, 1, (2,))
    waves(2, ORDER)
    with jax.named_scope("pack"):
        local_kv.wait()
        second_ring_done(0, (1,))
        second_ring_done(1, (1,))
        pack_weights(zh)
        pack_weights(1 - zh)
    kv_ready(z)
    with jax.named_scope("w_h2"):
        first_ring_done(1, (2,))
        near(1, 3, (2,))
        forward(1, 2, (2,))
        forward(1, 4, (2,))
    with jax.named_scope("w_g3"):
        forward(1, 0, (3,))
        near(1, 2, (3,))
        near(1, 4, (3,))
        forward(1, 1, (3,))
    kv_ready((z + 1) % 8)
    kv_ready((z + 7) % 8)
    waves(3, ORDER[:2])
    with jax.named_scope("query_0"):
        local_q.wait()
        second_ring_done(0, (0,))
        query_half(zh, slice(0, 512), True)
    waves(3, ORDER[2:])
    with jax.named_scope("w_i2"):
        forward(1, 3, (2,))
    kv_ready((z + 2) % 8)
    with jax.named_scope("w_h3"):
        first_ring_done(1, (3,))
        near(1, 3, (3,))
        forward(1, 2, (3,))
        forward(1, 4, (3,))
    kv_ready((z + 6) % 8)
    final = 5 - (zl + 1) // 2
    early = 3 + 2 * (zl // 3)
    between = 12 - final - early
    pairs = [
        (z, (z + 1) % 8),
        ((z + 7) % 8, (z + 2) % 8),
        ((z + 6) % 8, (z + early) % 8, (z + between) % 8),
        ((z + final) % 8,),
    ]
    waves(4, ORDER[:2])
    kv_ready((z + early) % 8)
    with jax.named_scope("query_1"):
        query_done(0)
    with jax.named_scope("w_i3"):
        forward(1, 3, (3,))
    attend(pairs[0], (0, 1), first=True)
    waves(4, ORDER[2:])
    attend(pairs[1], (0, 1))
    kv_ready((z + between) % 8)
    attend(pairs[2], (0, 1))
    waves(5, ORDER[:2])
    with jax.named_scope("drain_early"):
        take(has.at[0], har.at[0], hs.at[pl.ds(0, 7)]).wait_send()
        take(v4s.at[0], v4r.at[0], rows_of(240)).wait_send()
        take(wos.at[0], wor.at[0], rows_of(576)).wait_send()
        take(sibs.at[0], sibr.at[0], rows_of(768)).wait_send()
        take(nes.at[0], ner.at[0], rows_of(2048)).wait_send()
        take(nes.at[1], ner.at[0], rows_of(640)).wait_send()
        for k in (1, 2, 3):
            w0(k).wait_send()
    with jax.named_scope("query_1"):
        query_done(1)
    attend(pairs[0], (2, 3), first=True)
    attend(pairs[1], (2, 3))
    attend(pairs[2], (2, 3))
    waves(5, ORDER[2:])
    kv_ready((z + final) % 8)
    attend(pairs[3], (0, 1, 2, 3), last=True)

    with jax.named_scope("drain"):
        take(lss.at[0], lsr.at[0], rows_of(1024)).wait_send()
        take(fas.at[0], far.at[0], rows_of(1024)).wait_send()
        take(fas.at[1], far.at[0], rows_of(320)).wait_send()
        middle = (zl == 1) | (zl == 2)
        pl.when(middle)(lambda: take(fls.at[0], upr.at[0], rows_of(1280)).wait_send())
        pl.when(jnp.logical_not(middle))(lambda: take(fls.at[0], upr.at[0], rows_of(640)).wait_send())


def local(
    video_patches,
    frame_count,
    seen_frames,
    base_latents,
    vision_query,
    vision_kv,
    vision_out,
    hidden_states,
    text_query,
    text_kv,
):
    width = video_patches.shape[-1]
    vm = pl.BlockSpec(memory_space=pltpu.VMEM)
    hbm = pl.BlockSpec(memory_space=pl.ANY)
    dma = lambda n: pltpu.SemaphoreType.DMA((n,))
    latents_out, attended = pl.pallas_call(
        fused_kernel,
        name="fused",
        out_shape=(
            pltpu.VMEM((32, 8, 1280), BF16),
            pltpu.VMEM((256, 512), BF16),
        ),
        in_specs=[hbm, vm, vm, hbm, hbm, hbm, hbm, hbm, hbm, hbm],
        out_specs=(vm, vm),
        scratch_shapes=[
            pltpu.VMEM((64, 1280), BF16),
            pltpu.VMEM((192, 1280), BF16),
            pltpu.VMEM((2, 192, 1280), BF16),
            pltpu.VMEM((2048, 1280), BF16),
            pltpu.VMEM((512, 1280), BF16),
            pltpu.VMEM((8, 192, 1280), BF16),
            pltpu.VMEM((8, 4, 96, 128), BF16),
            pltpu.VMEM((8, 4, 96, 128), BF16),
            pltpu.VMEM((64, 1280), F32),
            pltpu.VMEM((32, 16, 640), BF16),
            pltpu.VMEM((2, 8, 16, 16, 640), BF16),
            pltpu.VMEM((16, 16, 640), BF16),
            pltpu.VMEM((16, 16, 640), BF16),
            pltpu.VMEM((4, 2, 4, 256, 512), BF16),
            pltpu.VMEM((4, 2, 4, 2, 40, 512), BF16),
            pltpu.VMEM((1280, 1024), BF16),
            pltpu.VMEM((256, 8192), BF16),
            pltpu.VMEM((256, 512), F32),
            pltpu.VMEM((256, 512), BF16),
            pltpu.VMEM((8, 256, 1024), BF16),
            pltpu.VMEM((2, 256, 256), F32),
            pltpu.VMEM((4, 256, 128), F32),
            pltpu.VMEM((4, 256, 256), F32),
            dma(18), dma(3), dma(3), dma(2), dma(25), dma(2), dma(10), dma(1), dma(4), dma(1), dma(1),
            dma(1), dma(4), dma(1), dma(4), dma(1), dma(20), dma(20), dma(8), dma(1), dma(8),
        ],
        compiler_params=pltpu.CompilerParams(
            collective_id=0, has_side_effects=True, vmem_limit_bytes=60 * 2**20
        ),
        cost_estimate=pl.CostEstimate(flops=14 * 10**9, bytes_accessed=40 * 10**6, transcendentals=3 * 10**6),
    )(
        video_patches.reshape(-1, width),
        frame_count.reshape(1, 1),
        seen_frames,
        base_latents,
        vision_query.T,
        vision_kv.transpose(0, 2, 1),
        vision_out,
        hidden_states,
        text_query,
        text_kv,
    )
    return latents_out[:, None], attended


def solution(mesh):
    placed = (
        P(None, "dp", None, None),
        P("dp"),
        P("dp", None),
        P(),
        P(None, "tensor"),
        P(None, None, "tensor"),
        P("tensor", None),
        P("dp", None),
        P("dp", "tensor"),
        P(None, "dp", "tensor"),
    )
    return jax.shard_map(
        local,
        mesh=mesh,
        in_specs=placed,
        out_specs=(P(None, "dp", "tensor", None), P("dp", "tensor")),
        check_vma=False,
    )
```

```python
import jax
import jax.numpy as jnp
from jax import lax
from jax.experimental import pallas as pl
from jax.experimental.pallas import tpu as pltpu
from jax.sharding import PartitionSpec as P

HEAD_DIM = 128
VHEAD_DIM = 96
EPSILON = 1e-05
MASKED = -1e30
LOG2E = 1.4426950408889634
MESH = pl.DeviceIdType.MESH
ORDER = (1, 3, 2, 0)
F32 = jnp.float32
BF16 = jnp.bfloat16


def layer_norm(values):
    average = jnp.mean(values, axis=-1, keepdims=True)
    centered = values - average
    variance = jnp.mean(centered * centered, axis=-1, keepdims=True)
    return centered * lax.rsqrt(variance + EPSILON)


def dot(a, b, ca=1, cb=0):
    return lax.dot_general(a, b, (((ca,), (cb,)), ((), ())), preferred_element_type=F32)


def fused_kernel(
    patches_in, frame_count, seen, base_in, wq_in, wkv_vis_in, wo_in, hidden_in, q_in, kv_in,
    lat_out, att_out,
    base, wq, wkv_vis, patches, ctx, wo, hs, hbuf, base32, latp, lall, xown, transit, g1, g2, wkv, tokn, qacc, qh, kv_text, bias, top, acc,
    lsem, w0s, w0r, nes, ner, fas, far, wos, wor, sibs, sibr, has, har, v4s, v4r, fls, upr, dnr, trr, lss, lsr,
):
    dp = lax.axis_index("dp")
    t = lax.axis_index("tensor")
    x = dp // 8
    zh = (dp // 4) % 2
    y = dp % 4
    zl = t // 2
    core = t % 2
    z = zh * 4 + zl

    def at(xx, zz, yy):
        return {"dp": (xx * 2 + zz) * 4 + yy, "tensor": t}

    def ring(offset):
        zz = (z + offset + 8) % 8
        return {"dp": (x * 2 + zz // 4) * 4 + y, "tensor": (zz % 4) * 2 + core}

    def tens(tt):
        return {"dp": dp, "tensor": tt}

    sibling = tens(t + 1 - 2 * core)

    def rc(src, dst, ss, rs, device):
        return pltpu.make_async_remote_copy(
            src_ref=src, dst_ref=dst, send_sem=ss, recv_sem=rs, device_id=device, device_id_type=MESH
        )

    barrier = pltpu.get_barrier_semaphore()

    for j in range(1, 16):
        greeted = {"dp": ((x + j // 4) % 4 * 2 + zh) * 4 + (y + j % 4) % 4, "tensor": t}
        pl.semaphore_signal(barrier, inc=1, device_id=greeted, device_id_type=MESH)
    pl.semaphore_signal(barrier, inc=1, device_id=at(x, 1 - zh, y), device_id_type=MESH)
    for j in range(1, 8):
        pl.semaphore_signal(barrier, inc=1, device_id=tens((t + j) % 8), device_id_type=MESH)
    for o in (1, -1, 2, -2):
        pl.semaphore_signal(barrier, inc=1, device_id=ring(o), device_id_type=MESH)

    def chunk(c):
        return (x + c) % 4

    def patch_load(c):
        rows = pl.ds(pl.multiple_of(chunk(c) * 512, 512), 512)
        return pltpu.make_async_copy(patches_in.at[rows], patches.at[rows], lsem.at[8 + c])

    vision_loads = (
        pltpu.make_async_copy(base_in, base, lsem.at[15]),
        pltpu.make_async_copy(wq_in, wq, lsem.at[16]),
        pltpu.make_async_copy(wkv_vis_in, wkv_vis, lsem.at[17]),
    )
    for cp in vision_loads:
        cp.start()
    for c in ORDER:
        patch_load(c).start()
    local_q = pltpu.make_async_copy(q_in, g1.at[x, zh, y], lsem.at[0])
    local_kv = pltpu.make_async_copy(kv_in, g2.at[x, zh, y], lsem.at[1])
    local_wo = pltpu.make_async_copy(wo_in, wo.at[t], lsem.at[2])
    local_hidden = pltpu.make_async_copy(hidden_in, tokn, lsem.at[12])
    for cp in (local_q, local_kv, local_wo, local_hidden):
        cp.start()

    def rows_of(n):
        return patches.at[pl.ds(0, n)]

    def take(sem_send, sem_recv, region):
        return rc(region, region, sem_send, sem_recv, sibling)

    halves = (pl.ds(0, 128), pl.ds(128, 128))
    quarters = ((pl.ds(0, 64), pl.ds(64, 64)), (pl.ds(128, 64), pl.ds(192, 64)))
    lanes = (pl.ds(0, 256), pl.ds(256, 256))

    def w0(k):
        if k == 1:
            src, dst = kv_in, g2.at[x, zh, y]
        else:
            src, dst = q_in.at[:, lanes[k - 2]], g1.at[x, zh, y, :, lanes[k - 2]]
        return rc(src, dst, w0s.at[k - 1], w0r.at[k - 1], at(x, 1 - zh, y))

    def along(d, o):
        return at(x, zh, (y + o + 4) % 4) if d == 0 else at((x + o + 4) % 4, zh, y)

    def kind(b, k):
        return {(0, 0): 0, (0, 1): 1, (1, 1): 2, (1, 2): 3, (1, 3): 4}[b, k]

    def piece(bx, zz, by, d, k, m=None):
        if k == 1:
            return g2.at[bx, zz, by, d] if m is None else g2.at[bx, zz, by, d, :, lanes[m]]
        rows = halves[d] if m is None else quarters[d][m]
        return g1.at[bx, zz, by, rows] if k == 0 else g1.at[bx, zz, by, rows, lanes[k - 2]]

    def near(b, s, ks):
        zz = zh if b == 0 else 1 - zh
        for k in ks:
            for d in range(2):
                j = max(s - 1, 0)
                bx, by = (x, (y + j) % 4) if d == 0 else ((x + j) % 4, y)
                dst = piece(bx, zz, by, d, k)
                src = dst
                if b == 0 and j == 0:
                    src = q_in.at[halves[d]] if k == 0 else kv_in.at[d]
                for o in (1, -1):
                    device = along(d if s == 0 else 1 - d, o)
                    rc(src, dst, nes.at[int(k == 1)], ner.at[s * 5 + kind(b, k)], device).start()

    def forward(b, s, ks):
        zz = zh if b == 0 else 1 - zh
        for k in ks:
            bytes_in = (g1.at[0, 0, pl.ds(0, 2)], g2.at[0, 0, pl.ds(0, 2)], g1.at[0, 0, 0], g1.at[0, 0, 0])[k]
            take(nes.at[0], ner.at[s * 5 + kind(b, k)], bytes_in).wait_recv()
            n = kind(b, k) + (0 if s == 0 else 5)
            for d in range(2):
                for m, o in enumerate((1, -1)):
                    if s == 0:
                        bx, by = (x, (y - o + 4) % 4) if d == 0 else ((x - o + 4) % 4, y)
                    else:
                        j = s - 1
                        bx, by = ((x - o + 4) % 4, (y + j) % 4) if d == 0 else ((x + j) % 4, (y - o + 4) % 4)
                    region = piece(bx, zz, by, d, k, m)
                    rc(region, region, fas.at[int(k == 1)], far.at[n], along(d if s == 0 else 1 - d, o)).start()

    def first_ring_done(b, ks):
        for k in ks:
            region = (g1.at[0, 0, 0], g2.at[0, 0, 0], g1.at[0, 0, 0, pl.ds(0, 128)], g1.at[0, 0, 0, pl.ds(0, 128)])[k]
            take(fas.at[0], far.at[kind(b, k)], region).wait_recv()

    def second_ring_done(b, ks):
        for k in ks:
            region = (g1.at[0, 0], g2.at[0, 0], g1.at[0, 0, pl.ds(0, 2)], g1.at[0, 0, pl.ds(0, 2)])[k]
            take(fas.at[0], far.at[5 + kind(b, k)], region).wait_recv()

    def start(copies):
        for cp in copies:
            cp.start()

    def arrived(copies):
        for cp in copies:
            cp.wait_recv()

    columns = (pl.ds(0, 640), pl.ds(640, 640))

    def quarter(d, px, py):
        return pl.ds(pl.multiple_of((px if d == 0 else py) * 48, 16), 48)

    def wo_z():
        rows = quarter(0, x, y), quarter(1, x, y)
        out = []
        for o, d in ((1, 0), (1, 1), (-1, 0), (-1, 1), (2, 0), (-2, 1)):
            dst = wo.at[t, rows[d], columns[d]]
            out.append(rc(wo_in.at[rows[d], columns[d]], dst, wos.at[0], wor.at[0], ring(o)))
        return out

    def wo_plane(j, inbound):
        out = []
        for o in (1, 3, 2):
            for d in range(2):
                sign = -o if inbound else o
                px, py = ((x + sign + 4) % 4, y) if d == 0 else (x, (y + sign + 4) % 4)
                rows = quarter(d, px, py) if inbound else quarter(d, x, y)
                region = wo.at[((zl + j) % 4) * 2 + core, rows, columns[d]]
                out.append(rc(region, region, wos.at[0], wor.at[j], at(px, zh, py)))
        return out

    def wo_sibling(j, inbound):
        region = wo.at[((zl + j) % 4) * 2 + (1 - core if inbound else core)]
        return rc(region, region, sibs.at[0], sibr.at[0], sibling)

    for cp in vision_loads:
        cp.wait()
    base32[...] = base[...].astype(F32)
    lat_norm = layer_norm(base32[...]).astype(BF16)
    q = dot(lat_norm, wq[...], 1, 1) * VHEAD_DIM ** (-0.5)
    k_lat = dot(lat_norm, wkv_vis[0], 1, 1).astype(BF16)
    v_lat = dot(lat_norm, wkv_vis[1], 1, 1).astype(BF16)
    lane = lax.broadcasted_iota(jnp.int32, (64, 192), 1)
    first_head = lane < VHEAD_DIM
    q_block = jnp.concatenate([jnp.where(first_head, q, 0.0), jnp.where(first_head, 0.0, q)], 0).astype(BF16)
    s_lat = dot(k_lat, q_block, 1, 1)
    m_lat = jnp.max(s_lat, axis=0, keepdims=True)

    def vision_chunk(c):
        ch = chunk(c)
        patch_load(c).wait()

        def norm(r, carry):
            rows = patches[pl.ds(pl.multiple_of(ch * 512 + r * 64, 64), 64), :].astype(F32)
            ctx[pl.ds(pl.multiple_of(r * 64, 64), 64), :] = layer_norm(rows).astype(BF16)
            return carry

        lax.fori_loop(0, 8, norm, 0)
        kc = dot(ctx[...], wkv_vis[0], 1, 1).astype(BF16)
        vc = dot(ctx[...], wkv_vis[1], 1, 1).astype(BF16)
        s = dot(kc, q_block, 1, 1).reshape(8, 64, 128)
        m = jnp.maximum(jnp.max(s, axis=1, keepdims=True), m_lat[None])
        e_ctx = jnp.exp(s - m)
        e_lat = jnp.exp(s_lat[None] - m)
        total = jnp.sum(e_ctx, axis=1, keepdims=True) + jnp.sum(e_lat, axis=1, keepdims=True)
        inverse = 1.0 / total
        p_ctx = (e_ctx * inverse).astype(BF16)
        p_lat = (e_lat * inverse).astype(BF16)
        mixed = []
        for v in range(8):
            p = jnp.concatenate([p_ctx[v], p_lat[v]], 0)
            values = jnp.concatenate([vc[v * 64:(v + 1) * 64], v_lat], 0)
            o = dot(p, values, 0, 0)
            mixed.append(jnp.where(first_head, o[:64], o[64:]))
        for u in range(8):
            rows = jnp.concatenate([o[u * 8:(u + 1) * 8] for o in mixed], 0)
            hs[u, ch, pl.ds(0, 64)] = rows[:, :128].astype(BF16)
            hs[u, ch, pl.ds(64, 32)] = jnp.concatenate([rows[:32, 128:], rows[32:, 128:]], 1).astype(BF16)

    def head_copy(c, j):
        ch = chunk(c)
        other = (t + j) % 8
        return rc(hs.at[other, ch], hbuf.at[t, ch], has.at[0], har.at[c], tens(other))

    def head_local(c):
        return pltpu.make_async_copy(hs.at[t, chunk(c)], hbuf.at[t, chunk(c)], lsem.at[4 + c])

    def head_start(c):
        for j in range(1, 8):
            head_copy(c, j).start()
        head_local(c).start()

    with jax.named_scope("vision_0"):
        vision_chunk(ORDER[0])
    with jax.named_scope("entry_barrier"):
        pl.semaphore_wait(barrier, 27)
    start(wo_z())
    head_start(ORDER[0])
    w0(1).start()
    near(0, 0, (1, 0))
    near(0, 1, (1, 0))
    with jax.named_scope("vision_1"):
        vision_chunk(ORDER[1])
    head_start(ORDER[1])
    with jax.named_scope("vision_2"):
        vision_chunk(ORDER[2])
    head_start(ORDER[2])
    with jax.named_scope("w_a"):
        forward(0, 0, (1, 0))
    with jax.named_scope("wo_plane"):
        take(wos.at[0], wor.at[0], rows_of(144)).wait_recv()
        for j in range(1, 4):
            start(wo_plane(j, False))
    local_wo.wait()
    wo_sibling(0, False).start()
    near(0, 2, (1, 0))
    with jax.named_scope("vision_3"):
        vision_chunk(ORDER[3])
    head_start(ORDER[3])
    near(0, 4, (1, 0))
    with jax.named_scope("w_b"):
        first_ring_done(0, (1, 0))
        near(0, 3, (1, 0))

    local_hidden.wait()

    def norm_tokens(r, carry):
        rows = pl.ds(pl.multiple_of(r * 16, 16), 16)
        tokn[rows, :] = layer_norm(tokn[rows, :].astype(F32)).astype(BF16)
        return carry

    with jax.named_scope("token_norm"):
        lax.fori_loop(0, 8, norm_tokens, 0)
    with jax.named_scope("text_kv"):
        w0(1).wait_recv()
        near(1, 0, (1,))
    with jax.named_scope("wait_wo_plane"):
        for j in range(1, 4):
            take(wos.at[0], wor.at[j], rows_of(144)).wait_recv()
            wo_sibling(j, False).start()
    with jax.named_scope("token_norm"):
        lax.fori_loop(8, 12, norm_tokens, 0)

    with jax.named_scope("wait_wo_sibling"):
        take(sibs.at[0], sibr.at[0], rows_of(768)).wait_recv()

    def v4(c, i):
        px, py = (x + c) % 4, (y + i) % 4
        device, mine, theirs, here = at(px, zh, py), px * 8 + zh * 4 + py, px * 8 + (1 - zh) * 4 + py, x * 4 + y
        return [
            rc(latp.at[mine], lall.at[zh, t, here], v4s.at[0], v4r.at[c], device),
            rc(latp.at[theirs], xown.at[here], v4s.at[0], v4r.at[c], device),
        ]

    def v4_arrived(c):
        take(v4s.at[0], v4r.at[c], latp.at[pl.ds(0, 6 if c == 0 else 8)]).wait_recv()

    local_lat = (
        pltpu.make_async_copy(latp.at[dp], lall.at[zh, t, x * 4 + y], lsem.at[13]),
        pltpu.make_async_copy(latp.at[x * 8 + (1 - zh) * 4 + y], xown.at[x * 4 + y], lsem.at[14]),
    )
    my_base = base32[pl.ds(pl.multiple_of(t * 8, 8), 8), :]

    def project(chunks):
        wide, narrow = [], []
        for c in chunks:
            ch = chunk(c)
            with jax.named_scope("wait_heads"):
                take(has.at[0], har.at[c], hs.at[pl.ds(0, 7), ch]).wait_recv()
                head_local(c).wait()
            wide.append(jnp.concatenate([hbuf[g, ch, pl.ds(0, 64)] for g in range(8)], 1))
            parts = []
            for g in range(8):
                packed = hbuf[g, ch, pl.ds(64, 32)]
                parts.append(jnp.concatenate([packed[:, :64], packed[:, 64:]], 0))
            narrow.append(jnp.concatenate(parts, 1))
        if chunks == ORDER[2:]:
            for k in (2, 3):
                w0(k).start()
        wide, narrow = jnp.concatenate(wide, 0), jnp.concatenate(narrow, 0)
        mix = dot(wide, wo[:, :128].reshape(1024, 1280)) + dot(narrow, wo[:, 128:].reshape(512, 1280))
        mix = layer_norm(mix.reshape(16, 8, 1280) + my_base[None])
        packed = jnp.concatenate([mix[:, :, :640], mix[:, :, 640:]], 1).astype(BF16)
        for n, c in enumerate(chunks):
            ch = chunk(c)
            lat_out[pl.ds(ch * 8, 8)] = mix[n * 8:(n + 1) * 8].astype(BF16)
            latp[pl.ds(ch * 8, 8)] = packed[n * 8:(n + 1) * 8]
        for c in chunks:
            for i in range(4):
                if c == 0 and i == 0:
                    start(local_lat)
                else:
                    start(v4(c, i))

    with jax.named_scope("project_0"):
        project(ORDER[:2])
    with jax.named_scope("project_1"):
        project(ORDER[2:])

    def part(c):
        return pl.ds(((x - c + 4) % 4) * 4, 4)

    def block(plane, own_core=True):
        return lall.at[plane // 4, (plane % 4) * 2 + (core if own_core else 1 - core)]

    def level(up):
        return zl if up else 3 - zl

    def flow(up, h, c, inbound, source=None):
        o = 1 if up else -1
        plane = (z - o * h + 8) % 8
        region = block(plane).at[part(c)]
        rs = upr if up else dnr
        src = region if source is None else source.at[part(c)]
        n = (h - 1 if inbound else h) * 4 + c
        return rc(src, region, fls.at[0], rs.at[n], ring(-o if inbound else o))

    def pass_on(up, c):
        o = 1 if up else -1
        return rc(xown.at[part(c)], transit.at[part(c)], fls.at[0], trr.at[(0 if up else 4) + c], ring(o))

    def sib(plane, c, inbound):
        region = block(plane, not inbound).at[part(c)]
        return rc(region, region, lss.at[0], lsr.at[plane], sibling)

    def sib_arrived(plane):
        take(lss.at[0], lsr.at[plane], block(plane, False)).wait_recv()

    def offset(up, h):
        return (z - h + 8) % 8 if up else (z + h) % 8

    def wave_own(c):
        if c == 0:
            for cp in local_lat:
                cp.wait()
        v4_arrived(c)
        for up in (True, False):
            at_level = level(up)
            pl.when(at_level < 3)(lambda: flow(up, 0, c, False).start())
            pl.when(at_level == 2)(lambda: pass_on(up, c).start())
            pl.when(at_level == 3)(lambda: flow(up, 0, c, False, xown).start())
        sib(z, c, False).start()

    def wave(h, c):
        for up in (True, False):
            at_level = level(up)
            if h == 1:
                @pl.when(at_level == 3)
                def _():
                    pass_on(up, c).wait_recv()
                    flow(up, 1, c, False, transit).start()

            @pl.when(at_level + 2 >= h)
            def _():
                flow(up, h, c, True).wait_recv()
                if h < 5:
                    pl.when(at_level < 3)(lambda: flow(up, h, c, False).start())
                sib(offset(up, h), c, False).start()

    def query_half(zz, cols, first):
        def step(i, carry):
            contracted = pl.ds(pl.multiple_of((i * 2 + zz) * 1024, 1024), 1024)
            part = dot(tokn[:, contracted], g1[i, zz, :, :, cols].reshape(1024, -1))
            qacc[:, cols] = qacc[:, cols] + part
            return carry

        if first:
            qacc[...] = jnp.zeros_like(qacc)
        lax.fori_loop(0, 4, step, 0)

    def query_done(half):
        cols = slice(half * 256, (half + 1) * 256)
        second_ring_done(1, (2 + half,))
        query_half(1 - zh, cols, False)
        qh[:, cols] = (qacc[:, cols] * (HEAD_DIM ** (-0.5) * LOG2E)).astype(BF16)

    def pack_weights(zz):
        for xx in range(4):
            rows = pl.ds(pl.multiple_of((xx * 2 + zz) * 160, 160), 160)
            for k in range(2):
                block = g2[xx, zz, :, k].astype(F32).reshape(160, 512)
                wkv[rows, k * 512:(k + 1) * 512] = block.astype(BF16)

    def project_text(plane):
        lat = lall[plane // 4, pl.ds((plane % 4) * 2, 2)].astype(F32).reshape(32, 16, 640)
        rows = jnp.concatenate([lat[:, :8], lat[:, 8:]], 2).reshape(256, 1280).astype(BF16)
        kv_text[plane] = dot(rows, wkv[...]).astype(BF16)

    def project_half(plane, half):
        lat = lall[plane // 4, (plane % 4) * 2 + half].astype(F32)
        rows = jnp.concatenate([lat[:, :8], lat[:, 8:]], 2).reshape(128, 1280).astype(BF16)
        kv_text[plane, pl.ds(pl.multiple_of(half * 128, 128), 128)] = dot(rows, wkv[...]).astype(BF16)

    def attend(planes, heads, first=False, last=False):
        with jax.named_scope("attend"):
            ones = jnp.ones((256, 128), BF16)
            own = {h: slice(h * 128, (h + 1) * 128) for h in heads}
            old = {} if first else {h: top[h] for h in heads}
            masks = [bias[plane // 4] for plane in planes]
            scores, new, totals = {}, {}, {}
            for h in heads:
                scores[h] = [
                    dot(qh[:, own[h]], kv_text[plane, :, own[h]], 1, 1) + mask for plane, mask in zip(planes, masks)
                ]
            for h in heads:
                m = scores[h][0]
                for s in scores[h][1:]:
                    m = jnp.maximum(m, s)
                m = jnp.max(m, axis=1, keepdims=True)
                new[h] = m if first else jnp.maximum(old[h], m)
            for h in heads:
                weights = [jnp.exp2(s - new[h][:, :1]).astype(BF16) for s in scores[h]]
                parts = [
                    dot(p, jnp.concatenate([kv_text[plane, :, 512 + h * 128:512 + (h + 1) * 128], ones], 1))
                    for plane, p in zip(planes, weights)
                ]
                totals[h] = sum(parts[1:], parts[0])
            for h in heads:
                total = totals[h]
                if not first:
                    shrink = jnp.exp2(old[h] - new[h])
                    total = total + acc[h] * jnp.concatenate([shrink, shrink], 1)
                if last:
                    result = total[:, :128] / total[:, 128:]
                    seen_any = bias[0, :, :1] == 0.0
                    att_out[:, own[h]] = jnp.where(seen_any, result, 0.0).astype(BF16)
                else:
                    acc[h] = total
                    top[h] = jnp.broadcast_to(new[h], (256, 128))

    def kv_ready(plane):
        sib_arrived(plane)
        with jax.named_scope("project_text"):
            project_text(plane)

    def waves(h, chunks):
        with jax.named_scope("wave_" + str(h)):
            for c in chunks:
                wave(h, c)

    with jax.named_scope("token_norm"):
        lax.fori_loop(12, 16, norm_tokens, 0)
    with jax.named_scope("wave_own"):
        for c in ORDER[:2]:
            wave_own(c)
        forward(0, 1, (1, 0))
        forward(0, 2, (1, 0))
        for c in ORDER[2:]:
            wave_own(c)
    with jax.named_scope("w_e"):
        w0(2).wait_recv()
        near(1, 0, (2,))
        near(1, 1, (2,))
    with jax.named_scope("w_c0"):
        forward(1, 0, (1,))
    with jax.named_scope("w_d"):
        for st in (4, 3):
            forward(0, st, (1, 0))
    with jax.named_scope("w_c"):
        first_ring_done(1, (1,))
        for st in (1, 2, 4, 3):
            near(1, st, (1,))
    with jax.named_scope("w_e"):
        w0(3).wait_recv()
        near(1, 0, (3,))
        near(1, 1, (3,))
    limit = jnp.minimum(seen[...], frame_count[...])
    row = lax.broadcasted_iota(jnp.int32, (256, 256), 0) % 128 // 8
    for zz in range(2):
        key_frame = row // 4 * 8 + zz * 4 + row % 4
        bias[zz] = jnp.where(key_frame < limit, 0.0, MASKED).T
    waves(1, ORDER)
    with jax.named_scope("w_f"):
        for st in (1, 2, 4, 3):
            forward(1, st, (1,))
    with jax.named_scope("w_g2"):
        forward(1, 0, (2,))
        near(1, 2, (2,))
        near(1, 4, (2,))
        forward(1, 1, (2,))
    waves(2, ORDER)
    with jax.named_scope("pack"):
        local_kv.wait()
        second_ring_done(0, (1,))
        second_ring_done(1, (1,))
        pack_weights(zh)
        pack_weights(1 - zh)
    kv_ready(z)
    with jax.named_scope("w_h2"):
        first_ring_done(1, (2,))
        near(1, 3, (2,))
        forward(1, 2, (2,))
        forward(1, 4, (2,))
    with jax.named_scope("w_g3"):
        forward(1, 0, (3,))
        near(1, 2, (3,))
        near(1, 4, (3,))
        forward(1, 1, (3,))
    kv_ready((z + 1) % 8)
    kv_ready((z + 7) % 8)
    waves(3, ORDER[:2])
    with jax.named_scope("query_0"):
        local_q.wait()
        second_ring_done(0, (0,))
        query_half(zh, slice(0, 512), True)
    waves(3, ORDER[2:])
    with jax.named_scope("w_i2"):
        forward(1, 3, (2,))
    kv_ready((z + 2) % 8)
    with jax.named_scope("w_h3"):
        first_ring_done(1, (3,))
        near(1, 3, (3,))
        forward(1, 2, (3,))
        forward(1, 4, (3,))
    kv_ready((z + 6) % 8)
    final = 5 - (zl + 1) // 2
    early = 3 + 2 * (zl // 3)
    between = 12 - final - early
    pairs = [
        (z, (z + 1) % 8),
        ((z + 7) % 8, (z + 2) % 8),
        ((z + 6) % 8, (z + early) % 8, (z + between) % 8),
        ((z + final) % 8,),
    ]
    waves(4, ORDER[:2])
    kv_ready((z + early) % 8)
    with jax.named_scope("query_1"):
        query_done(0)
    with jax.named_scope("w_i3"):
        forward(1, 3, (3,))
    attend(pairs[0], (0, 1), first=True)
    waves(4, ORDER[2:])
    attend(pairs[1], (0, 1))
    kv_ready((z + between) % 8)
    attend(pairs[2], (0, 1))
    waves(5, ORDER[:2])
    with jax.named_scope("drain_early"):
        take(has.at[0], har.at[0], hs.at[pl.ds(0, 7)]).wait_send()
        take(v4s.at[0], v4r.at[0], rows_of(240)).wait_send()
        take(wos.at[0], wor.at[0], rows_of(576)).wait_send()
        take(sibs.at[0], sibr.at[0], rows_of(768)).wait_send()
        take(nes.at[0], ner.at[0], rows_of(2048)).wait_send()
        take(nes.at[1], ner.at[0], rows_of(640)).wait_send()
        for k in (1, 2, 3):
            w0(k).wait_send()
    with jax.named_scope("query_1"):
        query_done(1)
    attend(pairs[0], (2, 3), first=True)
    attend(pairs[1], (2, 3))
    attend(pairs[2], (2, 3))
    waves(5, ORDER[2:])
    last_plane = (z + final) % 8
    with jax.named_scope("project_own_half"):
        project_half(last_plane, core)
    sib_arrived(last_plane)
    with jax.named_scope("project_other_half"):
        project_half(last_plane, 1 - core)
    attend(pairs[3], (0, 1, 2, 3), last=True)

    with jax.named_scope("drain"):
        take(lss.at[0], lsr.at[0], rows_of(1024)).wait_send()
        take(fas.at[0], far.at[0], rows_of(1024)).wait_send()
        take(fas.at[1], far.at[0], rows_of(320)).wait_send()
        middle = (zl == 1) | (zl == 2)
        pl.when(middle)(lambda: take(fls.at[0], upr.at[0], rows_of(1280)).wait_send())
        pl.when(jnp.logical_not(middle))(lambda: take(fls.at[0], upr.at[0], rows_of(640)).wait_send())


def local(
    video_patches,
    frame_count,
    seen_frames,
    base_latents,
    vision_query,
    vision_kv,
    vision_out,
    hidden_states,
    text_query,
    text_kv,
):
    width = video_patches.shape[-1]
    vm = pl.BlockSpec(memory_space=pltpu.VMEM)
    hbm = pl.BlockSpec(memory_space=pl.ANY)
    dma = lambda n: pltpu.SemaphoreType.DMA((n,))
    latents_out, attended = pl.pallas_call(
        fused_kernel,
        name="fused",
        out_shape=(
            pltpu.VMEM((32, 8, 1280), BF16),
            pltpu.VMEM((256, 512), BF16),
        ),
        in_specs=[hbm, vm, vm, hbm, hbm, hbm, hbm, hbm, hbm, hbm],
        out_specs=(vm, vm),
        scratch_shapes=[
            pltpu.VMEM((64, 1280), BF16),
            pltpu.VMEM((192, 1280), BF16),
            pltpu.VMEM((2, 192, 1280), BF16),
            pltpu.VMEM((2048, 1280), BF16),
            pltpu.VMEM((512, 1280), BF16),
            pltpu.VMEM((8, 192, 1280), BF16),
            pltpu.VMEM((8, 4, 96, 128), BF16),
            pltpu.VMEM((8, 4, 96, 128), BF16),
            pltpu.VMEM((64, 1280), F32),
            pltpu.VMEM((32, 16, 640), BF16),
            pltpu.VMEM((2, 8, 16, 16, 640), BF16),
            pltpu.VMEM((16, 16, 640), BF16),
            pltpu.VMEM((16, 16, 640), BF16),
            pltpu.VMEM((4, 2, 4, 256, 512), BF16),
            pltpu.VMEM((4, 2, 4, 2, 40, 512), BF16),
            pltpu.VMEM((1280, 1024), BF16),
            pltpu.VMEM((256, 8192), BF16),
            pltpu.VMEM((256, 512), F32),
            pltpu.VMEM((256, 512), BF16),
            pltpu.VMEM((8, 256, 1024), BF16),
            pltpu.VMEM((2, 256, 256), F32),
            pltpu.VMEM((4, 256, 128), F32),
            pltpu.VMEM((4, 256, 256), F32),
            dma(18), dma(3), dma(3), dma(2), dma(25), dma(2), dma(10), dma(1), dma(4), dma(1), dma(1),
            dma(1), dma(4), dma(1), dma(4), dma(1), dma(20), dma(20), dma(8), dma(1), dma(8),
        ],
        compiler_params=pltpu.CompilerParams(
            collective_id=0, has_side_effects=True, vmem_limit_bytes=60 * 2**20
        ),
        cost_estimate=pl.CostEstimate(flops=14 * 10**9, bytes_accessed=40 * 10**6, transcendentals=3 * 10**6),
    )(
        video_patches.reshape(-1, width),
        frame_count.reshape(1, 1),
        seen_frames,
        base_latents,
        vision_query.T,
        vision_kv.transpose(0, 2, 1),
        vision_out,
        hidden_states,
        text_query,
        text_kv,
    )
    return latents_out[:, None], attended


def solution(mesh):
    placed = (
        P(None, "dp", None, None),
        P("dp"),
        P("dp", None),
        P(),
        P(None, "tensor"),
        P(None, None, "tensor"),
        P("tensor", None),
        P("dp", None),
        P("dp", "tensor"),
        P(None, "dp", "tensor"),
    )
    return jax.shard_map(
        local,
        mesh=mesh,
        in_specs=placed,
        out_specs=(P(None, "dp", "tensor", None), P("dp", "tensor")),
        check_vma=False,
    )
```

```python
import jax
import jax.numpy as jnp
from jax import lax
from jax.experimental import pallas as pl
from jax.experimental.pallas import tpu as pltpu
from jax.sharding import PartitionSpec as P

HEAD_DIM = 128
VHEAD_DIM = 96
EPSILON = 1e-05
MASKED = -1e30
LOG2E = 1.4426950408889634
MESH = pl.DeviceIdType.MESH
ORDER = (2, 1, 3, 0)
F32 = jnp.float32
BF16 = jnp.bfloat16


def layer_norm(values):
    average = jnp.mean(values, axis=-1, keepdims=True)
    centered = values - average
    variance = jnp.mean(centered * centered, axis=-1, keepdims=True)
    return centered * lax.rsqrt(variance + EPSILON)


def dot(a, b, ca=1, cb=0):
    return lax.dot_general(a, b, (((ca,), (cb,)), ((), ())), preferred_element_type=F32)


def fused_kernel(
    patches_in, frame_count, seen, base_in, wq_in, wkv_vis_in, wo_in, hidden_in, q_in, kv_in,
    lat_out, att_out,
    base, wq, wkv_vis, patches, ctx, wo, hs, hbuf, base32, latp, lall, xown, transit, g1, g2, wkv, tokn, qacc, qh, kv_text, bias, top, acc,
    lsem, w0s, w0r, nes, ner, fas, far, wos, wor, sibs, sibr, has, har, v4s, v4r, fls, upr, dnr, trr, lss, lsr,
):
    dp = lax.axis_index("dp")
    t = lax.axis_index("tensor")
    x = dp // 8
    zh = (dp // 4) % 2
    y = dp % 4
    zl = t // 2
    core = t % 2
    z = zh * 4 + zl

    def at(xx, zz, yy):
        return {"dp": (xx * 2 + zz) * 4 + yy, "tensor": t}

    def ring(offset):
        zz = (z + offset + 8) % 8
        return {"dp": (x * 2 + zz // 4) * 4 + y, "tensor": (zz % 4) * 2 + core}

    def tens(tt):
        return {"dp": dp, "tensor": tt}

    sibling = tens(t + 1 - 2 * core)

    def rc(src, dst, ss, rs, device):
        return pltpu.make_async_remote_copy(
            src_ref=src, dst_ref=dst, send_sem=ss, recv_sem=rs, device_id=device, device_id_type=MESH
        )

    barrier = pltpu.get_barrier_semaphore()

    for j in range(1, 16):
        greeted = {"dp": ((x + j // 4) % 4 * 2 + zh) * 4 + (y + j % 4) % 4, "tensor": t}
        pl.semaphore_signal(barrier, inc=1, device_id=greeted, device_id_type=MESH)
    pl.semaphore_signal(barrier, inc=1, device_id=at(x, 1 - zh, y), device_id_type=MESH)
    for j in range(1, 8):
        pl.semaphore_signal(barrier, inc=1, device_id=tens((t + j) % 8), device_id_type=MESH)
    for o in (1, -1, 2, -2):
        pl.semaphore_signal(barrier, inc=1, device_id=ring(o), device_id_type=MESH)

    def chunk(c):
        return (x + c) % 4

    def patch_load(c):
        rows = pl.ds(pl.multiple_of(chunk(c) * 512, 512), 512)
        return pltpu.make_async_copy(patches_in.at[rows], patches.at[rows], lsem.at[8 + c])

    vision_loads = (
        pltpu.make_async_copy(base_in, base, lsem.at[15]),
        pltpu.make_async_copy(wq_in, wq, lsem.at[16]),
        pltpu.make_async_copy(wkv_vis_in, wkv_vis, lsem.at[17]),
    )
    for cp in vision_loads:
        cp.start()
    for c in ORDER:
        patch_load(c).start()
    local_q = pltpu.make_async_copy(q_in, g1.at[x, zh, y], lsem.at[0])
    local_kv = pltpu.make_async_copy(kv_in, g2.at[x, zh, y], lsem.at[1])
    local_wo = pltpu.make_async_copy(wo_in, wo.at[t], lsem.at[2])
    local_hidden = pltpu.make_async_copy(hidden_in, tokn, lsem.at[12])
    for cp in (local_q, local_kv, local_wo, local_hidden):
        cp.start()

    def rows_of(n):
        return patches.at[pl.ds(0, n)]

    def take(sem_send, sem_recv, region):
        return rc(region, region, sem_send, sem_recv, sibling)

    halves = (pl.ds(0, 128), pl.ds(128, 128))
    quarters = ((pl.ds(0, 64), pl.ds(64, 64)), (pl.ds(128, 64), pl.ds(192, 64)))
    lanes = (pl.ds(0, 256), pl.ds(256, 256))

    def w0(k):
        if k == 1:
            src, dst = kv_in, g2.at[x, zh, y]
        else:
            src, dst = q_in.at[:, lanes[k - 2]], g1.at[x, zh, y, :, lanes[k - 2]]
        return rc(src, dst, w0s.at[k - 1], w0r.at[k - 1], at(x, 1 - zh, y))

    def along(d, o):
        return at(x, zh, (y + o + 4) % 4) if d == 0 else at((x + o + 4) % 4, zh, y)

    def kind(b, k):
        return {(0, 0): 0, (0, 1): 1, (1, 1): 2, (1, 2): 3, (1, 3): 4}[b, k]

    def piece(bx, zz, by, d, k, m=None):
        if k == 1:
            return g2.at[bx, zz, by, d] if m is None else g2.at[bx, zz, by, d, :, lanes[m]]
        rows = halves[d] if m is None else quarters[d][m]
        return g1.at[bx, zz, by, rows] if k == 0 else g1.at[bx, zz, by, rows, lanes[k - 2]]

    def near(b, s, ks):
        zz = zh if b == 0 else 1 - zh
        for k in ks:
            for d in range(2):
                j = max(s - 1, 0)
                bx, by = (x, (y + j) % 4) if d == 0 else ((x + j) % 4, y)
                dst = piece(bx, zz, by, d, k)
                src = dst
                if b == 0 and j == 0:
                    src = q_in.at[halves[d]] if k == 0 else kv_in.at[d]
                for o in (1, -1):
                    device = along(d if s == 0 else 1 - d, o)
                    rc(src, dst, nes.at[int(k == 1)], ner.at[s * 5 + kind(b, k)], device).start()

    def forward(b, s, ks):
        zz = zh if b == 0 else 1 - zh
        for k in ks:
            bytes_in = (g1.at[0, 0, pl.ds(0, 2)], g2.at[0, 0, pl.ds(0, 2)], g1.at[0, 0, 0], g1.at[0, 0, 0])[k]
            take(nes.at[0], ner.at[s * 5 + kind(b, k)], bytes_in).wait_recv()
            n = kind(b, k) + (0 if s == 0 else 5)
            for d in range(2):
                for m, o in enumerate((1, -1)):
                    if s == 0:
                        bx, by = (x, (y - o + 4) % 4) if d == 0 else ((x - o + 4) % 4, y)
                    else:
                        j = s - 1
                        bx, by = ((x - o + 4) % 4, (y + j) % 4) if d == 0 else ((x + j) % 4, (y - o + 4) % 4)
                    region = piece(bx, zz, by, d, k, m)
                    rc(region, region, fas.at[int(k == 1)], far.at[n], along(d if s == 0 else 1 - d, o)).start()

    def first_ring_done(b, ks):
        for k in ks:
            region = (g1.at[0, 0, 0], g2.at[0, 0, 0], g1.at[0, 0, 0, pl.ds(0, 128)], g1.at[0, 0, 0, pl.ds(0, 128)])[k]
            take(fas.at[0], far.at[kind(b, k)], region).wait_recv()

    def second_ring_done(b, ks):
        for k in ks:
            region = (g1.at[0, 0], g2.at[0, 0], g1.at[0, 0, pl.ds(0, 2)], g1.at[0, 0, pl.ds(0, 2)])[k]
            take(fas.at[0], far.at[5 + kind(b, k)], region).wait_recv()

    def start(copies):
        for cp in copies:
            cp.start()

    def arrived(copies):
        for cp in copies:
            cp.wait_recv()

    columns = (pl.ds(0, 640), pl.ds(640, 640))

    def quarter(d, px, py):
        return pl.ds(pl.multiple_of((px if d == 0 else py) * 48, 16), 48)

    def wo_z():
        rows = quarter(0, x, y), quarter(1, x, y)
        out = []
        for o, d in ((1, 0), (1, 1), (-1, 0), (-1, 1), (2, 0), (-2, 1)):
            dst = wo.at[t, rows[d], columns[d]]
            out.append(rc(wo_in.at[rows[d], columns[d]], dst, wos.at[0], wor.at[0], ring(o)))
        return out

    def wo_plane(j, inbound):
        out = []
        for o in (1, 3, 2):
            for d in range(2):
                sign = -o if inbound else o
                px, py = ((x + sign + 4) % 4, y) if d == 0 else (x, (y + sign + 4) % 4)
                rows = quarter(d, px, py) if inbound else quarter(d, x, y)
                region = wo.at[((zl + j) % 4) * 2 + core, rows, columns[d]]
                out.append(rc(region, region, wos.at[0], wor.at[j], at(px, zh, py)))
        return out

    def wo_sibling(j, inbound):
        region = wo.at[((zl + j) % 4) * 2 + (1 - core if inbound else core)]
        return rc(region, region, sibs.at[0], sibr.at[0], sibling)

    for cp in vision_loads:
        cp.wait()
    base32[...] = base[...].astype(F32)
    lat_norm = layer_norm(base32[...]).astype(BF16)
    q = dot(lat_norm, wq[...], 1, 1) * VHEAD_DIM ** (-0.5)
    k_lat = dot(lat_norm, wkv_vis[0], 1, 1).astype(BF16)
    v_lat = dot(lat_norm, wkv_vis[1], 1, 1).astype(BF16)
    lane = lax.broadcasted_iota(jnp.int32, (64, 192), 1)
    first_head = lane < VHEAD_DIM
    q_block = jnp.concatenate([jnp.where(first_head, q, 0.0), jnp.where(first_head, 0.0, q)], 0).astype(BF16)
    s_lat = dot(k_lat, q_block, 1, 1)
    m_lat = jnp.max(s_lat, axis=0, keepdims=True)

    def vision_chunk(c):
        ch = chunk(c)
        patch_load(c).wait()

        def norm(r, carry):
            rows = patches[pl.ds(pl.multiple_of(ch * 512 + r * 64, 64), 64), :].astype(F32)
            ctx[pl.ds(pl.multiple_of(r * 64, 64), 64), :] = layer_norm(rows).astype(BF16)
            return carry

        lax.fori_loop(0, 8, norm, 0)
        kc = dot(ctx[...], wkv_vis[0], 1, 1).astype(BF16)
        vc = dot(ctx[...], wkv_vis[1], 1, 1).astype(BF16)
        s = dot(kc, q_block, 1, 1).reshape(8, 64, 128)
        m = jnp.maximum(jnp.max(s, axis=1, keepdims=True), m_lat[None])
        e_ctx = jnp.exp(s - m)
        e_lat = jnp.exp(s_lat[None] - m)
        total = jnp.sum(e_ctx, axis=1, keepdims=True) + jnp.sum(e_lat, axis=1, keepdims=True)
        inverse = 1.0 / total
        p_ctx = (e_ctx * inverse).astype(BF16)
        p_lat = (e_lat * inverse).astype(BF16)
        mixed = []
        for v in range(8):
            p = jnp.concatenate([p_ctx[v], p_lat[v]], 0)
            values = jnp.concatenate([vc[v * 64:(v + 1) * 64], v_lat], 0)
            o = dot(p, values, 0, 0)
            mixed.append(jnp.where(first_head, o[:64], o[64:]))
        for u in range(8):
            rows = jnp.concatenate([o[u * 8:(u + 1) * 8] for o in mixed], 0)
            hs[u, ch, pl.ds(0, 64)] = rows[:, :128].astype(BF16)
            hs[u, ch, pl.ds(64, 32)] = jnp.concatenate([rows[:32, 128:], rows[32:, 128:]], 1).astype(BF16)

    def head_copy(c, j):
        ch = chunk(c)
        other = (t + j) % 8
        return rc(hs.at[other, ch], hbuf.at[t, ch], has.at[0], har.at[c], tens(other))

    def head_start(c):
        for j in range(1, 8):
            head_copy(c, j).start()
        hbuf[t, chunk(c)] = hs[t, chunk(c)]

    with jax.named_scope("vision_0"):
        vision_chunk(ORDER[0])
    with jax.named_scope("entry_barrier"):
        pl.semaphore_wait(barrier, 27)
    start(wo_z())
    head_start(ORDER[0])
    w0(1).start()
    near(0, 0, (1, 0))
    near(0, 1, (1, 0))
    with jax.named_scope("vision_1"):
        vision_chunk(ORDER[1])
    head_start(ORDER[1])
    with jax.named_scope("vision_2"):
        vision_chunk(ORDER[2])
    head_start(ORDER[2])
    with jax.named_scope("w_a"):
        forward(0, 0, (1, 0))
    with jax.named_scope("wo_plane"):
        take(wos.at[0], wor.at[0], rows_of(144)).wait_recv()
        for j in range(1, 4):
            start(wo_plane(j, False))
    local_wo.wait()
    wo_sibling(0, False).start()
    near(0, 2, (1, 0))
    with jax.named_scope("vision_3"):
        vision_chunk(ORDER[3])
    head_start(ORDER[3])
    near(0, 4, (1, 0))
    with jax.named_scope("w_b"):
        first_ring_done(0, (1, 0))
        near(0, 3, (1, 0))

    local_hidden.wait()

    def norm_tokens(r, carry):
        rows = pl.ds(pl.multiple_of(r * 16, 16), 16)
        tokn[rows, :] = layer_norm(tokn[rows, :].astype(F32)).astype(BF16)
        return carry

    with jax.named_scope("token_norm"):
        lax.fori_loop(0, 8, norm_tokens, 0)
    with jax.named_scope("text_kv"):
        w0(1).wait_recv()
        near(1, 0, (1,))
    with jax.named_scope("wait_wo_plane"):
        for j in range(1, 4):
            take(wos.at[0], wor.at[j], rows_of(144)).wait_recv()
            wo_sibling(j, False).start()
    with jax.named_scope("token_norm"):
        lax.fori_loop(8, 12, norm_tokens, 0)

    with jax.named_scope("wait_wo_sibling"):
        take(sibs.at[0], sibr.at[0], rows_of(768)).wait_recv()

    def v4(c, i):
        px, py = (x + c) % 4, (y + i) % 4
        device, mine, theirs, here = at(px, zh, py), px * 8 + zh * 4 + py, px * 8 + (1 - zh) * 4 + py, x * 4 + y
        return [
            rc(latp.at[mine], lall.at[zh, t, here], v4s.at[0], v4r.at[c], device),
            rc(latp.at[theirs], xown.at[here], v4s.at[0], v4r.at[c], device),
        ]

    def v4_arrived(c):
        take(v4s.at[0], v4r.at[c], latp.at[pl.ds(0, 6 if c == 0 else 8)]).wait_recv()

    local_lat = (
        pltpu.make_async_copy(latp.at[dp], lall.at[zh, t, x * 4 + y], lsem.at[13]),
        pltpu.make_async_copy(latp.at[x * 8 + (1 - zh) * 4 + y], xown.at[x * 4 + y], lsem.at[14]),
    )
    my_base = base32[pl.ds(pl.multiple_of(t * 8, 8), 8), :]

    def project(chunks):
        wide, narrow = [], []
        for c in chunks:
            ch = chunk(c)
            with jax.named_scope("wait_heads"):
                take(has.at[0], har.at[c], hs.at[pl.ds(0, 7), ch]).wait_recv()
            wide.append(jnp.concatenate([hbuf[g, ch, pl.ds(0, 64)] for g in range(8)], 1))
            parts = []
            for g in range(8):
                packed = hbuf[g, ch, pl.ds(64, 32)]
                parts.append(jnp.concatenate([packed[:, :64], packed[:, 64:]], 0))
            narrow.append(jnp.concatenate(parts, 1))
        if chunks == ORDER[2:]:
            for k in (2, 3):
                w0(k).start()
        wide, narrow = jnp.concatenate(wide, 0), jnp.concatenate(narrow, 0)
        mix = dot(wide, wo[:, :128].reshape(1024, 1280)) + dot(narrow, wo[:, 128:].reshape(512, 1280))
        mix = layer_norm(mix.reshape(16, 8, 1280) + my_base[None])
        packed = jnp.concatenate([mix[:, :, :640], mix[:, :, 640:]], 1).astype(BF16)
        for n, c in enumerate(chunks):
            ch = chunk(c)
            lat_out[pl.ds(ch * 8, 8)] = mix[n * 8:(n + 1) * 8].astype(BF16)
            latp[pl.ds(ch * 8, 8)] = packed[n * 8:(n + 1) * 8]
        for c in chunks:
            for i in range(4):
                if c == 0 and i == 0:
                    start(local_lat)
                else:
                    start(v4(c, i))

    with jax.named_scope("project_0"):
        project(ORDER[:2])
    with jax.named_scope("project_1"):
        project(ORDER[2:])

    def part(c):
        return pl.ds(((x - c + 4) % 4) * 4, 4)

    def block(plane, own_core=True):
        return lall.at[plane // 4, (plane % 4) * 2 + (core if own_core else 1 - core)]

    def level(up):
        return zl if up else 3 - zl

    def flow(up, h, c, inbound, source=None):
        o = 1 if up else -1
        plane = (z - o * h + 8) % 8
        region = block(plane).at[part(c)]
        rs = upr if up else dnr
        src = region if source is None else source.at[part(c)]
        n = (h - 1 if inbound else h) * 4 + c
        return rc(src, region, fls.at[0], rs.at[n], ring(-o if inbound else o))

    def pass_on(up, c):
        o = 1 if up else -1
        return rc(xown.at[part(c)], transit.at[part(c)], fls.at[0], trr.at[(0 if up else 4) + c], ring(o))

    def sib(plane, c, inbound):
        region = block(plane, not inbound).at[part(c)]
        return rc(region, region, lss.at[0], lsr.at[plane], sibling)

    def sib_arrived(plane):
        take(lss.at[0], lsr.at[plane], block(plane, False)).wait_recv()

    def offset(up, h):
        return (z - h + 8) % 8 if up else (z + h) % 8

    def wave_own(c):
        if c == 0:
            for cp in local_lat:
                cp.wait()
        v4_arrived(c)
        for up in (True, False):
            at_level = level(up)
            pl.when(at_level < 3)(lambda: flow(up, 0, c, False).start())
            pl.when(at_level == 2)(lambda: pass_on(up, c).start())
            pl.when(at_level == 3)(lambda: flow(up, 0, c, False, xown).start())
        sib(z, c, False).start()

    def wave(h, c):
        for up in (True, False):
            at_level = level(up)
            if h == 1:
                @pl.when(at_level == 3)
                def _():
                    pass_on(up, c).wait_recv()
                    flow(up, 1, c, False, transit).start()

            @pl.when(at_level + 2 >= h)
            def _():
                flow(up, h, c, True).wait_recv()
                if h < 5:
                    pl.when(at_level < 3)(lambda: flow(up, h, c, False).start())
                sib(offset(up, h), c, False).start()

    def query_half(zz, cols, first):
        def step(i, carry):
            contracted = pl.ds(pl.multiple_of((i * 2 + zz) * 1024, 1024), 1024)
            part = dot(tokn[:, contracted], g1[i, zz, :, :, cols].reshape(1024, -1))
            qacc[:, cols] = qacc[:, cols] + part
            return carry

        if first:
            qacc[...] = jnp.zeros_like(qacc)
        lax.fori_loop(0, 4, step, 0)

    def query_done(half):
        cols = slice(half * 256, (half + 1) * 256)
        second_ring_done(1, (2 + half,))
        query_half(1 - zh, cols, False)
        qh[:, cols] = (qacc[:, cols] * (HEAD_DIM ** (-0.5) * LOG2E)).astype(BF16)

    def pack_weights(zz):
        for xx in range(4):
            rows = pl.ds(pl.multiple_of((xx * 2 + zz) * 160, 160), 160)
            for k in range(2):
                block = g2[xx, zz, :, k].astype(F32).reshape(160, 512)
                wkv[rows, k * 512:(k + 1) * 512] = block.astype(BF16)

    def project_text(plane):
        lat = lall[plane // 4, pl.ds((plane % 4) * 2, 2)].astype(F32).reshape(32, 16, 640)
        rows = jnp.concatenate([lat[:, :8], lat[:, 8:]], 2).reshape(256, 1280).astype(BF16)
        kv_text[plane] = dot(rows, wkv[...]).astype(BF16)

    def attend(planes, heads, first=False, last=False):
        with jax.named_scope("attend"):
            ones = jnp.ones((256, 128), BF16)
            own = {h: slice(h * 128, (h + 1) * 128) for h in heads}
            old = {} if first else {h: top[h] for h in heads}
            masks = [bias[plane // 4] for plane in planes]
            scores, new, totals = {}, {}, {}
            for h in heads:
                scores[h] = [
                    dot(qh[:, own[h]], kv_text[plane, :, own[h]], 1, 1) + mask for plane, mask in zip(planes, masks)
                ]
            for h in heads:
                m = scores[h][0]
                for s in scores[h][1:]:
                    m = jnp.maximum(m, s)
                m = jnp.max(m, axis=1, keepdims=True)
                new[h] = m if first else jnp.maximum(old[h], m)
            for h in heads:
                weights = [jnp.exp2(s - new[h][:, :1]).astype(BF16) for s in scores[h]]
                parts = [
                    dot(p, jnp.concatenate([kv_text[plane, :, 512 + h * 128:512 + (h + 1) * 128], ones], 1))
                    for plane, p in zip(planes, weights)
                ]
                totals[h] = sum(parts[1:], parts[0])
            for h in heads:
                total = totals[h]
                if not first:
                    shrink = jnp.exp2(old[h] - new[h])
                    total = total + acc[h] * jnp.concatenate([shrink, shrink], 1)
                if last:
                    result = total[:, :128] / total[:, 128:]
                    seen_any = bias[0, :, :1] == 0.0
                    att_out[:, own[h]] = jnp.where(seen_any, result, 0.0).astype(BF16)
                else:
                    acc[h] = total
                    top[h] = jnp.broadcast_to(new[h], (256, 128))

    def kv_ready(plane):
        sib_arrived(plane)
        with jax.named_scope("project_text"):
            project_text(plane)

    def waves(h, chunks):
        with jax.named_scope("wave_" + str(h)):
            for c in chunks:
                wave(h, c)

    with jax.named_scope("token_norm"):
        lax.fori_loop(12, 16, norm_tokens, 0)
    with jax.named_scope("wave_own"):
        for c in ORDER[:2]:
            wave_own(c)
        forward(0, 1, (1, 0))
        forward(0, 2, (1, 0))
        for c in ORDER[2:]:
            wave_own(c)
    with jax.named_scope("w_e"):
        w0(2).wait_recv()
        near(1, 0, (2,))
        near(1, 1, (2,))
    with jax.named_scope("w_c0"):
        forward(1, 0, (1,))
    with jax.named_scope("w_d"):
        for st in (4, 3):
            forward(0, st, (1, 0))
    with jax.named_scope("w_c"):
        first_ring_done(1, (1,))
        for st in (1, 2, 4, 3):
            near(1, st, (1,))
    with jax.named_scope("w_e"):
        w0(3).wait_recv()
        near(1, 0, (3,))
        near(1, 1, (3,))
    limit = jnp.minimum(seen[...], frame_count[...])
    row = lax.broadcasted_iota(jnp.int32, (256, 256), 0) % 128 // 8
    for zz in range(2):
        key_frame = row // 4 * 8 + zz * 4 + row % 4
        bias[zz] = jnp.where(key_frame < limit, 0.0, MASKED).T
    waves(1, ORDER)
    with jax.named_scope("w_f"):
        for st in (1, 2, 4, 3):
            forward(1, st, (1,))
    with jax.named_scope("w_g2"):
        forward(1, 0, (2,))
        near(1, 2, (2,))
        near(1, 4, (2,))
        forward(1, 1, (2,))
    waves(2, ORDER)
    with jax.named_scope("pack"):
        local_kv.wait()
        second_ring_done(0, (1,))
        second_ring_done(1, (1,))
        pack_weights(zh)
        pack_weights(1 - zh)
    kv_ready(z)
    with jax.named_scope("w_h2"):
        first_ring_done(1, (2,))
        near(1, 3, (2,))
        forward(1, 2, (2,))
        forward(1, 4, (2,))
    with jax.named_scope("w_g3"):
        forward(1, 0, (3,))
        near(1, 2, (3,))
        near(1, 4, (3,))
        forward(1, 1, (3,))
    kv_ready((z + 1) % 8)
    kv_ready((z + 7) % 8)
    waves(3, ORDER[:2])
    with jax.named_scope("query_0"):
        local_q.wait()
        second_ring_done(0, (0,))
        query_half(zh, slice(0, 512), True)
    waves(3, ORDER[2:])
    with jax.named_scope("w_i2"):
        forward(1, 3, (2,))
    kv_ready((z + 2) % 8)
    with jax.named_scope("w_h3"):
        first_ring_done(1, (3,))
        near(1, 3, (3,))
        forward(1, 2, (3,))
        forward(1, 4, (3,))
    kv_ready((z + 6) % 8)
    final = 5 - (zl + 1) // 2
    early = 3 + 2 * (zl // 3)
    between = 12 - final - early
    pairs = [
        (z, (z + 1) % 8),
        ((z + 7) % 8, (z + 2) % 8),
        ((z + 6) % 8, (z + early) % 8, (z + between) % 8),
        ((z + final) % 8,),
    ]
    waves(4, ORDER[:2])
    kv_ready((z + early) % 8)
    with jax.named_scope("query_1"):
        query_done(0)
    with jax.named_scope("w_i3"):
        forward(1, 3, (3,))
    attend(pairs[0], (0, 1), first=True)
    waves(4, ORDER[2:])
    attend(pairs[1], (0, 1))
    kv_ready((z + between) % 8)
    attend(pairs[2], (0, 1))
    waves(5, ORDER[:2])
    with jax.named_scope("drain_early"):
        take(has.at[0], har.at[0], hs.at[pl.ds(0, 7)]).wait_send()
        take(v4s.at[0], v4r.at[0], rows_of(240)).wait_send()
        take(wos.at[0], wor.at[0], rows_of(576)).wait_send()
        take(sibs.at[0], sibr.at[0], rows_of(768)).wait_send()
        take(nes.at[0], ner.at[0], rows_of(2048)).wait_send()
        take(nes.at[1], ner.at[0], rows_of(640)).wait_send()
        for k in (1, 2, 3):
            w0(k).wait_send()
    with jax.named_scope("query_1"):
        query_done(1)
    attend(pairs[0], (2, 3), first=True)
    attend(pairs[1], (2, 3))
    attend(pairs[2], (2, 3))
    waves(5, ORDER[2:])
    kv_ready((z + final) % 8)
    attend(pairs[3], (0, 1, 2, 3), last=True)

    with jax.named_scope("drain"):
        take(lss.at[0], lsr.at[0], rows_of(1024)).wait_send()
        take(fas.at[0], far.at[0], rows_of(1024)).wait_send()
        take(fas.at[1], far.at[0], rows_of(320)).wait_send()
        middle = (zl == 1) | (zl == 2)
        pl.when(middle)(lambda: take(fls.at[0], upr.at[0], rows_of(1280)).wait_send())
        pl.when(jnp.logical_not(middle))(lambda: take(fls.at[0], upr.at[0], rows_of(640)).wait_send())


def local(
    video_patches,
    frame_count,
    seen_frames,
    base_latents,
    vision_query,
    vision_kv,
    vision_out,
    hidden_states,
    text_query,
    text_kv,
):
    width = video_patches.shape[-1]
    vm = pl.BlockSpec(memory_space=pltpu.VMEM)
    hbm = pl.BlockSpec(memory_space=pl.ANY)
    dma = lambda n: pltpu.SemaphoreType.DMA((n,))
    latents_out, attended = pl.pallas_call(
        fused_kernel,
        name="fused",
        out_shape=(
            pltpu.VMEM((32, 8, 1280), BF16),
            pltpu.VMEM((256, 512), BF16),
        ),
        in_specs=[hbm, vm, vm, hbm, hbm, hbm, hbm, hbm, hbm, hbm],
        out_specs=(vm, vm),
        scratch_shapes=[
            pltpu.VMEM((64, 1280), BF16),
            pltpu.VMEM((192, 1280), BF16),
            pltpu.VMEM((2, 192, 1280), BF16),
            pltpu.VMEM((2048, 1280), BF16),
            pltpu.VMEM((512, 1280), BF16),
            pltpu.VMEM((8, 192, 1280), BF16),
            pltpu.VMEM((8, 4, 96, 128), BF16),
            pltpu.VMEM((8, 4, 96, 128), BF16),
            pltpu.VMEM((64, 1280), F32),
            pltpu.VMEM((32, 16, 640), BF16),
            pltpu.VMEM((2, 8, 16, 16, 640), BF16),
            pltpu.VMEM((16, 16, 640), BF16),
            pltpu.VMEM((16, 16, 640), BF16),
            pltpu.VMEM((4, 2, 4, 256, 512), BF16),
            pltpu.VMEM((4, 2, 4, 2, 40, 512), BF16),
            pltpu.VMEM((1280, 1024), BF16),
            pltpu.VMEM((256, 8192), BF16),
            pltpu.VMEM((256, 512), F32),
            pltpu.VMEM((256, 512), BF16),
            pltpu.VMEM((8, 256, 1024), BF16),
            pltpu.VMEM((2, 256, 256), F32),
            pltpu.VMEM((4, 256, 128), F32),
            pltpu.VMEM((4, 256, 256), F32),
            dma(18), dma(3), dma(3), dma(2), dma(25), dma(2), dma(10), dma(1), dma(4), dma(1), dma(1),
            dma(1), dma(4), dma(1), dma(4), dma(1), dma(20), dma(20), dma(8), dma(1), dma(8),
        ],
        compiler_params=pltpu.CompilerParams(
            collective_id=0, has_side_effects=True, vmem_limit_bytes=60 * 2**20
        ),
        cost_estimate=pl.CostEstimate(flops=14 * 10**9, bytes_accessed=40 * 10**6, transcendentals=3 * 10**6),
    )(
        video_patches.reshape(-1, width),
        frame_count.reshape(1, 1),
        seen_frames,
        base_latents,
        vision_query.T,
        vision_kv.transpose(0, 2, 1),
        vision_out,
        hidden_states,
        text_query,
        text_kv,
    )
    return latents_out[:, None], attended


def solution(mesh):
    placed = (
        P(None, "dp", None, None),
        P("dp"),
        P("dp", None),
        P(),
        P(None, "tensor"),
        P(None, None, "tensor"),
        P("tensor", None),
        P("dp", None),
        P("dp", "tensor"),
        P(None, "dp", "tensor"),
    )
    return jax.shard_map(
        local,
        mesh=mesh,
        in_specs=placed,
        out_specs=(P(None, "dp", "tensor", None), P("dp", "tensor")),
        check_vma=False,
    )
```
